32 devices in a mesh: seq: 4 (over y, x), batch: 8 (over z, core).
Axes of the slice: x: 2, y: 2, z: 4, core: 2. Of those that a mesh axis runs over, the one named last changes fastest.
Arguments:
- tokens: bfloat16 [64, 512, 768], P('batch', 'seq'), may hold values from -6 to 6
- values: float32 [64, 512], P('batch', 'seq'), may hold values from -4 to 4
- lengths: int32 [64], P('batch'), may hold values from 128 to 512, as said below
- merge: float32 [768], replicated, may hold values from -3 to 3
- w_query: bfloat16 [768, 768], replicated, may hold values from -0.21875 to 0.21875
- w_key: bfloat16 [768, 768], replicated, may hold values from -0.21875 to 0.21875
- w_value: bfloat16 [768, 768], replicated, may hold values from -0.21875 to 0.21875
- w_output: bfloat16 [768, 768], replicated, may hold values from -0.4375 to 0.4375
- b_query: float32 [768], replicated, may hold values from -3 to 3
- b_value: float32 [768], replicated, may hold values from -3 to 3
- b_output: float32 [768], replicated, may hold values from -3 to 3
- gain_one: float32 [768], replicated, may hold values from 0.5 to 1.5
- shift_one: float32 [768], replicated, may hold values from -2 to 2
- w_inner: bfloat16 [768, 3072], replicated, may hold values from -0.21875 to 0.21875
- b_inner: float32 [3072], replicated, may hold values from -3 to 3
- w_outer: bfloat16 [3072, 768], replicated, may hold values from -0.109375 to 0.109375
- b_outer: float32 [768], replicated, may hold values from -2 to 2
- gain_two: float32 [768], replicated, may hold values from 0.5 to 1.5
- shift_two: float32 [768], replicated, may hold values from -2 to 2
- cotangent: bfloat16 [64, 512, 768], P('batch', 'seq'), may hold values from -6 to 6
Outputs:
- layer_out: float32 [64, 512, 768], P('batch', 'seq')
- grad_tokens: float32 [64, 512, 768], P('batch', 'seq')
- grad_merge: float32 [768], P('batch')
- grad_w_query: float32 [768, 768], P('batch')
- grad_w_key: float32 [768, 768], P('batch')
- grad_w_value: float32 [768, 768], P('batch')
- grad_w_output: float32 [768, 768], P('batch')
- grad_b_query: float32 [768], P('batch')
- grad_b_value: float32 [768], P('batch')
- grad_b_output: float32 [768], P('batch')
- grad_gain_one: float32 [768], P('batch')
- grad_shift_one: float32 [768], P('batch')
- grad_w_inner: float32 [768, 3072], P('batch')
- grad_b_inner: float32 [3072], P('batch')
- grad_w_outer: float32 [3072, 768], P('batch')
- grad_b_outer: float32 [768], P('batch')
- grad_gain_two: float32 [768], P('batch')
- grad_shift_two: float32 [768], P('batch')
The draws below stay inside these ranges and needn't reach their ends.
Inputs may be any that keep to these rules, and one draw needn't show every extreme that they name: `lengths`: in each aligned block of 8 rows (the rows of one index of batch) one row, drawn from the seed, has all 512 slots real.
All inputs are finite; a program needn't handle non-finite values.
Results may differ from the reference program's by a relative error of at most 0.033.
Values may be sent and summed in bfloat16 or wider, within the bound.
No kernel may reach another device: no remote copies, remote signals or barrier semaphores. Data moves between devices by JAX's collectives and lax.ppermute only.
A program may use at most 256 MiB of HBM per device.

```python
import jax
import jax.numpy as jnp
from jax import lax

D = 768
H = 12
DH = 64
FF = 3072
LEN = 512
ROWS_DEV = 8
ROWS = 64


def unit_field(key, shape, bound):
    return jax.random.truncated_normal(key, -bound, bound, shape, jnp.float32)


def draw_tokens(key, part):
    key = jax.random.fold_in(key, 21)
    return unit_field(key, (ROWS, LEN, D), 6.0).astype(jnp.bfloat16)


def draw_values(key, part):
    key = jax.random.fold_in(key, 23)
    return unit_field(key, (ROWS, LEN), 4.0)


def draw_cotangent(key, part):
    key = jax.random.fold_in(key, 27)
    return unit_field(key, (ROWS, LEN, D), 6.0).astype(jnp.bfloat16)


def draw_lengths(key, part):
    key = jax.random.fold_in(key, 11)
    base = jax.random.randint(jax.random.fold_in(key, 1), (ROWS,), LEN // 4, LEN + 1)
    chosen = jax.random.randint(jax.random.fold_in(key, 2), (ROWS // ROWS_DEV,), 0, ROWS_DEV)
    spots = jnp.arange(ROWS) % ROWS_DEV == jnp.repeat(chosen, ROWS_DEV)
    return jnp.where(spots, LEN, base).astype(jnp.int32)


def normal_values(rng, dims, scale, most, kind=jnp.bfloat16):
    return jnp.clip(scale * jax.random.normal(rng, dims, jnp.float32), -most, most).astype(kind)


def setup_inputs(seed: int = 0) -> dict:
    key_list = jax.random.split(jax.random.key(seed), 21)
    tokens = draw_tokens(jax.random.fold_in(key_list[20], 71), 0)
    values = draw_values(jax.random.fold_in(key_list[20], 71), 0)
    lengths = draw_lengths(jax.random.fold_in(key_list[20], 71), 0)
    merge = normal_values(key_list[3], (D,), 0.5, 3.0, jnp.float32)
    w_query = normal_values(key_list[4], (D, D), D ** -0.5, 0.21875)
    w_key = normal_values(key_list[5], (D, D), D ** -0.5, 0.21875)
    w_value = normal_values(key_list[6], (D, D), D ** -0.5, 0.21875)
    w_output = normal_values(key_list[7], (D, D), (D // 4) ** -0.5, 0.4375)
    b_query = normal_values(key_list[8], (D,), 0.5, 3.0, jnp.float32)
    b_value = normal_values(key_list[9], (D,), 0.5, 3.0, jnp.float32)
    b_output = normal_values(key_list[10], (D,), 0.5, 3.0, jnp.float32)
    gain_one = jnp.clip(1.0 + 0.1 * jax.random.normal(key_list[11], (D,), jnp.float32), 0.5, 1.5)
    shift_one = normal_values(key_list[12], (D,), 0.3, 2.0, jnp.float32)
    w_inner = normal_values(key_list[13], (D, FF), D ** -0.5, 0.21875)
    b_inner = normal_values(key_list[14], (FF,), 0.5, 3.0, jnp.float32)
    w_outer = normal_values(key_list[15], (FF, D), FF ** -0.5, 0.109375)
    b_outer = normal_values(key_list[16], (D,), 0.3, 2.0, jnp.float32)
    gain_two = jnp.clip(1.0 + 0.1 * jax.random.normal(key_list[17], (D,), jnp.float32), 0.5, 1.5)
    shift_two = normal_values(key_list[18], (D,), 0.3, 2.0, jnp.float32)
    cotangent = draw_cotangent(jax.random.fold_in(key_list[20], 71), 0)
    return {"tokens": tokens, "values": values, "lengths": lengths, "merge": merge, "w_query": w_query, "w_key": w_key, "w_value": w_value, "w_output": w_output, "b_query": b_query, "b_value": b_value, "b_output": b_output, "gain_one": gain_one, "shift_one": shift_one, "w_inner": w_inner, "b_inner": b_inner, "w_outer": w_outer, "b_outer": b_outer, "gain_two": gain_two, "shift_two": shift_two, "cotangent": cotangent}


@jax.custom_vjp
def low(v):
    return lax.optimization_barrier(v.astype(jnp.bfloat16)).astype(jnp.float32)

@jax.custom_vjp
def low_back(v):
    return v

def low_keep(v):
    return (low(v), None)

def low_pass(kept, grad):
    return (grad,)

def back_keep(v):
    return (v, None)

def back_low(kept, grad):
    return (low(grad),)
low.defvjp(low_keep, low_pass)
low_back.defvjp(back_keep, back_low)

def matmul(left, right):
    return jnp.einsum('...d,de->...e', left, right, precision=lax.Precision.HIGHEST)

def layer_norm(inputs, gain, shift):
    center = inputs - lax.optimization_barrier(jnp.mean(inputs, axis=-1, keepdims=True))
    spread = lax.optimization_barrier(jnp.mean(center * center, axis=-1, keepdims=True))
    return center * lax.rsqrt(spread + 1e-05) * gain + shift

def layer(params, tokens, values, valid):
    merge, w_query, w_key, w_value, w_output, b_query, b_value, b_output, gain_one, shift_one, w_inner, b_inner, w_outer, b_outer, gain_two, shift_two = params
    group, slots, width = tokens.shape
    merged = tokens + values[..., None] * merge
    merged_low = low(merged)
    query = low(low_back(matmul(merged_low, w_query) + b_query)).reshape(group, slots, H, DH)
    key = low(low_back(matmul(merged_low, w_key))).reshape(group, slots, H, DH)
    value = low(low_back(matmul(merged_low, w_value) + b_value)).reshape(group, slots, H, DH)
    scores = jnp.einsum('gqhd,gkhd->ghqk', query, key, precision=lax.Precision.HIGHEST) * (1.0 / DH ** 0.5)
    scores = low_back(scores)
    scores = jnp.where(valid[:, None, None, :], scores, -1e+30)
    prob = low(jax.nn.softmax(scores, axis=-1))
    context = jnp.einsum('ghqk,gkhd->gqhd', prob, value, precision=lax.Precision.HIGHEST)
    context = low(low_back(context.reshape(group, slots, width)))
    attended = merged + low_back(matmul(context, w_output) + b_output)
    normed = layer_norm(attended, gain_one, shift_one)
    inner = low_back(matmul(low(normed), w_inner) + b_inner)
    activated = low(jax.nn.gelu(inner, approximate=False))
    summed = normed + low_back(matmul(activated, w_outer) + b_outer)
    return layer_norm(summed, gain_two, shift_two)

def reference(tokens, values, lengths, merge, w_query, w_key, w_value, w_output, b_query, b_value, b_output, gain_one, shift_one, w_inner, b_inner, w_outer, b_outer, gain_two, shift_two, cotangent):
    params = tuple((p.astype(jnp.float32) for p in (merge, w_query, w_key, w_value, w_output, b_query, b_value, b_output, gain_one, shift_one, w_inner, b_inner, w_outer, b_outer, gain_two, shift_two)))
    groups = ROWS // ROWS_DEV
    token_groups = tokens.astype(jnp.float32).reshape(groups, ROWS_DEV, LEN, D)
    value_groups = values.astype(jnp.float32).reshape(groups, ROWS_DEV, LEN)
    length_groups = lengths.reshape(groups, ROWS_DEV)
    cot_groups = cotangent.astype(jnp.float32).reshape(groups, ROWS_DEV, LEN, D)
    positions = jnp.arange(LEN, dtype=jnp.int32)

    def one_group(totals, items):
        block_tokens, block_values, block_lengths, block_cot = items
        valid = positions[None, :] < block_lengths[:, None]
        result, pull = jax.vjp(lambda pr, tk: layer(pr, tk, block_values, valid), params, block_tokens)
        grad_params, grad_input = pull(block_cot)
        totals = tuple((a + b for a, b in zip(totals, grad_params)))
        return (totals, (result, grad_input))
    start = tuple((jnp.zeros_like(p) for p in params))
    totals, (outputs, grads) = lax.scan(one_group, start, (token_groups, value_groups, length_groups, cot_groups))
    layer_out = outputs.reshape(ROWS, LEN, D)
    grad_tokens = grads.reshape(ROWS, LEN, D)
    return (layer_out, grad_tokens, totals[0], totals[1], totals[2], totals[3], totals[4], totals[5], totals[6], totals[7], totals[8], totals[9], totals[10], totals[11], totals[12], totals[13], totals[14], totals[15])
```

```python
import functools

import jax
import jax.numpy as jnp
from jax import lax
from jax.experimental import pallas as pl
from jax.experimental.pallas import tpu as pltpu
from jax.sharding import PartitionSpec as P

DH = 64
LOG2E = 1.4426950408889634
RSQRT2 = 0.7071067811865476
RSQRT2PI = 0.3989422804014327
EPS = 1e-05
bf16 = jnp.bfloat16
f32 = jnp.float32
NN = (((1,), (0,)), ((), ()))
NT = (((1,), (1,)), ((), ()))
TN = (((0,), (0,)), ((), ()))
Shape = jax.ShapeDtypeStruct
VM = pl.BlockSpec(memory_space=pltpu.VMEM)
SM = pl.BlockSpec(memory_space=pltpu.SMEM)
LIMIT = 60 * 1024 * 1024


def dot(left, right, dims=NN):
    return lax.dot_general(left, right, dims, preferred_element_type=f32)


def params(*semantics):
    return pltpu.CompilerParams(vmem_limit_bytes=LIMIT, dimension_semantics=semantics or None)


def whole(shape):
    return pl.BlockSpec(shape, lambda *_: (0,) * len(shape))


def row_sum(block):
    return jnp.sum(block, axis=0, keepdims=True)


def pack_kernel(parts, place_ref, lengths_ref, tokens_ref, values_ref, merge_ref, *outs):
    sends, value_sends, order_ref, own_ref = (
        outs[:parts],
        outs[parts : 2 * parts],
        outs[2 * parts],
        outs[2 * parts + 1],
    )
    rows = tokens_ref.shape[0]
    share = rows // parts
    me = place_ref[0]
    for i in range(rows):
        rank = jnp.int32(0)
        for j in range(rows):
            if j != i:
                ahead = lengths_ref[j] >= lengths_ref[i] if j < i else lengths_ref[j] > lengths_ref[i]
                rank = rank + ahead.astype(jnp.int32)
        turn = rank // parts
        spot = rank % parts
        owner = jnp.where(turn % 2 == 0, spot, parts - 1 - spot)
        order_ref[owner * share + turn] = jnp.int32(i)
    for r in range(share):
        own_ref[r] = lengths_ref[order_ref[me * share + r]]
    columns = values_ref[...].T
    lane = lax.broadcasted_iota(jnp.int32, columns.shape, 1)
    for d in range(parts):
        for r in range(share):
            row = order_ref[(me ^ d) * share + r]
            column = jnp.sum(jnp.where(lane == row, columns, 0.0), axis=1, keepdims=True)
            sends[d][r] = (tokens_ref[row].astype(f32) + column * merge_ref[...]).astype(bf16)
            value_sends[d][pl.ds(r, 1), :] = values_ref[pl.ds(row, 1), :]


def deal_kernel(parts, place_ref, order_ref, source_ref, *sends):
    share = source_ref.shape[0] // parts
    me = place_ref[0]
    for d in range(parts):
        for r in range(share):
            sends[d][r] = source_ref[order_ref[(me ^ d) * share + r]]


def undeal_kernel(parts, place_ref, order_ref, *refs):
    received, out_ref = refs[:parts], refs[parts]
    share = out_ref.shape[0] // parts
    me = place_ref[0]
    for d in range(parts):
        for r in range(share):
            out_ref[order_ref[(me ^ d) * share + r]] = received[d][r].astype(f32)


def attend(length, q_ref, k_ref, v_ref, put_context, lse_ref):
    span, width = q_ref.shape
    c = LOG2E / DH**0.5
    lane = lax.broadcasted_iota(jnp.int32, (1, 128), 1)
    low = lane < DH

    def branch(n):
        def pair(p, carry):
            sl = pl.ds(pl.multiple_of(p * 128, 128), 128)
            q, k, v = q_ref[:, sl], k_ref[:n, sl], v_ref[:n, sl]
            real = lax.broadcasted_iota(jnp.int32, (span, 128), 1) + (n - 128) < length
            found, sizes = [], []
            for h in range(2):
                mine = low if h == 0 else ~low
                s = dot(jnp.where(mine, q, jnp.zeros_like(q)), k, NT)
                tail = jnp.where(real, s[:, n - 128 :], -1e30)
                s = jnp.concatenate([s[:, : n - 128], tail], axis=1) if n > 128 else tail
                peak = jnp.max(s, axis=1, keepdims=True) * c
                e = jnp.exp2(s * c - peak)
                total = jnp.sum(e, axis=1, keepdims=True)
                found.append(dot(e.astype(bf16), jnp.where(mine, v, jnp.zeros_like(v))) / total)
                sizes.append(peak + jnp.log2(total))
            put_context(sl, (found[0] + found[1]).astype(bf16))
            kept = jnp.where(lane == 2 * p, sizes[0], lse_ref[...])
            lse_ref[...] = jnp.where(lane == 2 * p + 1, sizes[1], kept)
            return carry

        lse_ref[...] = jnp.zeros_like(lse_ref)
        lax.fori_loop(0, width // 128, pair, 0)

    blocks = (length + 127) // 128
    for b in range(1, span // 128 + 1):
        pl.when(blocks == b)(functools.partial(branch, 128 * b))


def attend_back(length, q_ref, k_ref, v_ref, ctx_ref, lse_ref, do_ref, put):
    span, width = q_ref.shape
    scale = 1.0 / DH**0.5
    c = LOG2E * scale
    lane = lax.broadcasted_iota(jnp.int32, (1, 128), 1)
    low = lane < DH

    def branch(n):
        def pair(p, carry):
            sl = pl.ds(pl.multiple_of(p * 128, 128), 128)
            q, k, v, do = q_ref[:, sl], k_ref[:n, sl], v_ref[:n, sl], do_ref[:, sl]
            real = lax.broadcasted_iota(jnp.int32, (span, 128), 1) + (n - 128) < length
            product = do.astype(f32) * ctx_ref[:, sl].astype(f32)
            sizes = lse_ref[...]
            dq = dk = dv = 0.0
            for h in range(2):
                mine = low if h == 0 else ~low
                qh = jnp.where(mine, q, jnp.zeros_like(q))
                doh = jnp.where(mine, do, jnp.zeros_like(do))
                kh = jnp.where(mine, k, jnp.zeros_like(k))
                delta = jnp.sum(jnp.where(mine, product, 0.0), axis=1, keepdims=True)
                lse = jnp.sum(jnp.where(lane == 2 * p + h, sizes, 0.0), axis=1, keepdims=True)
                prob = jnp.exp2(dot(qh, k, NT) * c - lse)
                tail = jnp.where(real, prob[:, n - 128 :], 0.0)
                prob = jnp.concatenate([prob[:, : n - 128], tail], axis=1) if n > 128 else tail
                ds = (prob * (dot(doh, v, NT) - delta)).astype(bf16)
                dq = dq + dot(ds, kh)
                dk = dk + dot(ds, qh, TN)
                dv = dv + dot(prob.astype(bf16), doh, TN)
            put(0, sl, 0, span, (dq * scale).astype(bf16))
            put(1, sl, 0, n, (dk * scale).astype(bf16))
            put(2, sl, 0, n, dv.astype(bf16))
            if n < span:
                blank = jnp.zeros((span - n, 128), bf16)
                put(1, sl, n, span, blank)
                put(2, sl, n, span, blank)
            return carry

        lax.fori_loop(0, width // 128, pair, 0)

    blocks = (length + 127) // 128
    for b in range(1, span // 128 + 1):
        pl.when(blocks == b)(functools.partial(branch, 128 * b))


def forward_kernel(
    parts, place_ref, own_ref, wq_ref, wk_ref, wv_ref, wo_ref, bq_ref, bv_ref, bo_ref, *refs
):
    pieces = refs[:parts]
    xc_ref, q_ref, k_ref, v_ref, lse_ref, hat_ref, rstd_ref = refs[parts:]
    me = place_ref[0]
    step = pieces[0].shape[1]
    for d in range(parts):
        xc_ref[1, pl.ds(pl.multiple_of((me ^ d) * step, step), step), :] = pieces[d][0]
    x = xc_ref[1]
    q_ref[...] = (dot(x, wq_ref[...]) + bq_ref[...]).astype(bf16)
    k_ref[...] = dot(x, wk_ref[...]).astype(bf16)
    v_ref[...] = (dot(x, wv_ref[...]) + bv_ref[...]).astype(bf16)

    def put(sl, block):
        xc_ref[0, :, sl] = block

    attend(own_ref[pl.program_id(0)], q_ref, k_ref, v_ref, put, lse_ref)
    a = xc_ref[1].astype(f32) + dot(xc_ref[0], wo_ref[...]) + bo_ref[...]
    center = a - jnp.mean(a, axis=1, keepdims=True)
    rstd = lax.rsqrt(jnp.mean(center * center, axis=1, keepdims=True) + EPS)
    hat_ref[...] = center * rstd
    rstd_ref[...] = jnp.broadcast_to(rstd, rstd_ref.shape)


def feed_kernel(
    parts,
    place_ref,
    hat_ref,
    gain_one_ref,
    shift_one_ref,
    wi_ref,
    bi_ref,
    wo_ref,
    bo_ref,
    gain_ref,
    shift_ref,
    *refs,
):
    cot = refs[:parts]
    act_ref, slope_ref, low_ref, branch_ref = refs[parts : parts + 4]
    outs = refs[parts + 4 : 2 * parts + 4]
    sums_ref, total_ref, cot_ref, out_ref = refs[2 * parts + 4 :]
    step = pl.program_id(0)
    count, width = total_ref.shape
    me = place_ref[0]
    share, slots = cot[0].shape[0], cot[0].shape[1]

    @pl.when(step == 0)
    def _():
        normed = hat_ref[...] * gain_one_ref[...] + shift_one_ref[...]
        low_ref[...] = normed.astype(bf16)
        total_ref[...] = normed + bo_ref[...]

    inner = dot(low_ref[...], wi_ref[...]) + bi_ref[...]
    phi = 0.5 + 0.5 * lax.erf(inner * RSQRT2)
    act = (inner * phi).astype(bf16)
    slope_ref[...] = (phi + inner * (jnp.exp(-0.5 * inner * inner) * RSQRT2PI)).astype(bf16)
    act_ref[...] = act
    total_ref[...] += dot(act, wo_ref[...])

    @pl.when(step == pl.num_programs(0) - 1)
    def _():
        for d in range(parts):
            for r in range(share):
                base = pl.multiple_of((r * parts + (me ^ d)) * slots, slots)
                cot_ref[pl.ds(base, slots), :] = cot[d][r]

        def block(i, carry):
            sl = pl.ds(pl.multiple_of(i * 128, 128), 128)
            a = total_ref[sl, :]
            center = a - jnp.mean(a, axis=1, keepdims=True)
            rstd = lax.rsqrt(jnp.mean(center * center, axis=1, keepdims=True) + EPS)
            hat = center * rstd
            out_ref[sl, :] = (hat * gain_ref[...] + shift_ref[...]).astype(bf16)
            g = cot_ref[sl, :].astype(f32)
            scaled = g * gain_ref[...]
            first = jnp.mean(scaled, axis=1, keepdims=True)
            second = jnp.mean(scaled * hat, axis=1, keepdims=True)
            back = rstd * (scaled - first - hat * second)
            total_ref[sl, :] = back
            low = back.astype(bf16)
            branch_ref[sl, :] = low
            return (
                carry[0] + row_sum(g * hat),
                carry[1] + row_sum(g),
                carry[2] + row_sum(low.astype(f32)),
            )

        blank = jnp.zeros((1, width), f32)
        sums = lax.fori_loop(0, count // 128, block, (blank, blank, blank))
        sums_ref[...] = jnp.concatenate(sums + (jnp.zeros((5, width), f32),), axis=0)
        for d in range(parts):
            for r in range(share):
                base = pl.multiple_of((r * parts + (me ^ d)) * slots, slots)
                outs[d][r] = out_ref[pl.ds(base, slots), :]


def feed_back_kernel(
    branch_ref,
    summed_ref,
    hat_ref,
    rstd_ref,
    slope_ref,
    wi_ref,
    wo_ref,
    gain_ref,
    inner_ref,
    bias_ref,
    attended_ref,
    low_ref,
    sums_ref,
    total_ref,
):
    step = pl.program_id(0)
    count, width = total_ref.shape
    inner = (dot(branch_ref[...], wo_ref[...], NT) * slope_ref[...].astype(f32)).astype(bf16)
    inner_ref[...] = inner
    bias_ref[...] = row_sum(inner.astype(f32))

    @pl.when(step == 0)
    def _():
        total_ref[...] = summed_ref[...]

    total_ref[...] += dot(inner, wi_ref[...], NT)

    @pl.when(step == pl.num_programs(0) - 1)
    def _():
        def block(i, carry):
            sl = pl.ds(pl.multiple_of(i * 128, 128), 128)
            g = total_ref[sl, :]
            hat = hat_ref[sl, :]
            scaled = g * gain_ref[...]
            first = jnp.mean(scaled, axis=1, keepdims=True)
            second = jnp.mean(scaled * hat, axis=1, keepdims=True)
            back = rstd_ref[sl, :1] * (scaled - first - hat * second)
            attended_ref[sl, :] = back
            low = back.astype(bf16)
            low_ref[sl, :] = low
            return (
                carry[0] + row_sum(g * hat),
                carry[1] + row_sum(g),
                carry[2] + row_sum(low.astype(f32)),
            )

        blank = jnp.zeros((1, width), f32)
        sums = lax.fori_loop(0, count // 128, block, (blank, blank, blank))
        sums_ref[...] = jnp.concatenate(sums + (jnp.zeros((5, width), f32),), axis=0)


def backward_kernel(
    parts,
    place_ref,
    own_ref,
    xc_ref,
    q_ref,
    k_ref,
    v_ref,
    lse_ref,
    low_ref,
    attended_ref,
    wq_ref,
    wk_ref,
    wv_ref,
    wo_ref,
    *refs,
):
    values = refs[:parts]
    grads_ref = refs[parts]
    outs = refs[parts + 1 : 2 * parts + 1]
    sums_ref, do_ref, value_ref = refs[2 * parts + 1 :]
    r = pl.program_id(0)
    me = place_ref[0]
    slots = outs[0].shape[1]
    do_ref[...] = dot(low_ref[...], wo_ref[...], NT).astype(bf16)
    grads_ref[0] = low_ref[...]

    def put(which, sl, start, stop, block):
        grads_ref[1 + which, start:stop, sl] = block

    attend_back(own_ref[r], q_ref, k_ref, v_ref, xc_ref.at[0], lse_ref, do_ref, put)
    for d in range(parts):
        base = pl.multiple_of((me ^ d) * slots, slots)
        value_ref[:, pl.ds(base, slots)] = jnp.broadcast_to(values[d][pl.ds(r, 1), :], (8, slots))
    dq, dk, dv = grads_ref[1], grads_ref[2], grads_ref[3]
    total = (
        attended_ref[...]
        + dot(dq, wq_ref[...], NT)
        + dot(dk, wk_ref[...], NT)
        + dot(dv, wv_ref[...], NT)
    )
    low = total.astype(bf16)
    attended_ref[...] = total
    for d in range(parts):
        base = pl.multiple_of((me ^ d) * slots, slots)
        outs[d][0] = attended_ref[pl.ds(base, slots), :].astype(bf16)
    weight = value_ref[...]
    high = weight.astype(bf16)
    rest = (weight - high.astype(f32)).astype(bf16)
    merge = (dot(high, low) + dot(rest, low))[:1]
    sums = jnp.concatenate(
        [
            row_sum(dq.astype(f32)),
            row_sum(dv.astype(f32)),
            merge,
            jnp.zeros((5, merge.shape[1]), f32),
        ],
        axis=0,
    )

    @pl.when(r == 0)
    def _():
        sums_ref[...] = sums

    @pl.when(r > 0)
    def _():
        sums_ref[...] += sums


def outer_grad_kernel(parts, place_ref, act_ref, branch_ref, keep_ref, send_ref):
    me, core = place_ref[0], place_ref[1]
    whole_grad = dot(act_ref[...], branch_ref[...], TN).astype(bf16)
    pairs, rows = keep_ref.shape[1], keep_ref.shape[2]
    for z in range(pairs):
        for unit in range(parts):
            base = (2 * z * parts + unit) * rows
            even = whole_grad[base : base + rows]
            odd = whole_grad[base + parts * rows : base + (parts + 1) * rows]
            keep_ref[unit ^ me, z] = jnp.where(core == 0, even, odd)
            send_ref[unit ^ me, z] = jnp.where(core == 0, odd, even)


def unit_grad_kernel(place_ref, left_ref, right_ref, keep_ref, send_ref):
    core = place_ref[1]
    left = left_ref[0] if len(left_ref.shape) == 3 else left_ref[...]
    right = right_ref[0] if len(right_ref.shape) == 3 else right_ref[...]
    whole_grad = dot(left, right, TN).astype(bf16)
    pairs, rows = keep_ref.shape[1], keep_ref.shape[2]
    for z in range(pairs):
        even = whole_grad[2 * z * rows : (2 * z + 1) * rows]
        odd = whole_grad[(2 * z + 1) * rows : (2 * z + 2) * rows]
        keep_ref[0, z] = jnp.where(core == 0, even, odd)
        send_ref[0, z] = jnp.where(core == 0, odd, even)


def swap(array, axis, size, distance):
    return lax.ppermute(array, axis, [(i, i ^ distance) for i in range(size)])


def add_low(first, *others):
    total = first.astype(f32)
    for other in others:
        total = total + other.astype(f32)
    return total.astype(bf16)


def halve(block, bit, size, distance):
    split = block.reshape((block.shape[0] // 2, 2) + block.shape[1:])
    send = lax.dynamic_index_in_dim(split, 1 - bit, 1, keepdims=False)
    keep = lax.dynamic_index_in_dim(split, bit, 1, keepdims=False)
    return keep, swap(send, "batch", size, distance)


def reduce_units(keep, send, me, place, parts, size):
    part = add_low(keep, swap(send, "batch", size, 1))
    block = add_low(part[0], *[swap(part[d], "seq", parts, d) for d in range(1, parts)])
    distance = 2
    while distance < size:
        bit = (place // distance) % 2
        block = add_low(*halve(block, bit, size, distance))
        distance *= 2
    block = block[0]
    pieces = [block] + [swap(block, "seq", parts, d) for d in range(1, parts)]
    stack = jnp.stack(pieces)
    return [
        lax.dynamic_index_in_dim(stack, me ^ unit, 0, keepdims=False).astype(f32)
        for unit in range(parts)
    ]


def reduce_vectors(block, place, parts, size):
    distance = 1
    while distance < size:
        bit = (place // distance) % 2
        keep, got = halve(block, bit, size, distance)
        block = keep + got
        distance *= 2
    distance = 1
    while distance < parts:
        block = block + swap(block, "seq", parts, distance)
        distance *= 2
    return block[0]


def body(
    parts,
    size,
    tokens,
    values,
    lengths,
    merge,
    w_query,
    w_key,
    w_value,
    w_output,
    b_query,
    b_value,
    b_output,
    gain_one,
    shift_one,
    w_inner,
    b_inner,
    w_outer,
    b_outer,
    gain_two,
    shift_two,
    cotangent,
):
    rows, slots, width = tokens.shape
    hidden = w_inner.shape[1]
    share = rows // parts
    span = slots * parts
    count = share * span
    me = lax.axis_index("seq")
    place = lax.axis_index("batch")
    spot = jnp.stack([me, place % 2]).astype(jnp.int32)
    line = lambda vector: vector.reshape(1, -1)
    piece = Shape((share, slots, width), bf16)

    packed = pl.pallas_call(
        functools.partial(pack_kernel, parts),
        in_specs=[SM, SM, VM, VM, VM],
        out_specs=[VM] * (2 * parts) + [SM, SM],
        out_shape=[piece] * parts
        + [Shape((share, slots), f32)] * parts
        + [Shape((rows,), jnp.int32), Shape((share,), jnp.int32)],
        compiler_params=params(),
        name="pack",
    )(spot, lengths, tokens, values, line(merge))
    order, own = packed[2 * parts :]

    def exchange(pieces):
        return [pieces[0]] + [swap(pieces[d], "seq", parts, d) for d in range(1, parts)]

    x_parts = exchange(packed[:parts])
    value_parts = exchange(packed[parts : 2 * parts])
    cot_parts = exchange(
        pl.pallas_call(
            functools.partial(deal_kernel, parts),
            in_specs=[SM, SM, VM],
            out_specs=[VM] * parts,
            out_shape=[piece] * parts,
            compiler_params=params(),
            name="deal",
        )(spot, order, cotangent)
    )

    by_row = pl.BlockSpec((span, width), lambda r: (r, 0))
    row_piece = pl.BlockSpec((1, slots, width), lambda r: (r, 0, 0))
    square = whole((width, width))
    vector = whole((1, width))
    thin = pl.BlockSpec((span, 128), lambda r: (r, 0))
    xc, query, key, value, lse, hat_one, rstd_one = pl.pallas_call(
        functools.partial(forward_kernel, parts),
        grid=(share,),
        in_specs=[SM, SM] + [square] * 4 + [vector] * 3 + [row_piece] * parts,
        out_specs=[pl.BlockSpec((2, span, width), lambda r: (0, r, 0))]
        + [by_row] * 3
        + [thin, by_row, thin],
        out_shape=[Shape((2, count, width), bf16)]
        + [Shape((count, width), bf16)] * 3
        + [Shape((count, 128), f32), Shape((count, width), f32), Shape((count, 128), f32)],
        compiler_params=params("arbitrary"),
        name="attention_forward",
    )(
        spot,
        own,
        w_query,
        w_key,
        w_value,
        w_output,
        line(b_query),
        line(b_value),
        line(b_output),
        *x_parts,
    )

    chunk = 512
    steps = hidden // chunk
    tall = whole((count, width))
    wi_spec = pl.BlockSpec((width, chunk), lambda i: (0, i))
    wo_spec = pl.BlockSpec((chunk, width), lambda i: (i, 0))
    bi_spec = pl.BlockSpec((1, chunk), lambda i: (0, i))
    mid = pl.BlockSpec((count, chunk), lambda i: (0, i))
    pieces_spec = whole((share, slots, width))
    fed = pl.pallas_call(
        functools.partial(feed_kernel, parts),
        grid=(steps,),
        in_specs=[SM, tall, vector, vector, wi_spec, bi_spec, wo_spec]
        + [vector] * 3
        + [pieces_spec] * parts,
        out_specs=[mid, mid, tall, tall] + [pieces_spec] * parts + [whole((8, width)), tall],
        out_shape=[Shape((count, hidden), bf16)] * 2
        + [Shape((count, width), bf16)] * 2
        + [piece] * parts
        + [Shape((8, width), f32), Shape((count, width), f32)],
        scratch_shapes=[pltpu.VMEM((count, width), bf16), pltpu.VMEM((count, width), bf16)],
        compiler_params=params("arbitrary"),
        name="feed_forward",
    )(
        spot,
        hat_one,
        line(gain_one),
        line(shift_one),
        w_inner,
        line(b_inner),
        w_outer,
        line(b_outer),
        line(gain_two),
        line(shift_two),
        *cot_parts,
    )
    act, slope, normed_low, d_branch = fed[:4]
    out_parts = fed[4 : 4 + parts]
    sums_two, d_summed = fed[4 + parts :]

    def undeal(pieces):
        return pl.pallas_call(
            functools.partial(undeal_kernel, parts),
            in_specs=[SM, SM] + [VM] * parts,
            out_specs=VM,
            out_shape=Shape((rows, slots, width), f32),
            compiler_params=params(),
            name="undeal",
        )(spot, order, *pieces)

    layer_out = undeal(exchange(out_parts))

    pairs = size // 2
    blk = width // size
    unit_shape = Shape((parts, pairs, blk, width), bf16)
    per_chunk = pairs * width // hidden
    outer_keep, outer_send = pl.pallas_call(
        functools.partial(outer_grad_kernel, parts),
        grid=(hidden // width,),
        in_specs=[SM, pl.BlockSpec((count, width), lambda i: (0, i)), tall],
        out_specs=[pl.BlockSpec((parts, per_chunk, blk, width), lambda i: (0, i, 0, 0))] * 2,
        out_shape=[unit_shape] * 2,
        compiler_params=params("arbitrary"),
        name="outer_grad",
    )(spot, act, d_branch)

    d_inner, inner_bias, d_attended, d_attn, sums_one = pl.pallas_call(
        feed_back_kernel,
        grid=(steps,),
        in_specs=[tall, tall, tall, whole((count, 128)), mid, wi_spec, wo_spec, vector],
        out_specs=[mid, bi_spec, tall, tall, whole((8, width))],
        out_shape=[
            Shape((count, hidden), bf16),
            Shape((1, hidden), f32),
            Shape((count, width), f32),
            Shape((count, width), bf16),
            Shape((8, width), f32),
        ],
        scratch_shapes=[pltpu.VMEM((count, width), f32)],
        compiler_params=params("arbitrary"),
        name="feed_backward",
    )(d_branch, d_summed, hat_one, rstd_one, slope, w_inner, w_outer, line(gain_one))

    def unit_grads(left, right, left_spec, right_spec, name):
        return pl.pallas_call(
            unit_grad_kernel,
            grid_spec=pltpu.PrefetchScalarGridSpec(
                num_scalar_prefetch=1,
                grid=(parts,),
                in_specs=[left_spec, right_spec],
                out_specs=[pl.BlockSpec((1, pairs, blk, width), lambda d, spot: (d, 0, 0, 0))] * 2,
            ),
            out_shape=[unit_shape] * 2,
            compiler_params=params("arbitrary"),
            name=name,
        )(spot, left, right)

    inner_keep, inner_send = unit_grads(
        normed_low,
        d_inner,
        pl.BlockSpec((count, width), lambda d, spot: (0, 0)),
        pl.BlockSpec((count, width), lambda d, spot: (0, d ^ spot[0])),
        "inner_grad",
    )

    small = whole((share, slots))
    back = pl.pallas_call(
        functools.partial(backward_kernel, parts),
        grid=(share,),
        in_specs=[
            SM,
            SM,
            pl.BlockSpec((1, span, width), lambda r: (0, r, 0)),
            by_row,
            by_row,
            by_row,
            thin,
            by_row,
            by_row,
        ]
        + [square] * 4
        + [small] * parts,
        out_specs=[pl.BlockSpec((4, span, width), lambda r: (0, r, 0))]
        + [row_piece] * parts
        + [whole((8, width))],
        out_shape=[Shape((4, count, width), bf16)] + [piece] * parts + [Shape((8, width), f32)],
        scratch_shapes=[pltpu.VMEM((span, width), bf16), pltpu.VMEM((8, span), f32)],
        compiler_params=params("arbitrary"),
        name="attention_backward",
    )(
        spot,
        own,
        xc,
        query,
        key,
        value,
        lse,
        d_attn,
        d_attended,
        w_query,
        w_key,
        w_value,
        w_output,
        *value_parts,
    )
    grads, token_parts, sums_zero = back[0], back[1 : 1 + parts], back[1 + parts]
    grad_tokens = undeal(exchange(token_parts))

    last_keep, last_send = unit_grads(
        xc,
        grads,
        pl.BlockSpec((1, count, width), lambda d, spot: (jnp.minimum(d ^ spot[0], 1), 0, 0)),
        pl.BlockSpec((1, count, width), lambda d, spot: (d ^ spot[0], 0, 0)),
        "square_grad",
    )

    outer_units = reduce_units(outer_keep, outer_send, me, place, parts, size)
    inner_units = reduce_units(inner_keep, inner_send, me, place, parts, size)
    last_units = reduce_units(last_keep, last_send, me, place, parts, size)

    nine = jnp.concatenate([sums_two[:3], sums_one[:3], sums_zero[:3]], axis=0)
    vectors = jnp.concatenate(
        [
            nine.reshape(9, size, blk).transpose(1, 0, 2).reshape(size, 9 * blk),
            inner_bias.reshape(size, hidden // size),
        ],
        axis=1,
    )
    vectors = reduce_vectors(vectors, place, parts, size)
    nine = [vectors[i * blk : (i + 1) * blk] for i in range(9)]
    grad_gain_two, grad_shift_two, grad_b_outer = nine[:3]
    grad_gain_one, grad_shift_one, grad_b_output = nine[3:6]
    grad_b_query, grad_b_value, grad_merge = nine[6:]
    return (
        layer_out,
        grad_tokens,
        grad_merge,
        last_units[1],
        last_units[2],
        last_units[3],
        last_units[0],
        grad_b_query,
        grad_b_value,
        grad_b_output,
        grad_gain_one,
        grad_shift_one,
        jnp.concatenate(inner_units, axis=1),
        vectors[9 * blk :],
        jnp.concatenate(outer_units, axis=0),
        grad_b_outer,
        grad_gain_two,
        grad_shift_two,
    )


def solution(mesh):
    parts, size = mesh.shape["seq"], mesh.shape["batch"]
    rowwise = P("batch", "seq", None)
    in_specs = (rowwise, P("batch", "seq"), P("batch")) + (P(),) * 16 + (rowwise,)
    matrix, vector = P("batch", None), P("batch")
    out_specs = (
        (rowwise, rowwise, vector)
        + (matrix,) * 4
        + (vector,) * 5
        + (matrix, vector, matrix)
        + (vector,) * 3
    )
    return jax.shard_map(
        functools.partial(body, parts, size),
        mesh=mesh,
        in_specs=in_specs,
        out_specs=out_specs,
        check_vma=False,
    )
```

```python
import functools

import jax
import jax.numpy as jnp
from jax import lax
from jax.experimental import pallas as pl
from jax.experimental.pallas import tpu as pltpu
from jax.sharding import PartitionSpec as P

DH = 64
LOG2E = 1.4426950408889634
RSQRT2 = 0.7071067811865476
RSQRT2PI = 0.3989422804014327
EPS = 1e-05
EXTRA = 16
bf16 = jnp.bfloat16
f32 = jnp.float32
NN = (((1,), (0,)), ((), ()))
NT = (((1,), (1,)), ((), ()))
TN = (((0,), (0,)), ((), ()))
Shape = jax.ShapeDtypeStruct
VM = pl.BlockSpec(memory_space=pltpu.VMEM)
SM = pl.BlockSpec(memory_space=pltpu.SMEM)
BLOCK = 256


def dot(left, right, dims=NN):
    return lax.dot_general(left, right, dims, preferred_element_type=f32)


def params(limit, *semantics):
    return pltpu.CompilerParams(
        vmem_limit_bytes=limit * 1024 * 1024, dimension_semantics=semantics or None
    )


class Sequence:
    def __init__(self):
        self.last = ()

    def __call__(
        self, kernel, outs, ins, scratch=(), grid=None, prefetch=0, limit=16, alias=None, heavy=False, name=None
    ):
        count, extra = len(ins), len(self.last)

        def run(*refs):
            kernel(*refs[:count], *refs[count + extra :])

        got = pl.pallas_call(
            run,
            grid_spec=pltpu.PrefetchScalarGridSpec(
                num_scalar_prefetch=prefetch,
                grid=grid or (),
                in_specs=[spec for spec, _ in ins[prefetch:]]
                + [pl.BlockSpec(memory_space=pl.ANY)] * extra,
                out_specs=[spec for spec, _ in outs],
                scratch_shapes=list(scratch),
            ),
            out_shape=[shape for _, shape in outs],
            input_output_aliases=alias or {},
            compiler_params=params(limit, *(["arbitrary"] * len(grid or ()))),
            cost_estimate=pl.CostEstimate(
                flops=10**12 if heavy else 10**3,
                transcendentals=0,
                bytes_accessed=10**9 if heavy else 10**3,
            ),
            name=name,
        )(*[array for _, array in ins], *self.last)
        self.last = (min(got, key=lambda array: array.size),)
        return got


def whole(shape):
    return pl.BlockSpec(shape, lambda *_: (0,) * len(shape))


def row_sum(block):
    return jnp.sum(block, axis=0, keepdims=True)


def pack_kernel(parts, place_ref, lengths_ref, tokens_ref, values_ref, merge_ref, *outs):
    order_ref, own_ref = outs[-2:]
    rows = tokens_ref.shape[0]
    share = rows // parts
    me = place_ref[0]
    for i in range(rows):
        rank = jnp.int32(0)
        for j in range(rows):
            if j != i:
                ahead = lengths_ref[j] >= lengths_ref[i] if j < i else lengths_ref[j] > lengths_ref[i]
                rank = rank + ahead.astype(jnp.int32)
        turn = rank // parts
        spot = rank % parts
        owner = jnp.where(turn % 2 == 0, spot, parts - 1 - spot)
        order_ref[owner * share + turn] = jnp.int32(i)
    for r in range(share):
        own_ref[r] = lengths_ref[order_ref[me * share + r]]
    columns = values_ref[...].T
    lane = lax.broadcasted_iota(jnp.int32, columns.shape, 1)
    for r in range(share):
        for d in range(parts):
            row = order_ref[(me ^ d) * share + r]
            column = jnp.sum(jnp.where(lane == row, columns, 0.0), axis=1, keepdims=True)
            outs[r * parts + d][...] = (
                tokens_ref[row].astype(f32) + column * merge_ref[...]
            ).astype(bf16)


def deal_kernel(parts, place_ref, order_ref, source_ref, values_ref, *sends):
    rows, slots, width = source_ref.shape
    share = rows // parts
    me = place_ref[0]
    for d in range(parts):
        for r in range(share):
            row = order_ref[(me ^ d) * share + r]
            sends[d][r, :slots] = source_ref[row]
            value = values_ref[pl.ds(row, 1), :]
            high = value.astype(bf16).astype(f32)
            rest = value - high
            middle = rest.astype(bf16).astype(f32)
            three = jnp.concatenate(
                [high, middle, rest - middle, jnp.zeros((EXTRA - 3, slots), f32)], axis=0
            )
            if width > slots:
                three = jnp.concatenate([three, jnp.zeros((EXTRA, width - slots), f32)], axis=1)
            sends[d][r, slots:] = three.astype(bf16)


def undeal_kernel(parts, row, place_ref, order_ref, *refs):
    pieces, out_ref = refs[:parts], refs[-1]
    for d in range(parts):

        @pl.when(pl.program_id(0) == d)
        def _(d=d):
            piece = pieces[d][...] if row is None else pieces[d][row]
            out_ref[0] = piece.astype(f32)


def attend(length, q_ref, k_ref, v_ref, put_context, lse_ref):
    span, width = q_ref.shape
    c = LOG2E / DH**0.5
    lane = lax.broadcasted_iota(jnp.int32, (1, 128), 1)
    low = lane < DH

    def branch(n):
        def pair(p, carry):
            sl = pl.ds(pl.multiple_of(p * 128, 128), 128)
            q, k, v = q_ref[:, sl], k_ref[:n, sl], v_ref[:n, sl]
            real = lax.broadcasted_iota(jnp.int32, (span, 128), 1) + (n - 128) < length
            found, sizes = [], []
            for h in range(2):
                mine = low if h == 0 else ~low
                s = dot(jnp.where(mine, q, jnp.zeros_like(q)), k, NT)
                tail = jnp.where(real, s[:, n - 128 :], -1e30)
                s = jnp.concatenate([s[:, : n - 128], tail], axis=1) if n > 128 else tail
                peak = jnp.max(s, axis=1, keepdims=True) * c
                e = jnp.exp2(s * c - peak)
                total = jnp.sum(e, axis=1, keepdims=True)
                found.append(dot(e.astype(bf16), jnp.where(mine, v, jnp.zeros_like(v))) / total)
                sizes.append(peak + jnp.log2(total))
            put_context(sl, (found[0] + found[1]).astype(bf16))
            kept = jnp.where(lane == 2 * p, sizes[0], lse_ref[...])
            lse_ref[...] = jnp.where(lane == 2 * p + 1, sizes[1], kept)
            return carry

        lse_ref[...] = jnp.zeros_like(lse_ref)
        lax.fori_loop(0, width // 128, pair, 0)

    blocks = (length + 127) // 128
    for b in range(1, span // 128 + 1):
        pl.when(blocks == b)(functools.partial(branch, 128 * b))


def attend_back(length, q_ref, k_ref, v_ref, ctx_ref, lse_ref, do_ref, put):
    span, width = q_ref.shape
    scale = 1.0 / DH**0.5
    c = LOG2E * scale
    lane = lax.broadcasted_iota(jnp.int32, (1, 128), 1)
    low = lane < DH

    def branch(n):
        def pair(p, carry):
            sl = pl.ds(pl.multiple_of(p * 128, 128), 128)
            q, k, v, do = q_ref[:, sl], k_ref[:n, sl], v_ref[:n, sl], do_ref[:, sl]
            real = lax.broadcasted_iota(jnp.int32, (span, 128), 1) + (n - 128) < length
            product = do.astype(f32) * ctx_ref[:, sl].astype(f32)
            sizes = lse_ref[...]
            dq = dk = dv = 0.0
            for h in range(2):
                mine = low if h == 0 else ~low
                qh = jnp.where(mine, q, jnp.zeros_like(q))
                doh = jnp.where(mine, do, jnp.zeros_like(do))
                kh = jnp.where(mine, k, jnp.zeros_like(k))
                delta = jnp.sum(jnp.where(mine, product, 0.0), axis=1, keepdims=True)
                lse = jnp.sum(jnp.where(lane == 2 * p + h, sizes, 0.0), axis=1, keepdims=True)
                prob = jnp.exp2(dot(qh, k, NT) * c - lse)
                tail = jnp.where(real, prob[:, n - 128 :], 0.0)
                prob = jnp.concatenate([prob[:, : n - 128], tail], axis=1) if n > 128 else tail
                ds = (prob * (dot(doh, v, NT) - delta)).astype(bf16)
                dq = dq + dot(ds, kh)
                dk = dk + dot(ds, qh, TN)
                dv = dv + dot(prob.astype(bf16), doh, TN)
            put(0, sl, 0, span, (dq * scale).astype(bf16))
            put(1, sl, 0, n, (dk * scale).astype(bf16))
            put(2, sl, 0, n, dv.astype(bf16))
            if n < span:
                blank = jnp.zeros((span - n, 128), bf16)
                put(1, sl, n, span, blank)
                put(2, sl, n, span, blank)
            return carry

        lax.fori_loop(0, width // 128, pair, 0)

    blocks = (length + 127) // 128
    for b in range(1, span // 128 + 1):
        pl.when(blocks == b)(functools.partial(branch, 128 * b))


def forward_kernel(
    parts, row, place_ref, own_ref, wq_ref, wk_ref, wv_ref, wo_ref, bq_ref, bv_ref, bo_ref, *refs
):
    pieces = refs[:parts]
    xc_ref, q_ref, k_ref, v_ref, lse_ref, hat_ref, rstd_ref = refs[parts:]
    me = place_ref[0]
    step = pieces[0].shape[0]
    for d in range(parts):
        xc_ref[1, pl.ds(pl.multiple_of((me ^ d) * step, step), step), :] = pieces[d][...]
    x = xc_ref[1]
    q_ref[...] = (dot(x, wq_ref[...]) + bq_ref[...]).astype(bf16)
    k_ref[...] = dot(x, wk_ref[...]).astype(bf16)
    v_ref[...] = (dot(x, wv_ref[...]) + bv_ref[...]).astype(bf16)

    def put(sl, block):
        xc_ref[0, :, sl] = block

    attend(own_ref[row], q_ref, k_ref, v_ref, put, lse_ref)
    a = xc_ref[1].astype(f32) + dot(xc_ref[0], wo_ref[...]) + bo_ref[...]
    center = a - jnp.mean(a, axis=1, keepdims=True)
    rstd = lax.rsqrt(jnp.mean(center * center, axis=1, keepdims=True) + EPS)
    hat_ref[...] = center * rstd
    rstd_ref[...] = jnp.broadcast_to(rstd, rstd_ref.shape)


def split_cores(core, block, pairs, step, keep, send):
    for z in range(pairs):
        even, odd = block[2 * z * step : (2 * z + 1) * step], block[(2 * z + 1) * step : (2 * z + 2) * step]
        keep(z, jnp.where(core == 0, even, odd))
        send(z, jnp.where(core == 0, odd, even))


def norm_back(g, hat, rstd, gain):
    scaled = g * gain
    first = jnp.mean(scaled, axis=1, keepdims=True)
    second = jnp.mean(scaled * hat, axis=1, keepdims=True)
    return rstd * (scaled - first - hat * second)


def feed_kernel(
    parts,
    share,
    steps,
    place_ref,
    gain_one_ref,
    shift_one_ref,
    wi_ref,
    bi_ref,
    wo_ref,
    bo_ref,
    gain_ref,
    shift_ref,
    *refs,
):
    hats, refs = refs[:share], refs[share:]
    cot = refs[:parts]
    slope_ref, low_ref, branch_ref = refs[parts : parts + 3]
    outs = refs[parts + 3 : 2 * parts + 3]
    sums_ref, total_ref, keep_ref, send_ref, act_ref, cot_ref, out_ref = refs[2 * parts + 3 :]
    step = pl.program_id(0)
    count, width = total_ref.shape
    chunk = wi_ref.shape[1]
    me, core = place_ref[0], place_ref[1]
    slots = outs[0].shape[1]
    span = count // share

    def pieces():
        for d in range(parts):
            for r in range(share):
                yield d, r, pl.ds(pl.multiple_of((r * parts + (me ^ d)) * slots, slots), slots)

    @pl.when(step == 0)
    def _():
        for r in range(share):
            normed = hats[r][...] * gain_one_ref[...] + shift_one_ref[...]
            low_ref[r * span : (r + 1) * span] = normed.astype(bf16)
            total_ref[r * span : (r + 1) * span] = normed + bo_ref[...]

    def run(last):
        def first(i):
            return dot(low_ref[i * BLOCK : (i + 1) * BLOCK], wi_ref[...]) + bi_ref[...]

        if last:
            for d, r, place in pieces():
                cot_ref[place, :] = cot[d][r, :slots]
        blocks = count // BLOCK
        ahead = first(0)
        sums = [0.0, 0.0, 0.0]
        for i in range(blocks):
            inner = ahead
            if i + 1 < blocks:
                ahead = first(i + 1)
            sl = slice(i * BLOCK, (i + 1) * BLOCK)
            phi = 0.5 + 0.5 * lax.erf(inner * RSQRT2)
            act = (inner * phi).astype(bf16)
            slope_ref[0, sl] = (phi + inner * (jnp.exp(-0.5 * inner * inner) * RSQRT2PI)).astype(bf16)
            act_ref[sl, pl.ds(pl.multiple_of(step * chunk, chunk), chunk)] = act
            a = total_ref[sl] + dot(act, wo_ref[...])
            if not last:
                total_ref[sl] = a
                continue
            center = a - jnp.mean(a, axis=1, keepdims=True)
            rstd = lax.rsqrt(jnp.mean(center * center, axis=1, keepdims=True) + EPS)
            hat = center * rstd
            out_ref[sl] = (hat * gain_ref[...] + shift_ref[...]).astype(bf16)
            g = cot_ref[sl].astype(f32)
            back = norm_back(g, hat, rstd, gain_ref[...])
            total_ref[sl] = back
            low = back.astype(bf16)
            branch_ref[sl] = low
            for k, term in enumerate((g * hat, g, low.astype(f32))):
                sums[k] = sums[k] + row_sum(term)
        if last:
            sums_ref[...] = jnp.concatenate(sums + [jnp.zeros((5, width), f32)], axis=0)
            for d, r, place in pieces():
                outs[d][r] = out_ref[place, :]

    pl.when(step < steps - 1)(functools.partial(run, False))
    pl.when(step == steps - 1)(functools.partial(run, True))

    @pl.when(step >= steps)
    def _():
        here = pl.ds(pl.multiple_of((step - steps) * chunk, chunk), chunk)
        grad = dot(act_ref[:, here], branch_ref[...], TN).astype(bf16)
        pairs, rows = keep_ref.shape[1], keep_ref.shape[2]

        def put(ref):
            def store(z, block):
                for unit in range(parts):
                    ref[unit ^ me, z] = block[unit * rows : (unit + 1) * rows]

            return store

        split_cores(core, grad, pairs, parts * rows, put(keep_ref), put(send_ref))


def feed_back_kernel(share, units, last, place_ref, branch_ref, before_ref, low_ref, *refs):
    slope_ref, wi_ref, wo_ref, *refs = refs
    if last:
        hats, rstds, refs = refs[:share], refs[share : 2 * share], refs[2 * share :]
        contexts, refs = refs[:share], refs[share:]
        gain_ref, keep_ref, send_ref, bias_ref, total_ref, attn_ref, sums_ref, inner_ref = refs
    else:
        keep_ref, send_ref, bias_ref, total_ref, inner_ref = refs
    step = pl.program_id(0)
    count, width = total_ref.shape
    span = count // share
    blocks = count // BLOCK

    @pl.when(step == 0)
    def _():
        total_ref[...] = before_ref[...]

    def run(ending):
        def first(i):
            return dot(branch_ref[i * BLOCK : (i + 1) * BLOCK], wo_ref[...], NT)

        ahead = first(0)
        bias = 0.0
        sums = [0.0, 0.0, 0.0]
        for i in range(blocks):
            now = ahead
            if i + 1 < blocks:
                ahead = first(i + 1)
            sl = slice(i * BLOCK, (i + 1) * BLOCK)
            inner = (now * slope_ref[0, sl].astype(f32)).astype(bf16)
            inner_ref[sl] = inner
            bias = bias + row_sum(inner.astype(f32))
            g = total_ref[sl] + dot(inner, wi_ref[...], NT)
            if not ending:
                total_ref[sl] = g
                continue
            r, start = i * BLOCK // span, i * BLOCK % span
            here = slice(start, start + BLOCK)
            hat = hats[r][here]
            back = norm_back(g, hat, rstds[r][here, :1], gain_ref[...])
            total_ref[sl] = back
            low = back.astype(bf16)
            attn_ref[sl] = low
            for k, term in enumerate((g * hat, g, low.astype(f32))):
                sums[k] = sums[k] + row_sum(term)
        bias_ref[...] = bias
        if ending:
            sums_ref[...] = jnp.concatenate(sums + [jnp.zeros((5, width), f32)], axis=0)
        grad = dot(low_ref[...], inner_ref[...], TN).astype(bf16)
        put_unit(place_ref[1], grad, keep_ref, send_ref)

    if not last:
        run(False)
        return
    pl.when(step < units - 1)(functools.partial(run, False))
    pl.when(step == units - 1)(functools.partial(run, True))

    @pl.when(step == units)
    def _():
        grad = 0.0
        for r in range(share):
            grad = grad + dot(contexts[r][0], attn_ref[r * span : (r + 1) * span], TN)
        put_unit(place_ref[1], grad.astype(bf16), keep_ref, send_ref)


def put_unit(core, grad, keep_ref, send_ref):
    pairs, rows = keep_ref.shape[1], keep_ref.shape[2]

    def put(ref):
        def store(z, block):
            ref[0, z] = block

        return store

    split_cores(core, grad, pairs, rows, put(keep_ref), put(send_ref))


def backward_kernel(
    parts,
    row,
    place_ref,
    own_ref,
    xc_ref,
    q_ref,
    k_ref,
    v_ref,
    lse_ref,
    low_ref,
    attended_ref,
    wq_ref,
    wk_ref,
    wv_ref,
    wo_ref,
    *refs,
):
    values = refs[:parts]
    grads_ref = refs[parts]
    outs = refs[parts + 1 : 2 * parts + 1]
    sums_ref, do_ref, total_ref, value_ref = refs[2 * parts + 1 :]
    me = place_ref[0]
    slots = outs[0].shape[0]
    do_ref[...] = dot(low_ref[...], wo_ref[...], NT).astype(bf16)

    def put(which, sl, start, stop, block):
        grads_ref[which, start:stop, sl] = block

    attend_back(own_ref[row], q_ref, k_ref, v_ref, xc_ref.at[0], lse_ref, do_ref, put)
    for d in range(parts):
        base = pl.multiple_of((me ^ d) * slots, slots)
        value_ref[:, pl.ds(base, slots)] = values[d][0, :, :slots]
    dq, dk, dv = grads_ref[0], grads_ref[1], grads_ref[2]
    total = (
        attended_ref[...]
        + dot(dq, wq_ref[...], NT)
        + dot(dk, wk_ref[...], NT)
        + dot(dv, wv_ref[...], NT)
    )
    low = total.astype(bf16)
    total_ref[...] = low
    for d in range(parts):
        base = pl.multiple_of((me ^ d) * slots, slots)
        outs[d][...] = total_ref[pl.ds(base, slots), :]
    merge = row_sum(dot(value_ref[...], low))
    sums_ref[...] = jnp.concatenate(
        [
            row_sum(dq.astype(f32)),
            row_sum(dv.astype(f32)),
            merge,
            jnp.zeros((5, merge.shape[1]), f32),
        ],
        axis=0,
    )


def unit_grad_kernel(share, place_ref, *refs):
    lefts, rights = refs[:share], refs[share : 2 * share]
    *vectors, keep_ref, send_ref = refs[2 * share :]
    core = place_ref[1]
    total = 0.0
    for left_ref, right_ref in zip(lefts, rights):
        total = total + dot(left_ref[0], right_ref[0], TN)
    grad = total.astype(bf16)
    if not vectors:
        put_unit(core, grad, keep_ref, send_ref)
        return
    pairs, rows, width = keep_ref.shape[1:]
    rows = rows - EXTRA
    for z in range(pairs):
        found = []
        for b in (2 * z, 2 * z + 1):
            vector = vectors[0][b]
            blank = jnp.zeros((EXTRA - vector.shape[0], width), f32)
            tail = jnp.concatenate([vector, blank], axis=0).astype(bf16)
            found.append((grad[b * rows : (b + 1) * rows], tail))
        for k in range(2):
            place = slice(0, rows) if k == 0 else slice(rows, rows + EXTRA)
            keep_ref[0, z, place] = jnp.where(core == 0, found[0][k], found[1][k])
            send_ref[0, z, place] = jnp.where(core == 0, found[1][k], found[0][k])


def plane_first_kernel(place_ref, keep_ref, got_ref, *outs):
    keep_x, send_x, keep_y, send_y = outs
    units, blocks, rows = keep_ref.shape[:3]
    half = rows // 2
    for d in range(units):
        for i in range(blocks):
            total = (keep_ref[d, i].astype(f32) + got_ref[d, i].astype(f32)).astype(bf16)
            (send_x if d % 2 else keep_x)[d // 2, i] = total[:half]
            (send_y if d // 2 else keep_y)[d % 2, i] = total[half:]


def plane_second_kernel(place_ref, keep_x, got_x, keep_y, got_y, *outs):
    blocks = keep_x.shape[1]
    for i in range(blocks):
        for j in range(2):
            outs[j][0, i] = (keep_x[j, i].astype(f32) + got_x[j, i].astype(f32)).astype(bf16)
            outs[2 + j][0, i] = (keep_y[j, i].astype(f32) + got_y[j, i].astype(f32)).astype(bf16)


def plane_third_kernel(spot, place_ref, keep_x, got_x, keep_y, got_y, *outs):
    blocks, half = keep_x.shape[1:3]
    bit = place_ref[spot]
    for i in range(blocks // 2):
        for out, j in ((outs[0], 2 * i + bit), (outs[1], 2 * i + 1 - bit)):
            out[0, i, :half] = (keep_x[0, j].astype(f32) + got_x[0, j].astype(f32)).astype(bf16)
            out[0, i, half:] = (keep_y[0, j].astype(f32) + got_y[0, j].astype(f32)).astype(bf16)


def quarter_kernel(parts, place_ref, first_ref, second_ref, *outs):
    me = place_ref[0]
    units, blocks, rows = first_ref.shape[:3]
    half = rows // 2
    for u in range(units):
        for i in range(blocks):
            total = (first_ref[u, i].astype(f32) + second_ref[u, i].astype(f32)).astype(bf16)
            for d in range(parts):
                for h in range(2):

                    @pl.when((me ^ d) == 2 * u + h)
                    def _(d=d, h=h, i=i, total=total):
                        outs[d][0, i] = total[h * half : (h + 1) * half]


def last_kernel(terms, place_ref, *refs):
    terms_refs, outs = refs[:terms], refs[terms:]
    total = terms_refs[0][0, 0].astype(f32)
    for ref in terms_refs[1:]:
        total = total + ref[0, 0].astype(f32)
    rows = total.shape[0] - EXTRA
    outs[0][...] = total[:rows]
    outs[1][...] = total[rows:]


def join_kernel(counts, place_ref, *refs):
    refs, outs = refs[:-2], refs[-2:]
    base = at = 0
    for count in counts:
        group = refs[at : at + count]
        at += count
        units, _, rows, _ = group[0].shape
        for u in range(units):
            total = group[0][u, 0].astype(f32)
            for ref in group[1:]:
                total = total + ref[u, 0].astype(f32)
            total = total.astype(bf16)
            outs[0][base + u, 0] = total[: rows // 2]
            outs[1][base + u, 0] = total[rows // 2 :]
        base += units


def both_kernel(place_ref, x_ref, got_x, y_ref, got_y, *outs):
    for out, one, two in ((outs[0], x_ref, got_x), (outs[1], y_ref, got_y)):
        out[...] = (one[...].astype(f32) + two[...].astype(f32)).astype(bf16)


def inner_last_kernel(place_ref, x_ref, got_x, y_ref, got_y, columns_ref, square_ref):
    units, _, half, width = x_ref.shape
    for u in range(units):
        for one, two, place in ((x_ref, got_x, slice(0, half)), (y_ref, got_y, slice(half, 2 * half))):
            total = one[u, 0].astype(f32) + two[u, 0].astype(f32)
            if u < units - 1:
                columns_ref[place, u * width : (u + 1) * width] = total
            else:
                square_ref[place] = total


def finish_kernel(parts, whole_units, place_ref, *refs):
    pieces, outs = refs[:parts], refs[parts:]
    me = place_ref[0]
    rows = pieces[0].shape[2]
    for q in range(parts):
        for d in range(parts):

            @pl.when((me ^ d) == q)
            def _(q=q, d=d):
                out, at = (outs[0], q) if whole_units else (outs[q // 2], q % 2)
                out[at * rows : (at + 1) * rows] = pieces[d][0, 0].astype(f32)


def swap(array, axis, size, distance):
    return lax.ppermute(array, axis, [(i, i ^ distance) for i in range(size)])


def merge_kernel(spot, terms, split, apart, place_ref, *refs):
    terms_refs, outs = refs[:terms], refs[terms:]
    units, blocks = terms_refs[0].shape[:2]
    for u in range(units):

        def total(i):
            found = terms_refs[0][u, i].astype(f32)
            for ref in terms_refs[1:]:
                found = found + ref[u, i].astype(f32)
            return found.astype(bf16)

        if split:
            bit = place_ref[spot]
            for i in range(blocks // 2):
                outs[0][u, i] = total(2 * i + bit)
                outs[1][u, i] = total(2 * i + 1 - bit)
        else:
            for i in range(blocks):
                if apart:
                    outs[u][0, i] = total(i)
                else:
                    outs[0][u, i] = total(i)


def body(
    parts,
    size,
    tokens,
    values,
    lengths,
    merge,
    w_query,
    w_key,
    w_value,
    w_output,
    b_query,
    b_value,
    b_output,
    gain_one,
    shift_one,
    w_inner,
    b_inner,
    w_outer,
    b_outer,
    gain_two,
    shift_two,
    cotangent,
):
    rows, slots, width = tokens.shape
    hidden = w_inner.shape[1]
    share = rows // parts
    span = slots * parts
    count = share * span
    pairs = size // 2
    blk = width // size
    me = lax.axis_index("seq")
    place = lax.axis_index("batch")
    bits = size.bit_length() - 1
    spot = jnp.stack([me] + [(place >> k) & 1 for k in range(bits)]).astype(jnp.int32)
    line = lambda vector: vector.reshape(1, -1)
    low = lambda *shape: Shape(shape, bf16)
    full = lambda *shape: Shape(shape, f32)
    others = range(1, parts)
    call = Sequence()

    def exchange(pieces):
        return [pieces[0]] + [swap(pieces[d], "seq", parts, d) for d in others]

    packed = call(
        functools.partial(pack_kernel, parts),
        [(VM, low(slots, width))] * rows
        + [(SM, Shape((rows,), jnp.int32)), (SM, Shape((share,), jnp.int32))],
        [(SM, spot), (SM, lengths), (VM, tokens), (VM, values), (VM, line(merge))],
        name="pack",
    )
    order, own = packed[rows:]
    x_parts = [exchange(packed[r * parts : (r + 1) * parts]) for r in range(share)]
    cot_parts = exchange(
        call(
            functools.partial(deal_kernel, parts),
            [(VM, low(share, slots + EXTRA, width))] * parts,
            [(SM, spot), (SM, order), (VM, cotangent), (VM, values)],
            name="deal",
        )
    )

    forward = []
    for r in range(share):
        forward.append(
            call(
                functools.partial(forward_kernel, parts, r),
                [(VM, low(2, span, width))]
                + [(VM, low(span, width))] * 3
                + [(VM, full(span, 128)), (VM, full(span, width)), (VM, full(span, 128))],
                [(SM, spot), (SM, own)]
                + [(VM, w) for w in (w_query, w_key, w_value, w_output)]
                + [(VM, line(b)) for b in (b_query, b_value, b_output)]
                + [(VM, x) for x in x_parts[r]],
                limit=28,
                heavy=True,
            name="attention_forward",
            )
        )
    hats = [f[5] for f in forward]
    rstds = [f[6] for f in forward]

    chunk = width
    steps = hidden // chunk
    per_chunk = pairs * width // hidden
    unit_shape = low(parts, pairs, blk, width)
    clip = lambda i: jnp.minimum(i, steps - 1)
    outer_spec = pl.BlockSpec(
        (parts, per_chunk, blk, width), lambda i: (0, jnp.maximum(i - steps, 0), 0, 0)
    )
    fed = call(
        functools.partial(feed_kernel, parts, share, steps),
        [(pl.BlockSpec((1, count, chunk), lambda i: (clip(i), 0, 0)), low(steps, count, chunk))]
        + [(VM, low(count, width))] * 2
        + [(VM, low(share, slots, width))] * parts
        + [(VM, full(8, width)), (VM, full(count, width))]
        + [(outer_spec, unit_shape)] * 2,
        [
            (SM, spot),
            (VM, line(gain_one)),
            (VM, line(shift_one)),
            (pl.BlockSpec((width, chunk), lambda i: (0, clip(i))), w_inner),
            (pl.BlockSpec((1, chunk), lambda i: (0, clip(i))), line(b_inner)),
            (pl.BlockSpec((chunk, width), lambda i: (clip(i), 0)), w_outer),
            (VM, line(b_outer)),
            (VM, line(gain_two)),
            (VM, line(shift_two)),
        ]
        + [(VM, hat) for hat in hats]
        + [(VM, c) for c in cot_parts],
        scratch=[pltpu.VMEM((count, hidden), bf16)] + [pltpu.VMEM((count, width), bf16)] * 2,
        grid=(2 * steps,),
        limit=44,
        heavy=True,
            name="feed_forward",
    )
    slope, normed_low, d_branch = fed[:3]
    out_parts = exchange(fed[3 : 3 + parts])
    sums_two, d_summed, outer_keep, outer_send = fed[3 + parts :]
    outer_got = swap(outer_send, "batch", size, 1)

    def feed_back(start, units, before, last):
        found = units + 1 if last else units
        unit = lambda i: start + jnp.minimum(i, units - 1)
        outs = [
            (pl.BlockSpec((1, pairs, blk, width), lambda i: (i, 0, 0, 0)), low(found, pairs, blk, width))
        ] * 2 + [
            (pl.BlockSpec((1, width), lambda i: (0, unit(i) - start)), full(1, units * width)),
            (VM, full(count, width)),
        ]
        ins = [
            (SM, spot),
            (VM, d_branch),
            (VM, before),
            (VM, normed_low),
            (pl.BlockSpec((1, count, width), lambda i: (unit(i), 0, 0)), slope),
            (pl.BlockSpec((width, width), lambda i: (0, unit(i))), w_inner),
            (pl.BlockSpec((width, width), lambda i: (unit(i), 0)), w_outer),
        ]
        if last:
            ins += [(VM, hat) for hat in hats] + [(VM, rstd) for rstd in rstds]
            ins += [(pl.BlockSpec((1, span, width), lambda i: (0, 0, 0)), f[0]) for f in forward]
            ins += [(VM, line(gain_one))]
            outs += [(VM, low(count, width)), (VM, full(8, width))]
        return call(
            functools.partial(feed_back_kernel, share, units, last),
            outs,
            ins,
            scratch=[pltpu.VMEM((count, width), bf16)],
            grid=(found,),
            limit=40,
            heavy=True,
            name="feed_backward",
        )

    def unit_grads(start, units, vectors=None):
        rows = blk if vectors is None else blk + EXTRA
        return call(
            functools.partial(unit_grad_kernel, share),
            [
                (pl.BlockSpec((1, pairs, rows, width), lambda i: (i, 0, 0, 0)), low(units, pairs, rows, width))
            ]
            * 2,
            [(SM, spot)]
            + [(pl.BlockSpec((1, span, width), lambda i: (1, 0, 0)), f[0]) for f in forward]
            + [(pl.BlockSpec((1, span, width), lambda i: (start + i, 0, 0)), g) for g in grads]
            + ([] if vectors is None else [(VM, vectors)]),
            grid=(units,),
            limit=24,
            heavy=True,
            name="square_grad",
        )

    def merge_terms(terms, bit=None, apart=False, name=None):
        units, blocks, rows, _ = terms[0].shape
        if bit is not None:
            outs = [low(units, blocks // 2, rows, width)] * 2
        elif apart:
            outs = [low(1, blocks, rows, width)] * units
        else:
            outs = [low(units, blocks, rows, width)]
        return call(
            functools.partial(merge_kernel, 0 if bit is None else 1 + bit, len(terms), bit is not None, apart),
            [(VM, shape) for shape in outs],
            [(SM, spot)] + [(VM, term) for term in terms],
            name=name,
        )

    def send_core(block):
        return swap(block, "batch", size, 1)

    def send_line(keep, send, bit):
        return [keep, swap(send, "batch", size, 1 << bit)]

    def lines(terms, start, name):
        for bit in range(start, bits):
            terms = send_line(*merge_terms(terms, bit, name=name), bit)
        return terms

    def simple(kernel, ins, outs, name, heavy=False):
        return call(
            kernel,
            [(VM, shape) for shape in outs],
            [(SM, spot)] + [(VM, array) for array in ins],
            heavy=heavy,
            name=name,
        )

    def undeal(pieces, r, before=None, row=None):
        place = lambda d, spot, order: (order[(spot[0] ^ d) * share + r], 0, 0)
        ins = [(None, spot), (None, order)] + [(VM, piece) for piece in pieces]
        if before is not None:
            ins += [(pl.BlockSpec(memory_space=pl.ANY), before)]
        return call(
            functools.partial(undeal_kernel, parts, row),
            [(pl.BlockSpec((1, slots, width), place), full(rows, slots, width))],
            ins,
            grid=(parts,),
            prefetch=2,
            alias=None if before is None else {len(ins) - 1: 0},
            name="undeal",
        )[0]

    square = whole((width, width))
    grads, token_parts, sums_zero = [], [], []

    def backward(r):
        xc, query, key, value, lse = forward[r][:5]
        by_row = pl.BlockSpec((span, width), lambda i: (r, 0))
        value_spec = pl.BlockSpec((1, EXTRA, width), lambda i: (r, slots // EXTRA, 0))
        back = call(
            functools.partial(backward_kernel, parts, r),
            [(VM, low(3, span, width))]
            + [(VM, low(slots, width))] * parts
            + [(VM, full(8, width))],
            [(SM, spot), (SM, own), (pl.BlockSpec((1, span, width), lambda i: (0, 0, 0)), xc)]
            + [(VM, array) for array in (query, key, value, lse)]
            + [(by_row, d_attn), (by_row, d_attended)]
            + [(square, w) for w in (w_query, w_key, w_value, w_output)]
            + [(value_spec, c) for c in cot_parts],
            scratch=[pltpu.VMEM((span, width), bf16)] * 2 + [pltpu.VMEM((EXTRA, span), bf16)],
            grid=(1,),
            limit=32,
            heavy=True,
            name="attention_backward",
        )
        grads.append(back[0])
        token_parts.append(exchange(back[1 : 1 + parts]))
        sums_zero.append(back[1 + parts])

    half = parts // 2
    *inner_first, bias_first, partial = feed_back(0, half, d_summed, False)
    first_got = send_core(inner_first[1])
    layer_out = None
    for r in range(share):
        layer_out = undeal(out_parts, r, layer_out, r)
    keep_x, send_x, keep_y, send_y = simple(
        plane_first_kernel, [outer_keep, outer_got], [low(2, pairs, blk // 2, width)] * 4, "outer_core", True
    )
    got_x, got_y = swap(send_x, "seq", parts, 1), swap(send_y, "seq", parts, 2)
    first_line = send_line(*merge_terms([inner_first[0], first_got], 1, name="inner_core"), 1)
    *inner_rest, bias_rest, d_attended, d_attn, sums_one = feed_back(half, parts - half, partial, True)
    rest_got = send_core(inner_rest[1])
    first_line = lines(first_line, 2, "inner_line")
    keep_x, send_x, keep_y, send_y = simple(
        plane_second_kernel,
        [keep_x, got_x, keep_y, got_y],
        [low(1, pairs, blk // 2, width)] * 4,
        "outer_plane",
        True,
    )
    got_x, got_y = swap(send_x, "seq", parts, 2), swap(send_y, "seq", parts, 1)
    rest_line = send_line(*merge_terms([inner_rest[0], rest_got], 1, name="inner_core"), 1)
    backward(0)
    outer_line = send_line(
        *simple(
            functools.partial(plane_third_kernel, 2),
            [keep_x, got_x, keep_y, got_y],
            [low(1, pairs // 2, blk, width)] * 2,
            "outer_plane",
        ),
        1,
    )
    rest_line = lines(rest_line, 2, "inner_line")
    (first_sum,) = merge_terms(first_line, name="inner_line")
    grad_tokens = None
    for r in range(1, share):
        backward(r)
        grad_tokens = undeal(token_parts[r - 1], r - 1, grad_tokens)
    outer_line = lines(outer_line, 2, "outer_line")

    per_row = -(-(9 * blk + hidden // size) // width)
    nine = jnp.concatenate([sums_two[:3], sums_one[:3], sum(sums_zero)[:3]], axis=0)
    vectors = jnp.concatenate(
        [
            nine.reshape(9, size, blk).transpose(1, 0, 2).reshape(size, 9 * blk),
            jnp.concatenate([bias_first, bias_rest], axis=1).reshape(size, hidden // size),
        ],
        axis=1,
    )
    used = vectors.shape[1]
    vectors = jnp.pad(vectors, ((0, 0), (0, per_row * width - used))).reshape(size, per_row, width)

    query_keep, query_send = unit_grads(0, 1, vectors)
    query_got = send_core(query_send)
    pair_keep, pair_send = unit_grads(1, 2)
    pair_got = send_core(pair_send)
    grad_tokens = undeal(token_parts[-1], share - 1, grad_tokens)
    (outer_block,) = merge_terms(outer_line, name="outer_line")
    outer_all = exchange([outer_block] * parts)
    query_line = send_line(*merge_terms([query_keep, query_got], 1, name="query_core"), 1)
    inner_x, inner_y = simple(
        functools.partial(join_kernel, (1, 2)),
        [first_sum, *rest_line],
        [low(parts + 1, 1, blk // 2, width)] * 2,
        "inner_join",
        True,
    )
    got_x, got_y = swap(inner_x, "seq", parts, 1), swap(inner_y, "seq", parts, 2)
    pair_planes = exchange(
        simple(
            functools.partial(quarter_kernel, parts),
            [pair_keep, pair_got],
            [low(1, pairs, blk // 2, width)] * parts,
            "pair_core",
        )
    )
    (grad_w_outer,) = simple(
        functools.partial(finish_kernel, parts, True),
        outer_all,
        [full(parts * blk, width)],
        "outer_finish",
    )
    query_line = lines(query_line, 2, "query_line")
    inner_x, inner_y = simple(
        both_kernel,
        [inner_x, got_x, inner_y, got_y],
        [low(parts + 1, 1, blk // 2, width)] * 2,
        "inner_plane",
    )
    got_x, got_y = swap(inner_x, "seq", parts, 2), swap(inner_y, "seq", parts, 1)
    pair_line = send_line(*merge_terms(pair_planes, 1, name="pair_plane"), 1)
    (query_block,) = merge_terms(query_line, name="query_line")
    query_all = exchange([query_block] * parts)
    for bit in range(2, bits):
        pair_line = send_line(*merge_terms(pair_line, bit, name="pair_line"), bit)
    grad_w_inner, grad_w_output = simple(
        inner_last_kernel,
        [inner_x, got_x, inner_y, got_y],
        [full(blk, parts * width), full(blk, width)],
        "inner_finish",
    )
    (pair_block,) = merge_terms(pair_line, name="pair_line")
    pair_all = exchange([pair_block] * parts)
    grad_w_query, vectors = simple(
        functools.partial(last_kernel, parts),
        query_all,
        [full(blk, width), full(EXTRA, width)],
        "query_finish",
    )
    grad_w_key, grad_w_value = simple(
        functools.partial(finish_kernel, parts, False),
        pair_all,
        [full(blk, width)] * 2,
        "pair_finish",
    )
    vectors = vectors.reshape(-1)
    nine = [vectors[i * blk : (i + 1) * blk] for i in range(9)]
    grad_gain_two, grad_shift_two, grad_b_outer = nine[:3]
    grad_gain_one, grad_shift_one, grad_b_output = nine[3:6]
    grad_b_query, grad_b_value, grad_merge = nine[6:]
    return (
        layer_out,
        grad_tokens,
        grad_merge,
        grad_w_query,
        grad_w_key,
        grad_w_value,
        grad_w_output,
        grad_b_query,
        grad_b_value,
        grad_b_output,
        grad_gain_one,
        grad_shift_one,
        grad_w_inner,
        vectors[9 * blk : used],
        grad_w_outer,
        grad_b_outer,
        grad_gain_two,
        grad_shift_two,
    )


def solution(mesh):
    parts, size = mesh.shape["seq"], mesh.shape["batch"]
    rowwise = P("batch", "seq", None)
    in_specs = (rowwise, P("batch", "seq"), P("batch")) + (P(),) * 16 + (rowwise,)
    matrix, vector = P("batch", None), P("batch")
    out_specs = (
        (rowwise, rowwise, vector)
        + (matrix,) * 4
        + (vector,) * 5
        + (matrix, vector, matrix)
        + (vector,) * 3
    )
    return jax.shard_map(
        functools.partial(body, parts, size),
        mesh=mesh,
        in_specs=in_specs,
        out_specs=out_specs,
        check_vma=False,
    )
```

```python
import functools

import jax
import jax.numpy as jnp
from jax import lax
from jax.experimental import pallas as pl
from jax.experimental.pallas import tpu as pltpu
from jax.sharding import PartitionSpec as P

DH = 64
LOG2E = 1.4426950408889634
RSQRT2 = 0.7071067811865476
RSQRT2PI = 0.3989422804014327
EPS = 1e-05
EXTRA = 16
bf16 = jnp.bfloat16
f32 = jnp.float32
NN = (((1,), (0,)), ((), ()))
NT = (((1,), (1,)), ((), ()))
TN = (((0,), (0,)), ((), ()))
Shape = jax.ShapeDtypeStruct
VM = pl.BlockSpec(memory_space=pltpu.VMEM)
SM = pl.BlockSpec(memory_space=pltpu.SMEM)
ANY = pl.BlockSpec(memory_space=pl.ANY)
HBM = pl.BlockSpec(memory_space=pltpu.HBM)
BLOCK = 256


def dot(left, right, dims=NN):
    return lax.dot_general(left, right, dims, preferred_element_type=f32)


def params(limit, *semantics):
    return pltpu.CompilerParams(
        vmem_limit_bytes=limit * 1024 * 1024, dimension_semantics=semantics or None
    )


class Sequence:
    def __init__(self):
        self.last = ()

    def __call__(
        self, kernel, outs, ins, scratch=(), grid=None, prefetch=0, limit=6, alias=None, heavy=False, name=None
    ):
        count, extra = len(ins), len(self.last)

        outs = [*outs, (ANY, Shape((8, 128), f32))]
        results = len(outs) - 1

        def run(*refs):
            refs = refs[:count] + refs[count + extra :]
            kernel(*refs[: count + results], *refs[count + results + 1 :])

        *got, token = pl.pallas_call(
            run,
            grid_spec=pltpu.PrefetchScalarGridSpec(
                num_scalar_prefetch=prefetch,
                grid=grid or (),
                in_specs=[spec for spec, _ in ins[prefetch:]]
                + [ANY] * extra,
                out_specs=[spec for spec, _ in outs],
                scratch_shapes=list(scratch),
            ),
            out_shape=[shape for _, shape in outs],
            input_output_aliases=alias or {},
            compiler_params=params(limit, *(["arbitrary"] * len(grid or ()))),
            cost_estimate=pl.CostEstimate(
                flops=10**12 if heavy else 10**3,
                transcendentals=0,
                bytes_accessed=10**9 if heavy else 10**3,
            ),
            name=name,
        )(*[array for _, array in ins], *self.last)
        self.last = (token,)
        return got


class Moves:
    def __init__(self, semaphores):
        self.semaphores = semaphores
        self.used = 0
        self.out = []

    def start(self, source, target):
        copy = pltpu.make_async_copy(source, target, self.semaphores.at[self.used])
        self.used += 1
        copy.start()
        return copy

    def send(self, source, target):
        self.out.append(self.start(source, target))

    def finish(self):
        for copy in self.out:
            copy.wait()


class Unpack:
    def __init__(self, moves, pieces, target, low_ref, full_ref):
        self.moves, self.target, self.low_ref, self.full_ref = moves, target, low_ref, full_ref
        self.coming = [moves.start(piece, low_ref.at[k]) for k, piece in enumerate(pieces)]

    def run(self, places):
        for k, place in enumerate(places):
            self.coming[k].wait()
            self.full_ref[k] = self.low_ref[k].astype(f32)
            self.moves.send(self.full_ref.at[k], self.target.at[place])


def row_sum(block):
    return jnp.sum(block, axis=0, keepdims=True)


def pack_kernel(parts, place_ref, lengths_ref, tokens_ref, values_ref, merge_ref, *outs):
    order_ref, own_ref = outs[-2:]
    rows = tokens_ref.shape[0]
    share = rows // parts
    me = place_ref[0]
    for i in range(rows):
        rank = jnp.int32(0)
        for j in range(rows):
            if j != i:
                ahead = lengths_ref[j] >= lengths_ref[i] if j < i else lengths_ref[j] > lengths_ref[i]
                rank = rank + ahead.astype(jnp.int32)
        turn = rank // parts
        spot = rank % parts
        owner = jnp.where(turn % 2 == 0, spot, parts - 1 - spot)
        order_ref[owner * share + turn] = jnp.int32(i)
    for r in range(share):
        own_ref[r] = lengths_ref[order_ref[me * share + r]]
    columns = values_ref[...].T
    lane = lax.broadcasted_iota(jnp.int32, columns.shape, 1)
    for r in range(share):
        for d in range(parts):
            row = order_ref[(me ^ d) * share + r]
            column = jnp.sum(jnp.where(lane == row, columns, 0.0), axis=1, keepdims=True)
            outs[r * parts + d][...] = (
                tokens_ref[row].astype(f32) + column * merge_ref[...]
            ).astype(bf16)


def deal_kernel(parts, place_ref, order_ref, source_ref, values_ref, *sends):
    rows, slots, width = source_ref.shape
    share = rows // parts
    me = place_ref[0]
    for d in range(parts):
        for r in range(share):
            row = order_ref[(me ^ d) * share + r]
            sends[d][r, :slots] = source_ref[row]
            value = values_ref[pl.ds(row, 1), :]
            high = value.astype(bf16).astype(f32)
            rest = value - high
            middle = rest.astype(bf16).astype(f32)
            three = jnp.concatenate(
                [high, middle, rest - middle, jnp.zeros((EXTRA - 3, slots), f32)], axis=0
            )
            if width > slots:
                three = jnp.concatenate([three, jnp.zeros((EXTRA, width - slots), f32)], axis=1)
            sends[d][r, slots:] = three.astype(bf16)


def undeal_kernel(parts, share, place_ref, order_ref, *refs):
    pieces, (out_hbm, low_ref, full_ref, sems) = refs[:parts], refs[parts:]
    moves = Moves(sems)
    me = place_ref[0]
    places = [(d, r) for d in range(parts) for r in range(share)]
    unpack = Unpack(moves, [pieces[d].at[r] for d, r in places], out_hbm, low_ref, full_ref)
    unpack.run([order_ref[(me ^ d) * share + r] for d, r in places])
    moves.finish()


def attend(length, q_ref, k_ref, v_ref, put_context, lse_ref):
    pairs, span, _ = q_ref.shape
    c = LOG2E / DH**0.5
    lane = lax.broadcasted_iota(jnp.int32, (1, 128), 1)
    low = lane < DH

    def branch(n):
        def pair(p, carry):
            sl = pl.ds(pl.multiple_of(p * 128, 128), 128)
            q, k, v = q_ref[p], k_ref[p, :n], v_ref[p, :n]
            real = lax.broadcasted_iota(jnp.int32, (span, 128), 1) + (n - 128) < length
            found, sizes = [], []
            for h in range(2):
                mine = low if h == 0 else ~low
                s = dot(jnp.where(mine, q, jnp.zeros_like(q)), k, NT)
                tail = jnp.where(real, s[:, n - 128 :], -1e30)
                s = jnp.concatenate([s[:, : n - 128], tail], axis=1) if n > 128 else tail
                peak = jnp.max(s, axis=1, keepdims=True) * c
                e = jnp.exp2(s * c - peak)
                total = jnp.sum(e, axis=1, keepdims=True)
                found.append(dot(e.astype(bf16), jnp.where(mine, v, jnp.zeros_like(v))) / total)
                sizes.append(peak + jnp.log2(total))
            put_context(sl, (found[0] + found[1]).astype(bf16))
            kept = jnp.where(lane == 2 * p, sizes[0], lse_ref[...])
            lse_ref[...] = jnp.where(lane == 2 * p + 1, sizes[1], kept)
            return carry

        lse_ref[...] = jnp.zeros_like(lse_ref)
        lax.fori_loop(0, pairs, pair, 0)

    blocks = (length + 127) // 128
    for b in range(1, span // 128 + 1):
        pl.when(blocks == b)(functools.partial(branch, 128 * b))


def attend_back(length, q_ref, k_ref, v_ref, ctx_ref, lse_ref, do_ref, get, put):
    pairs, span, _ = q_ref.shape
    scale = 1.0 / DH**0.5
    c = LOG2E * scale
    lane = lax.broadcasted_iota(jnp.int32, (1, 128), 1)
    low = lane < DH

    def branch(n):
        def pair(p, carry):
            sl = pl.ds(pl.multiple_of(p * 128, 128), 128)
            get(p)
            q, k, v, do = q_ref[p], k_ref[p, :n], v_ref[p, :n], do_ref[:, sl]
            real = lax.broadcasted_iota(jnp.int32, (span, 128), 1) + (n - 128) < length
            product = do.astype(f32) * ctx_ref[:, sl].astype(f32)
            sizes = lse_ref[...]
            dq = dk = dv = 0.0
            for h in range(2):
                mine = low if h == 0 else ~low
                qh = jnp.where(mine, q, jnp.zeros_like(q))
                doh = jnp.where(mine, do, jnp.zeros_like(do))
                kh = jnp.where(mine, k, jnp.zeros_like(k))
                delta = jnp.sum(jnp.where(mine, product, 0.0), axis=1, keepdims=True)
                lse = jnp.sum(jnp.where(lane == 2 * p + h, sizes, 0.0), axis=1, keepdims=True)
                prob = jnp.exp2(dot(qh, k, NT) * c - lse)
                tail = jnp.where(real, prob[:, n - 128 :], 0.0)
                prob = jnp.concatenate([prob[:, : n - 128], tail], axis=1) if n > 128 else tail
                ds = (prob * (dot(doh, v, NT) - delta)).astype(bf16)
                dq = dq + dot(ds, kh)
                dk = dk + dot(ds, qh, TN)
                dv = dv + dot(prob.astype(bf16), doh, TN)
            dk, dv = (dk * scale).astype(bf16), dv.astype(bf16)
            if n < span:
                blank = jnp.zeros((span - n, 128), bf16)
                dk = jnp.concatenate([dk, blank], axis=0)
                dv = jnp.concatenate([dv, blank], axis=0)
            put(p, sl, (dq * scale).astype(bf16), dk, dv)
            return carry

        lax.fori_loop(0, pairs, pair, 0)

    blocks = (length + 127) // 128
    for b in range(1, span // 128 + 1):
        pl.when(blocks == b)(functools.partial(branch, 128 * b))


def forward_kernel(
    parts, row, place_ref, own_ref, bq_ref, bv_ref, bo_ref, wq_hbm, wk_hbm, wv_hbm, wo_hbm, *refs
):
    pieces = refs[:parts]
    xc_hbm, q_hbm, k_hbm, v_hbm, lse_hbm, hat_hbm, rstd_hbm = refs[parts : parts + 7]
    w_ref, xc_ref, q_ref, k_ref, v_ref, lse_ref, hat_ref, rstd_ref, sems = refs[parts + 7 :]
    moves = Moves(sems)
    me = place_ref[0]
    step = pieces[0].shape[0]
    arriving = []
    for d in range(parts):
        here = pl.ds(pl.multiple_of((me ^ d) * step, step), step)
        arriving.append(moves.start(pieces[d], xc_ref.at[1, here]))
    hbm = (wq_hbm, wk_hbm, wv_hbm, wo_hbm)
    weights = [moves.start(w, w_ref.at[k]) for k, w in enumerate(hbm)]
    for copy in arriving:
        copy.wait()
    moves.send(xc_ref.at[1], xc_hbm.at[1])
    x = xc_ref[1]
    weights[0].wait()

    def by_pair(ref, block):
        for p in range(ref.shape[0]):
            ref[p] = block[:, p * 128 : (p + 1) * 128].astype(bf16)

    by_pair(q_ref, dot(x, w_ref[0]) + bq_ref[...])
    moves.send(q_ref, q_hbm)
    weights[1].wait()
    by_pair(k_ref, dot(x, w_ref[1]))
    moves.send(k_ref, k_hbm)
    weights[2].wait()
    by_pair(v_ref, dot(x, w_ref[2]) + bv_ref[...])
    moves.send(v_ref, v_hbm)

    def put(sl, block):
        xc_ref[0, :, sl] = block

    attend(own_ref[row], q_ref, k_ref, v_ref, put, lse_ref)
    moves.send(xc_ref.at[0], xc_hbm.at[0])
    moves.send(lse_ref, lse_hbm)
    weights[3].wait()
    for i in range(xc_ref.shape[1] // BLOCK):
        sl = slice(i * BLOCK, (i + 1) * BLOCK)
        a = xc_ref[1, sl].astype(f32) + dot(xc_ref[0, sl], w_ref[3]) + bo_ref[...]
        center = a - jnp.mean(a, axis=1, keepdims=True)
        rstd = lax.rsqrt(jnp.mean(center * center, axis=1, keepdims=True) + EPS)
        hat_ref[sl] = center * rstd
        rstd_ref[sl] = jnp.broadcast_to(rstd, (BLOCK, rstd_ref.shape[1]))
        moves.send(hat_ref.at[sl], hat_hbm.at[sl])
    moves.send(rstd_ref, rstd_hbm)
    moves.finish()


def norm_back(g, hat, rstd, gain):
    scaled = g * gain
    first = jnp.mean(scaled, axis=1, keepdims=True)
    second = jnp.mean(scaled * hat, axis=1, keepdims=True)
    return rstd * (scaled - first - hat * second)


def feed_kernel(
    parts,
    share,
    steps,
    place_ref,
    gain_one_ref,
    shift_one_ref,
    wi_ref,
    bi_ref,
    wo_ref,
    bo_ref,
    gain_ref,
    shift_ref,
    *refs,
):
    hats, refs = refs[:share], refs[share:]
    cots, refs = refs[:parts], refs[parts:]
    slope_ref, low_hbm, branch_hbm, summed_hbm, *refs = refs
    outs, refs = refs[:parts], refs[parts:]
    sums_ref, keep_ref, send_ref, total_ref, low_ref, branch_ref, act_ref, cot_ref, out_ref, sems = refs
    step = pl.program_id(0)
    count, width = total_ref.shape
    chunk = wi_ref.shape[1]
    me = place_ref[0]
    slots = outs[0].shape[1]
    span = count // share
    blocks = count // BLOCK

    def place(d, r):
        return pl.ds(pl.multiple_of((r * parts + (me ^ d)) * slots, slots), slots)

    rows = [slice(r * span, (r + 1) * span) for r in range(share)]
    pairs = [(d, r) for d in range(parts) for r in range(share)]
    coming = [(hats[r], total_ref.at[rows[r]]) for r in range(share)]
    coming += [(cots[d].at[r, :slots], cot_ref.at[place(d, r)]) for d, r in pairs]
    going = [(low_ref, low_hbm), (branch_ref, branch_hbm), (total_ref, summed_hbm)]
    going += [(out_ref.at[place(d, r)], outs[d].at[r]) for d, r in pairs]
    copies = [
        pltpu.make_async_copy(source, target, sems.at[k])
        for k, (source, target) in enumerate(coming + going)
    ]
    coming, going = copies[: len(coming)], copies[len(coming) :]

    @pl.when(step == 0)
    def _():
        for copy in coming:
            copy.start()
        for r in range(share):
            coming[r].wait()
            normed = total_ref[rows[r]] * gain_one_ref[...] + shift_one_ref[...]
            low_ref[rows[r]] = normed.astype(bf16)
            total_ref[rows[r]] = normed + bo_ref[...]
        going[0].start()

    def run(last):
        def first(i):
            return dot(low_ref[i * BLOCK : (i + 1) * BLOCK], wi_ref[...]) + bi_ref[...]

        if last:
            for copy in coming[share:]:
                copy.wait()
        ahead = first(0)
        sums = [0.0, 0.0, 0.0]
        for i in range(blocks):
            inner = ahead
            if i + 1 < blocks:
                ahead = first(i + 1)
            sl = slice(i * BLOCK, (i + 1) * BLOCK)
            phi = 0.5 + 0.5 * lax.erf(inner * RSQRT2)
            act = (inner * phi).astype(bf16)
            slope_ref[0, sl] = (phi + inner * (jnp.exp(-0.5 * inner * inner) * RSQRT2PI)).astype(bf16)
            act_ref[sl, pl.ds(pl.multiple_of(step * chunk, chunk), chunk)] = act
            a = total_ref[sl] + dot(act, wo_ref[...])
            if not last:
                total_ref[sl] = a
                continue
            center = a - jnp.mean(a, axis=1, keepdims=True)
            rstd = lax.rsqrt(jnp.mean(center * center, axis=1, keepdims=True) + EPS)
            hat = center * rstd
            out_ref[sl] = (hat * gain_ref[...] + shift_ref[...]).astype(bf16)
            g = cot_ref[sl].astype(f32)
            back = norm_back(g, hat, rstd, gain_ref[...])
            total_ref[sl] = back
            low = back.astype(bf16)
            branch_ref[sl] = low
            for k, term in enumerate((g * hat, g, low.astype(f32))):
                sums[k] = sums[k] + row_sum(term)
        if last:
            for copy in going[1:]:
                copy.start()
            sums_ref[...] = jnp.concatenate(sums + [jnp.zeros((5, width), f32)], axis=0)

    pl.when(step < steps - 1)(functools.partial(run, False))
    pl.when(step == steps - 1)(functools.partial(run, True))

    @pl.when(step >= steps)
    def _():
        here = pl.ds(pl.multiple_of((step - steps) * chunk, chunk), chunk)
        grad = dot(act_ref[:, here], branch_ref[...], TN).astype(bf16)
        core = place_ref[1]
        pairs, height = keep_ref.shape[1], keep_ref.shape[2]
        for z in range(pairs):
            for unit in range(parts):
                base = (2 * z * parts + unit) * height
                even = grad[base : base + height]
                odd = grad[base + parts * height : base + (parts + 1) * height]
                keep_ref[unit ^ me, z] = jnp.where(core == 0, even, odd)
                send_ref[unit ^ me, z] = jnp.where(core == 0, odd, even)

    @pl.when(step == 2 * steps - 1)
    def _():
        for copy in going:
            copy.wait()


def feed_back_kernel(share, place_ref, gain_ref, *refs):
    (branch_hbm, summed_hbm, low_hbm, slope_hbm, wi_hbm, wo_hbm), refs = refs[:6], refs[6:]
    hats_hbm, rstds_hbm, refs = refs[:share], refs[share : 2 * share], refs[2 * share :]
    keep_hbm, send_hbm, bias_ref, attended_hbm, attn_hbm, sums_ref, *refs = refs
    branch_ref, low_ref, slope_ref, wi_ref, wo_ref, inner_ref, total_ref, *refs = refs
    attn_ref, hat_ref, rstd_ref, keep_ref, send_ref, sems = refs
    moves = Moves(sems)
    me = place_ref[0]
    count, width = total_ref.shape
    span = count // share
    blocks = count // BLOCK
    units = slope_ref.shape[0]
    coming = [[] for _ in range(units)]

    def take(u, source, target):
        coming[u].append(moves.start(source, target))

    for u in range(units):
        chunk = slice(u * width, (u + 1) * width)
        take(u, wo_hbm.at[chunk], wo_ref.at[u])
        if u == 0:
            take(u, branch_hbm, branch_ref)
        take(u, slope_hbm.at[u], slope_ref.at[u])
        take(u, wi_hbm.at[:, chunk], wi_ref.at[u])
        if u == 0:
            take(u, summed_hbm, total_ref)
            take(u, low_hbm, low_ref)
    for r in range(share):
        rows = slice(r * span, (r + 1) * span)
        take(units - 1, hats_hbm[r], hat_ref.at[rows])
        take(units - 1, rstds_hbm[r], rstd_ref.at[rows])
    for u in range(units):
        last = u == units - 1
        for copy in coming[u]:
            copy.wait()

        def first(i):
            return dot(branch_ref[i * BLOCK : (i + 1) * BLOCK], wo_ref[u], NT)

        ahead = first(0)
        bias = 0.0
        sums = [0.0, 0.0, 0.0]
        for i in range(blocks):
            now = ahead
            if i + 1 < blocks:
                ahead = first(i + 1)
            sl = slice(i * BLOCK, (i + 1) * BLOCK)
            inner = (now * slope_ref[u, sl].astype(f32)).astype(bf16)
            inner_ref[sl] = inner
            bias = bias + row_sum(inner.astype(f32))
            g = total_ref[sl] + dot(inner, wi_ref[u], NT)
            if not last:
                total_ref[sl] = g
                continue
            hat = hat_ref[sl]
            back = norm_back(g, hat, rstd_ref[sl, :1], gain_ref[...])
            total_ref[sl] = back
            low = back.astype(bf16)
            attn_ref[sl] = low
            for k, term in enumerate((g * hat, g, low.astype(f32))):
                sums[k] = sums[k] + row_sum(term)
        bias_ref[u : u + 1] = bias
        if last:
            moves.send(total_ref, attended_hbm)
            moves.send(attn_ref, attn_hbm)
            sums_ref[...] = jnp.concatenate(sums + [jnp.zeros((5, width), f32)], axis=0)
        grad = dot(low_ref[...], inner_ref[...], TN).astype(bf16)
        put_unit(place_ref[1], grad, keep_ref, send_ref, u)
        moves.send(send_ref.at[u], send_hbm.at[u ^ me])
        moves.send(keep_ref.at[u], keep_hbm.at[u ^ me])
    moves.finish()


def put_unit(core, grad, keep_ref, send_ref, unit):
    pairs = keep_ref.shape[1]
    rows = grad.shape[0] // (2 * pairs)
    for z in range(pairs):
        even = grad[2 * z * rows : (2 * z + 1) * rows]
        odd = grad[(2 * z + 1) * rows : (2 * z + 2) * rows]
        keep_ref[unit, z] = jnp.where(core == 0, even, odd)
        send_ref[unit, z] = jnp.where(core == 0, odd, even)


def square_kernel(share, place_ref, two_ref, one_ref, bias_ref, *refs):
    zeros, refs = refs[:share], refs[share:]
    xc_hbm, grads_hbm, refs = refs[:share], refs[share : 2 * share], refs[2 * share :]
    outs_hbm, (xc_ref, grads_ref, *outs, sems) = refs[:4], refs[4:]
    moves = Moves(sems)
    core = place_ref[1]
    units, span = grads_ref.shape[0], grads_ref.shape[1] // share
    coming = [[] for _ in range(units)]
    for u in range(units):
        for r in range(share):
            rows = slice(r * span, (r + 1) * span)
            if u < 2:
                coming[u].append(moves.start(xc_hbm[r].at[u], xc_ref.at[u, rows]))
            coming[u].append(moves.start(grads_hbm[r].at[u], grads_ref.at[u, rows]))
    zero = zeros[0][0:3]
    for ref in zeros[1:]:
        zero = zero + ref[0:3]
    vectors = jnp.concatenate([two_ref[0:3], one_ref[0:3], zero, bias_ref[...]], axis=0)
    blank = jnp.zeros((EXTRA - vectors.shape[0], vectors.shape[1]), f32)
    vectors = jnp.concatenate([vectors, blank], axis=0)
    for u in range(units):
        for copy in coming[u]:
            copy.wait()
        grad = dot(xc_ref[min(u, 1)], grads_ref[u], TN).astype(bf16)
        group, at = u // 2, u % 2
        keep_ref, send_ref = outs[2 * group : 2 * group + 2]
        pairs, rows, width = keep_ref.shape[1:]
        tail = EXTRA if group == 0 else 0
        rows = rows - tail

        def block(b):
            found = grad[b * rows : (b + 1) * rows]
            if not tail:
                return found
            extra = vectors if u == 0 else jnp.zeros_like(vectors)
            return jnp.concatenate([found.astype(f32), extra], axis=0).astype(bf16)

        for z in range(pairs):
            even, odd = block(2 * z), block(2 * z + 1)
            keep_ref[at, z] = jnp.where(core == 0, even, odd)
            send_ref[at, z] = jnp.where(core == 0, odd, even)
        for k, ref in ((1, send_ref), (0, keep_ref)):
            moves.send(ref.at[at], outs_hbm[2 * group + k].at[at])
    moves.finish()


def backward_kernel(parts, row, place_ref, own_ref, *refs):
    hbm, refs = refs[:11], refs[11:]
    wo_hbm, low_hbm, q_hbm, k_hbm, v_hbm, xc_hbm, lse_hbm, attended_hbm, wq_hbm, wk_hbm, wv_hbm = hbm
    values, refs = refs[:parts], refs[parts:]
    before, refs = (refs[:parts], refs[parts:]) if row else ((), refs)
    grads_hbm, outs, sums_ref, refs = refs[0], refs[1 : 1 + parts], refs[1 + parts], refs[2 + parts :]
    *refs, sems, in_sems = refs
    if row:
        *refs, before_ref = refs
    w_ref, low_ref, qkv_ref, context_ref, lse_ref, attended_ref, grads_ref, do_ref, total_ref, value_ref = refs
    moves = Moves(sems)
    me = place_ref[0]
    slots = outs[0].shape[1]
    span, width = low_ref.shape
    rows = slice(row * span, (row + 1) * span)

    def inward(p, k):
        return pltpu.make_async_copy(
            (q_hbm, k_hbm, v_hbm)[k].at[p], qkv_ref.at[k, p], in_sems.at[p, k]
        )

    early = [moves.start(wo_hbm, w_ref.at[0]), moves.start(low_hbm.at[rows], low_ref)]
    early += [moves.start(lse_hbm, lse_ref), moves.start(xc_hbm.at[0], context_ref)]
    for p in range(width // 128):
        for k in range(3):
            inward(p, k).start()
    late = [moves.start(ref, w_ref.at[1 + k]) for k, ref in enumerate((wq_hbm, wk_hbm, wv_hbm))]
    late.append(moves.start(attended_hbm.at[rows], attended_ref))
    for d, pieces in enumerate(before):
        late.append(moves.start(pieces, before_ref.at[d]))
    for d in range(parts):
        here = pl.ds(pl.multiple_of((me ^ d) * slots, slots), slots)
        late.append(moves.start(values[d].at[row, slots:, :slots], value_ref.at[:, here]))
    for copy in early:
        copy.wait()
    moves.send(low_ref, grads_hbm.at[0])
    do_ref[...] = dot(low_ref[...], w_ref[0], NT).astype(bf16)

    def get(p):
        for k in range(3):
            inward(p, k).wait()

    def put(p, sl, *blocks):
        for k, block in enumerate(blocks):
            grads_ref[k, :, sl] = block

    q_ref, k_ref, v_ref = [qkv_ref.at[k] for k in range(3)]
    attend_back(own_ref[row], q_ref, k_ref, v_ref, context_ref, lse_ref, do_ref, get, put)
    moves.send(grads_ref, grads_hbm.at[pl.ds(1, 3)])
    for copy in late:
        copy.wait()
    for d in range(len(before)):
        moves.send(before_ref.at[d], outs[d].at[pl.ds(0, row)])
    dq, dk, dv = grads_ref[0], grads_ref[1], grads_ref[2]
    low = (
        attended_ref[...]
        + dot(dq, w_ref[1], NT)
        + dot(dk, w_ref[2], NT)
        + dot(dv, w_ref[3], NT)
    ).astype(bf16)
    total_ref[...] = low
    for d in range(parts):
        here = pl.ds(pl.multiple_of((me ^ d) * slots, slots), slots)
        moves.send(total_ref.at[here], outs[d].at[row])
    merge = row_sum(dot(value_ref[...], low))
    sums_ref[...] = jnp.concatenate(
        [
            row_sum(dq.astype(f32)),
            row_sum(dv.astype(f32)),
            merge,
            jnp.zeros((5, merge.shape[1]), f32),
        ],
        axis=0,
    )
    moves.finish()


def plane_first_kernel(place_ref, keep_ref, got_ref, *outs):
    keep_x, send_x, keep_y, send_y = outs
    half = keep_x.shape[2]
    units, blocks = keep_ref.shape[:2]
    for d in range(units):
        for i in range(blocks):
            total = (keep_ref[d, i].astype(f32) + got_ref[d, i].astype(f32)).astype(bf16)
            (send_x if d % 2 else keep_x)[d // 2, i] = total[:half]
            (send_y if d // 2 else keep_y)[d % 2, i] = total[half:]


def plane_second_kernel(groups, place_ref, *refs):
    terms, outs = refs[: 4 * groups], refs[4 * groups :]
    for g in range(groups):
        keep_x, got_x, keep_y, got_y = terms[4 * g : 4 * g + 4]
        for i in range(keep_x.shape[1]):
            for j in range(2):
                outs[j][g, i] = (keep_x[j, i].astype(f32) + got_x[j, i].astype(f32)).astype(bf16)
                outs[2 + j][g, i] = (keep_y[j, i].astype(f32) + got_y[j, i].astype(f32)).astype(bf16)


def plane_third_kernel(spot, place_ref, keep_x, got_x, keep_y, got_y, *outs):
    groups, blocks = keep_x.shape[:2]
    bit = place_ref[spot]
    for g in range(groups):
        for i in range(blocks // 2):
            for out, j in ((outs[0], 2 * i + bit), (outs[1], 2 * i + 1 - bit)):
                top = keep_x[g, j].astype(f32) + got_x[g, j].astype(f32)
                bottom = keep_y[g, j].astype(f32) + got_y[g, j].astype(f32)
                out[g, i] = jnp.concatenate([top, bottom], axis=0).astype(bf16)


def quarter_kernel(parts, place_ref, keep_ref, got_ref, *outs):
    me = place_ref[0]
    units, blocks, rows = keep_ref.shape[:3]
    half = rows // 2
    for u in range(units):
        for i in range(blocks):
            total = (keep_ref[u, i].astype(f32) + got_ref[u, i].astype(f32)).astype(bf16)
            for d in range(parts):
                for h in range(2):

                    @pl.when((me ^ d) == 2 * u + h)
                    def _(d=d, h=h, i=i, total=total):
                        outs[d][0, i] = total[h * half : (h + 1) * half]


def total_kernel(parts, rows, place_ref, *refs):
    pieces, outs = refs[:parts], refs[parts:]
    for u in range(2):
        total = pieces[0][u, 0].astype(f32)
        for piece in pieces[1:]:
            total = total + piece[u, 0].astype(f32)
        outs[u][...] = total[:rows]
        if u == 0:
            outs[2][...] = total[rows:]


def fourth_kernel(parts, bit_spot, place_ref, *refs):
    pieces, outs = refs[:parts], refs[parts:]
    blocks = pieces[0].shape[1]
    bit = place_ref[bit_spot]

    def total(i):
        found = pieces[0][0, i].astype(f32)
        for piece in pieces[1:]:
            found = found + piece[0, i].astype(f32)
        return found.astype(bf16)

    for i in range(blocks // 2):
        outs[0][0, i] = total(2 * i + bit)
        outs[1][0, i] = total(2 * i + 1 - bit)


def merge_kernel(spot, place_ref, keep_ref, got_ref, *outs):
    groups, blocks = keep_ref.shape[:2]

    def total(g, i):
        return (keep_ref[g, i].astype(f32) + got_ref[g, i].astype(f32)).astype(bf16)

    for g in range(groups):
        if spot is None:
            for i in range(blocks):
                outs[0][g, i] = total(g, i)
            continue
        bit = place_ref[spot]
        for i in range(blocks // 2):
            outs[0][g, i] = total(g, 2 * i + bit)
            outs[1][g, i] = total(g, 2 * i + 1 - bit)


def finish_kernel(parts, place_ref, *refs):
    pieces, outs = refs[:parts], refs[parts:]
    me = place_ref[0]
    rows, width = pieces[0].shape[2:]
    for q in range(parts):
        for d in range(parts):

            @pl.when((me ^ d) == q)
            def _(q=q, d=d):
                if pieces[d].shape[0] == 2:
                    outs[0][q * rows : (q + 1) * rows] = pieces[d][0, 0].astype(f32)
                    outs[1][:, q * width : (q + 1) * width] = pieces[d][1, 0].astype(f32)
                else:
                    outs[q // 2][q % 2 * rows : (q % 2 + 1) * rows] = pieces[d][0, 0].astype(f32)


def swap(array, axis, size, distance):
    return lax.ppermute(array, axis, [(i, i ^ distance) for i in range(size)])


def body(
    parts,
    size,
    tokens,
    values,
    lengths,
    merge,
    w_query,
    w_key,
    w_value,
    w_output,
    b_query,
    b_value,
    b_output,
    gain_one,
    shift_one,
    w_inner,
    b_inner,
    w_outer,
    b_outer,
    gain_two,
    shift_two,
    cotangent,
):
    rows, slots, width = tokens.shape
    hidden = w_inner.shape[1]
    share = rows // parts
    span = slots * parts
    count = share * span
    pairs = size // 2
    blk = width // size
    me = lax.axis_index("seq")
    place = lax.axis_index("batch")
    bits = size.bit_length() - 1
    spot = jnp.stack([me] + [(place >> k) & 1 for k in range(bits)]).astype(jnp.int32)
    line = lambda vector: vector.reshape(1, -1)
    low = lambda *shape: Shape(shape, bf16)
    full = lambda *shape: Shape(shape, f32)
    others = range(1, parts)
    call = Sequence()

    def exchange(pieces):
        return [pieces[0]] + [swap(pieces[d], "seq", parts, d) for d in others]

    packed = call(
        functools.partial(pack_kernel, parts),
        [(VM, low(slots, width))] * rows
        + [(SM, Shape((rows,), jnp.int32)), (SM, Shape((share,), jnp.int32))],
        [(SM, spot), (SM, lengths), (VM, tokens), (VM, values), (VM, line(merge))],
        name="pack",
    )
    order, own = packed[rows:]
    x_parts = [exchange(packed[r * parts : (r + 1) * parts]) for r in range(share)]
    cot_parts = exchange(
        call(
            functools.partial(deal_kernel, parts),
            [(VM, low(share, slots + EXTRA, width))] * parts,
            [(SM, spot), (SM, order), (VM, cotangent), (VM, values)],
            name="deal",
        )
    )

    forward = []
    DMA = pltpu.SemaphoreType.DMA
    for r in range(share):
        results = (
            [low(2, span, width)]
            + [low(width // 128, span, 128)] * 3
            + [full(span, 128), full(span, width), full(span, 128)]
        )
        forward.append(
            call(
                functools.partial(forward_kernel, parts, r),
                [(HBM, shape) for shape in results],
                [(SM, spot), (SM, own)]
                + [(VM, line(b)) for b in (b_query, b_value, b_output)]
                + [(HBM, w) for w in (w_query, w_key, w_value, w_output)]
                + [(HBM, x) for x in x_parts[r]],
                scratch=[pltpu.VMEM((4, width, width), bf16)]
                + [pltpu.VMEM(shape.shape, shape.dtype) for shape in results]
                + [DMA((4 + parts + 2 * parts + 6,))],
                limit=60,
                heavy=True,
                name="attention_forward",
            )
        )
    hats = [f[5] for f in forward]
    rstds = [f[6] for f in forward]

    chunk = width
    steps = hidden // chunk
    clip = lambda i: jnp.minimum(i, steps - 1)
    tall_low, tall_full = low(count, width), full(count, width)
    piece_low = low(share, slots, width)
    unit_low = low(parts, pairs, blk, width)
    outer_spec = pl.BlockSpec(
        (parts, pairs // steps, blk, width), lambda i: (0, jnp.maximum(i - steps, 0), 0, 0)
    )
    fed = call(
        functools.partial(feed_kernel, parts, share, steps),
        [(pl.BlockSpec((1, count, chunk), lambda i: (clip(i), 0, 0)), low(steps, count, chunk))]
        + [(HBM, tall_low), (HBM, tall_low), (HBM, tall_full)]
        + [(HBM, piece_low)] * parts
        + [(VM, full(8, width))]
        + [(outer_spec, unit_low)] * 2,
        [
            (SM, spot),
            (VM, line(gain_one)),
            (VM, line(shift_one)),
            (pl.BlockSpec((width, chunk), lambda i: (0, clip(i))), w_inner),
            (pl.BlockSpec((1, chunk), lambda i: (0, clip(i))), line(b_inner)),
            (pl.BlockSpec((chunk, width), lambda i: (clip(i), 0)), w_outer),
            (VM, line(b_outer)),
            (VM, line(gain_two)),
            (VM, line(shift_two)),
        ]
        + [(HBM, hat) for hat in hats]
        + [(HBM, c) for c in cot_parts],
        scratch=[pltpu.VMEM((count, width), f32)]
        + [pltpu.VMEM((count, width), bf16)] * 2
        + [pltpu.VMEM((count, hidden), bf16)]
        + [pltpu.VMEM((count, width), bf16)] * 2
        + [DMA((share + 3 + 2 * share * parts,))],
        grid=(2 * steps,),
        limit=60,
        heavy=True,
        name="feed_forward",
    )
    slope, normed_low, d_branch, d_summed = fed[:4]
    out_parts = exchange(fed[4 : 4 + parts])
    sums_two, outer_keep, outer_send = fed[4 + parts :]
    outer_got = swap(outer_send, "batch", size, 1)

    inner_keep, inner_send, inner_bias, d_attended, d_attn, sums_one = call(
        functools.partial(feed_back_kernel, share),
        [(HBM, unit_low)] * 2
        + [(VM, full(steps, width)), (HBM, tall_full), (HBM, tall_low), (VM, full(8, width))],
        [(SM, spot), (VM, line(gain_one))]
        + [(HBM, a) for a in (d_branch, d_summed, normed_low, slope, w_inner, w_outer)]
        + [(HBM, hat) for hat in hats]
        + [(HBM, rstd) for rstd in rstds],
        scratch=[pltpu.VMEM((count, width), bf16)] * 2
        + [pltpu.VMEM((steps, count, width), bf16)]
        + [pltpu.VMEM((steps, width, width), bf16)] * 2
        + [pltpu.VMEM((count, width), bf16), pltpu.VMEM((count, width), f32)]
        + [pltpu.VMEM((count, width), bf16), pltpu.VMEM((count, width), f32)]
        + [pltpu.VMEM((count, 128), f32)]
        + [pltpu.VMEM(unit_low.shape, bf16)] * 2
        + [DMA((3 * steps + 3 + 2 * share + 2 + 2 * steps,))],
        limit=60,
        heavy=True,
        name="feed_backward",
    )
    inner_got = swap(inner_send, "batch", size, 1)

    def simple(kernel, ins, outs, name, heavy=False):
        return call(
            kernel,
            [(VM, shape) for shape in outs],
            [(SM, spot)] + [(VM, array) for array in ins],
            heavy=heavy,
            name=name,
        )

    def plane_first(keep, got, name):
        rows = keep.shape[2]
        first, rest = low(2, pairs, blk // 2, width), low(2, pairs, rows - blk // 2, width)
        keep_x, send_x, keep_y, send_y = simple(
            plane_first_kernel, [keep, got], [first, first, rest, rest], name
        )
        return keep_x, swap(send_x, "seq", parts, 1), keep_y, swap(send_y, "seq", parts, 2)

    def plane_second(groups, name):
        count = len(groups)
        first, rest = [low(count, *groups[0][k].shape[1:]) for k in (0, 2)]
        keep_x, send_x, keep_y, send_y = simple(
            functools.partial(plane_second_kernel, count),
            [term for terms in groups for term in terms],
            [first, first, rest, rest],
            name,
        )
        return keep_x, swap(send_x, "seq", parts, 2), keep_y, swap(send_y, "seq", parts, 1)

    def plane_third(terms, name):
        shape = low(terms[0].shape[0], pairs // 2, terms[0].shape[2] + terms[2].shape[2], width)
        keep, send = simple(
            functools.partial(plane_third_kernel, 2), list(terms), [shape, shape], name
        )
        return keep, swap(send, "batch", size, 2)

    def merge_terms(spot_index, terms, name):
        groups, blocks, rows, _ = terms[0].shape
        if spot_index is None:
            shapes = [low(groups, blocks, rows, width)]
        else:
            shapes = [low(groups, blocks // 2, rows, width)] * 2
        kernel = functools.partial(merge_kernel, spot_index)
        return simple(kernel, terms, shapes, name)

    def along_line(terms, name):
        for bit in range(2, bits):
            keep, send = merge_terms(1 + bit, terms, name)
            terms = keep, swap(send, "batch", size, 1 << bit)
        return terms

    def gather(terms, name):
        (block,) = merge_terms(None, terms, name)
        return exchange([block] * parts)

    def undeal(pieces):
        return call(
            functools.partial(undeal_kernel, parts, share),
            [(HBM, full(rows, slots, width))],
            [(SM, spot), (SM, order)] + [(HBM, piece) for piece in pieces],
            scratch=[pltpu.VMEM((rows, slots, width), dtype) for dtype in (bf16, f32)]
            + [DMA((2 * rows,))],
            limit=16,
            heavy=True,
            name="undeal",
        )[0]

    layer_out = undeal(out_parts)
    outer_terms = plane_first(outer_keep, outer_got, "outer_core")
    inner_terms = plane_first(inner_keep, inner_got, "inner_core")

    grads, token_parts, sums_zero = [], [], []
    pair_count = width // 128
    for r in range(share):
        xc, query, key, value, lse = forward[r][:5]
        back = call(
            functools.partial(backward_kernel, parts, r),
            [(HBM, low(4, span, width))]
            + [(HBM, low(r + 1, slots, width))] * parts
            + [(VM, full(8, width))],
            [(SM, spot), (SM, own)]
            + [(HBM, array) for array in (w_output, d_attn, query, key, value, xc, lse, d_attended)]
            + [(HBM, w) for w in (w_query, w_key, w_value)]
            + [(HBM, c) for c in cot_parts]
            + [(HBM, piece) for piece in token_parts],
            scratch=[
                pltpu.VMEM((4, width, width), bf16),
                pltpu.VMEM((span, width), bf16),
                pltpu.VMEM((3, pair_count, span, 128), bf16),
                pltpu.VMEM((span, width), bf16),
                pltpu.VMEM((span, 128), f32),
                pltpu.VMEM((span, width), f32),
                pltpu.VMEM((3, span, width), bf16),
                pltpu.VMEM((span, width), bf16),
                pltpu.VMEM((span, width), bf16),
                pltpu.VMEM((EXTRA, span), bf16),
            ]
            + ([pltpu.VMEM((parts, r, slots, width), bf16)] if r else [])
            + [DMA((10 + 4 * parts,)), DMA((pair_count, 3))],
            limit=60,
            heavy=True,
            name="attention_backward",
        )
        grads.append(back[0])
        token_parts = back[1 : 1 + parts]
        sums_zero.append(back[1 + parts])
        if r == 0:
            feed_terms = plane_second([outer_terms, inner_terms], "feed_plane")
    feed_terms = plane_third(feed_terms, "feed_plane")
    token_parts = exchange(token_parts)

    early_low, late_low = low(2, pairs, blk + EXTRA, width), low(2, pairs, blk, width)
    early_keep, early_send, late_keep, late_send = call(
        functools.partial(square_kernel, share),
        [(HBM, early_low)] * 2 + [(HBM, late_low)] * 2,
        [(SM, spot)]
        + [(VM, sums) for sums in (sums_two, sums_one, inner_bias, *sums_zero)]
        + [(HBM, f[0]) for f in forward]
        + [(HBM, g) for g in grads],
        scratch=[pltpu.VMEM((2, count, width), bf16), pltpu.VMEM((4, count, width), bf16)]
        + [pltpu.VMEM(early_low.shape, bf16)] * 2
        + [pltpu.VMEM(late_low.shape, bf16)] * 2
        + [DMA((6 * share + 8,))],
        limit=60,
        heavy=True,
        name="square_grad",
    )
    early_got = swap(early_send, "batch", size, 1)
    late_got = swap(late_send, "batch", size, 1)
    feed_terms = along_line(feed_terms, "feed_line")
    grad_tokens = undeal(token_parts)
    early_terms = merge_terms(2, [early_keep, early_got], "early_core")
    early_terms = early_terms[0], swap(early_terms[1], "batch", size, 2)
    quarters = exchange(
        simple(
            functools.partial(quarter_kernel, parts),
            [late_keep, late_got],
            [low(1, pairs, blk // 2, width)] * parts,
            "late_core",
        )
    )
    feed_all = gather(feed_terms, "feed_line")
    early_terms = along_line(early_terms, "early_line")
    late_keep, late_send = simple(
        functools.partial(fourth_kernel, parts, 2),
        quarters,
        [low(1, pairs // 2, blk // 2, width)] * 2,
        "late_plane",
    )
    late_terms = late_keep, swap(late_send, "batch", size, 2)
    grad_w_outer, grad_w_inner = simple(
        functools.partial(finish_kernel, parts),
        feed_all,
        [full(parts * blk, width), full(blk, parts * width)],
        "feed_finish",
    )
    late_terms = along_line(late_terms, "late_line")
    late_all = gather(late_terms, "late_line")
    early_all = gather(early_terms, "early_line")
    grad_w_key, grad_w_value = simple(
        functools.partial(finish_kernel, parts), late_all, [full(blk, width)] * 2, "late_finish"
    )
    grad_w_output, grad_w_query, vectors = simple(
        functools.partial(total_kernel, parts, blk),
        early_all,
        [full(blk, width)] * 2 + [full(EXTRA, width)],
        "early_finish",
    )
    nine = lax.dynamic_slice(vectors, (0, place * blk), (9, blk))
    grad_b_inner = lax.dynamic_slice(
        vectors[9 : 9 + steps].reshape(-1), (place * (hidden // size),), (hidden // size,)
    )
    grad_gain_two, grad_shift_two, grad_b_outer = nine[0], nine[1], nine[2]
    grad_gain_one, grad_shift_one, grad_b_output = nine[3], nine[4], nine[5]
    grad_b_query, grad_b_value, grad_merge = nine[6], nine[7], nine[8]
    return (
        layer_out,
        grad_tokens,
        grad_merge,
        grad_w_query,
        grad_w_key,
        grad_w_value,
        grad_w_output,
        grad_b_query,
        grad_b_value,
        grad_b_output,
        grad_gain_one,
        grad_shift_one,
        grad_w_inner,
        grad_b_inner,
        grad_w_outer,
        grad_b_outer,
        grad_gain_two,
        grad_shift_two,
    )


def solution(mesh):
    parts, size = mesh.shape["seq"], mesh.shape["batch"]
    rowwise = P("batch", "seq", None)
    in_specs = (rowwise, P("batch", "seq"), P("batch")) + (P(),) * 16 + (rowwise,)
    matrix, vector = P("batch", None), P("batch")
    out_specs = (
        (rowwise, rowwise, vector)
        + (matrix,) * 4
        + (vector,) * 5
        + (matrix, vector, matrix)
        + (vector,) * 3
    )
    return jax.shard_map(
        functools.partial(body, parts, size),
        mesh=mesh,
        in_specs=in_specs,
        out_specs=out_specs,
        check_vma=False,
    )
```

```python
import functools

import jax
import jax.numpy as jnp
from jax import lax
from jax.experimental import pallas as pl
from jax.experimental.pallas import tpu as pltpu
from jax.sharding import PartitionSpec as P

DH = 64
LOG2E = 1.4426950408889634
RSQRT2 = 0.7071067811865476
RSQRT2PI = 0.3989422804014327
EPS = 1e-05
EXTRA = 16
bf16 = jnp.bfloat16
f32 = jnp.float32
NN = (((1,), (0,)), ((), ()))
NT = (((1,), (1,)), ((), ()))
TN = (((0,), (0,)), ((), ()))
Shape = jax.ShapeDtypeStruct
VM = pl.BlockSpec(memory_space=pltpu.VMEM)
SM = pl.BlockSpec(memory_space=pltpu.SMEM)
ANY = pl.BlockSpec(memory_space=pl.ANY)
HBM = pl.BlockSpec(memory_space=pltpu.HBM)
BLOCK = 256


def dot(left, right, dims=NN):
    return lax.dot_general(left, right, dims, preferred_element_type=f32)


def params(limit, *semantics):
    return pltpu.CompilerParams(
        vmem_limit_bytes=limit * 1024 * 1024, dimension_semantics=semantics or None
    )


class Sequence:
    def __init__(self):
        self.last = ()

    def __call__(
        self, kernel, outs, ins, scratch=(), grid=None, prefetch=0, limit=6, alias=None, heavy=False, name=None
    ):
        count, extra = len(ins), len(self.last)

        outs = [*outs, (ANY, Shape((8, 128), f32))]
        results = len(outs) - 1

        def run(*refs):
            refs = refs[:count] + refs[count + extra :]
            kernel(*refs[: count + results], *refs[count + results + 1 :])

        *got, token = pl.pallas_call(
            run,
            grid_spec=pltpu.PrefetchScalarGridSpec(
                num_scalar_prefetch=prefetch,
                grid=grid or (),
                in_specs=[spec for spec, _ in ins[prefetch:]]
                + [ANY] * extra,
                out_specs=[spec for spec, _ in outs],
                scratch_shapes=list(scratch),
            ),
            out_shape=[shape for _, shape in outs],
            input_output_aliases=alias or {},
            compiler_params=params(limit, *(["arbitrary"] * len(grid or ()))),
            cost_estimate=pl.CostEstimate(
                flops=10**12 if heavy else 10**3,
                transcendentals=0,
                bytes_accessed=10**9 if heavy else 10**3,
            ),
            name=name,
        )(*[array for _, array in ins], *self.last)
        self.last = (token,)
        return got


class Moves:
    def __init__(self, semaphores):
        self.semaphores = semaphores
        self.used = 0
        self.out = []

    def start(self, source, target):
        copy = pltpu.make_async_copy(source, target, self.semaphores.at[self.used])
        self.used += 1
        copy.start()
        return copy

    def send(self, source, target):
        self.out.append(self.start(source, target))

    def finish(self):
        for copy in self.out:
            copy.wait()


class Unpack:
    def __init__(self, moves, pieces, target, low_ref, full_ref):
        self.moves, self.target, self.low_ref, self.full_ref = moves, target, low_ref, full_ref
        self.coming = [moves.start(piece, low_ref.at[k]) for k, piece in enumerate(pieces)]

    def run(self, places):
        for k, place in enumerate(places):
            self.coming[k].wait()
            self.full_ref[k] = self.low_ref[k].astype(f32)
            self.moves.send(self.full_ref.at[k], self.target.at[place])


def row_sum(block):
    return jnp.sum(block, axis=0, keepdims=True)


def pack_kernel(parts, place_ref, lengths_ref, tokens_ref, values_ref, merge_ref, *outs):
    order_ref, own_ref = outs[-2:]
    rows = tokens_ref.shape[0]
    share = rows // parts
    me = place_ref[0]
    for i in range(rows):
        rank = jnp.int32(0)
        for j in range(rows):
            if j != i:
                ahead = lengths_ref[j] >= lengths_ref[i] if j < i else lengths_ref[j] > lengths_ref[i]
                rank = rank + ahead.astype(jnp.int32)
        turn = rank // parts
        spot = rank % parts
        owner = jnp.where(turn % 2 == 0, spot, parts - 1 - spot)
        order_ref[owner * share + turn] = jnp.int32(i)
    for r in range(share):
        own_ref[r] = lengths_ref[order_ref[me * share + r]]
    columns = values_ref[...].T
    lane = lax.broadcasted_iota(jnp.int32, columns.shape, 1)
    for r in range(share):
        for d in range(parts):
            row = order_ref[(me ^ d) * share + r]
            column = jnp.sum(jnp.where(lane == row, columns, 0.0), axis=1, keepdims=True)
            outs[r * parts + d][...] = (
                tokens_ref[row].astype(f32) + column * merge_ref[...]
            ).astype(bf16)


def deal_kernel(parts, place_ref, order_ref, source_ref, values_ref, *sends):
    rows, slots, width = source_ref.shape
    share = rows // parts
    me = place_ref[0]
    for d in range(parts):
        for r in range(share):
            row = order_ref[(me ^ d) * share + r]
            sends[d][r, :slots] = source_ref[row]
            value = values_ref[pl.ds(row, 1), :]
            high = value.astype(bf16).astype(f32)
            rest = value - high
            middle = rest.astype(bf16).astype(f32)
            three = jnp.concatenate(
                [high, middle, rest - middle, jnp.zeros((EXTRA - 3, slots), f32)], axis=0
            )
            if width > slots:
                three = jnp.concatenate([three, jnp.zeros((EXTRA, width - slots), f32)], axis=1)
            sends[d][r, slots:] = three.astype(bf16)


def undeal_kernel(parts, share, place_ref, order_ref, *refs):
    pieces, (out_hbm, low_ref, full_ref, sems) = refs[:parts], refs[parts:]
    moves = Moves(sems)
    me = place_ref[0]
    places = [(d, r) for d in range(parts) for r in range(share)]
    unpack = Unpack(moves, [pieces[d].at[r] for d, r in places], out_hbm, low_ref, full_ref)
    unpack.run([order_ref[(me ^ d) * share + r] for d, r in places])
    moves.finish()


def attend(length, q_ref, k_ref, v_ref, put_context, lse_ref):
    pairs, span, _ = q_ref.shape
    c = LOG2E / DH**0.5
    lane = lax.broadcasted_iota(jnp.int32, (1, 128), 1)
    low = lane < DH

    def branch(n):
        def pair(p, carry):
            sl = pl.ds(pl.multiple_of(p * 128, 128), 128)
            q, k, v = q_ref[p], k_ref[p, :n], v_ref[p, :n]
            real = lax.broadcasted_iota(jnp.int32, (span, 128), 1) + (n - 128) < length
            found, sizes = [], []
            for h in range(2):
                mine = low if h == 0 else ~low
                s = dot(jnp.where(mine, q, jnp.zeros_like(q)), k, NT)
                tail = jnp.where(real, s[:, n - 128 :], -1e30)
                s = jnp.concatenate([s[:, : n - 128], tail], axis=1) if n > 128 else tail
                peak = jnp.max(s, axis=1, keepdims=True) * c
                e = jnp.exp2(s * c - peak)
                total = jnp.sum(e, axis=1, keepdims=True)
                found.append(dot(e.astype(bf16), jnp.where(mine, v, jnp.zeros_like(v))) / total)
                sizes.append(peak + jnp.log2(total))
            put_context(sl, (found[0] + found[1]).astype(bf16))
            kept = jnp.where(lane == 2 * p, sizes[0], lse_ref[...])
            lse_ref[...] = jnp.where(lane == 2 * p + 1, sizes[1], kept)
            return carry

        lse_ref[...] = jnp.zeros_like(lse_ref)
        lax.fori_loop(0, pairs, pair, 0)

    blocks = (length + 127) // 128
    for b in range(1, span // 128 + 1):
        pl.when(blocks == b)(functools.partial(branch, 128 * b))


def attend_back(length, q_ref, k_ref, v_ref, ctx_ref, lse_ref, do_ref, get, put):
    pairs, span, _ = q_ref.shape
    scale = 1.0 / DH**0.5
    c = LOG2E * scale
    lane = lax.broadcasted_iota(jnp.int32, (1, 128), 1)
    low = lane < DH

    def branch(n):
        def pair(p, carry):
            sl = pl.ds(pl.multiple_of(p * 128, 128), 128)
            get(p)
            q, k, v, do = q_ref[p], k_ref[p, :n], v_ref[p, :n], do_ref[:, sl]
            real = lax.broadcasted_iota(jnp.int32, (span, 128), 1) + (n - 128) < length
            product = do.astype(f32) * ctx_ref[:, sl].astype(f32)
            sizes = lse_ref[...]
            dq = dk = dv = 0.0
            for h in range(2):
                mine = low if h == 0 else ~low
                qh = jnp.where(mine, q, jnp.zeros_like(q))
                doh = jnp.where(mine, do, jnp.zeros_like(do))
                kh = jnp.where(mine, k, jnp.zeros_like(k))
                delta = jnp.sum(jnp.where(mine, product, 0.0), axis=1, keepdims=True)
                lse = jnp.sum(jnp.where(lane == 2 * p + h, sizes, 0.0), axis=1, keepdims=True)
                prob = jnp.exp2(dot(qh, k, NT) * c - lse)
                tail = jnp.where(real, prob[:, n - 128 :], 0.0)
                prob = jnp.concatenate([prob[:, : n - 128], tail], axis=1) if n > 128 else tail
                ds = (prob * (dot(doh, v, NT) - delta)).astype(bf16)
                dq = dq + dot(ds, kh)
                dk = dk + dot(ds, qh, TN)
                dv = dv + dot(prob.astype(bf16), doh, TN)
            dk, dv = (dk * scale).astype(bf16), dv.astype(bf16)
            if n < span:
                blank = jnp.zeros((span - n, 128), bf16)
                dk = jnp.concatenate([dk, blank], axis=0)
                dv = jnp.concatenate([dv, blank], axis=0)
            put(p, sl, (dq * scale).astype(bf16), dk, dv)
            return carry

        lax.fori_loop(0, pairs, pair, 0)

    blocks = (length + 127) // 128
    for b in range(1, span // 128 + 1):
        pl.when(blocks == b)(functools.partial(branch, 128 * b))


def forward_kernel(
    parts, row, place_ref, own_ref, bq_ref, bv_ref, bo_ref, wq_hbm, wk_hbm, wv_hbm, wo_hbm, *refs
):
    pieces = refs[:parts]
    xc_hbm, q_hbm, k_hbm, v_hbm, lse_hbm, hat_hbm, rstd_hbm = refs[parts : parts + 7]
    w_ref, xc_ref, q_ref, k_ref, v_ref, lse_ref, hat_ref, rstd_ref, sems = refs[parts + 7 :]
    moves = Moves(sems)
    me = place_ref[0]
    step = pieces[0].shape[0]
    arriving = []
    for d in range(parts):
        here = pl.ds(pl.multiple_of((me ^ d) * step, step), step)
        arriving.append(moves.start(pieces[d], xc_ref.at[1, here]))
    hbm = (wq_hbm, wk_hbm, wv_hbm, wo_hbm)
    weights = [moves.start(w, w_ref.at[k]) for k, w in enumerate(hbm)]
    for copy in arriving:
        copy.wait()
    moves.send(xc_ref.at[1], xc_hbm.at[1])
    x = xc_ref[1]
    weights[0].wait()

    def by_pair(ref, block):
        for p in range(ref.shape[0]):
            ref[p] = block[:, p * 128 : (p + 1) * 128].astype(bf16)

    by_pair(q_ref, dot(x, w_ref[0]) + bq_ref[...])
    moves.send(q_ref, q_hbm)
    weights[1].wait()
    by_pair(k_ref, dot(x, w_ref[1]))
    moves.send(k_ref, k_hbm)
    weights[2].wait()
    by_pair(v_ref, dot(x, w_ref[2]) + bv_ref[...])
    moves.send(v_ref, v_hbm)

    def put(sl, block):
        xc_ref[0, :, sl] = block

    attend(own_ref[row], q_ref, k_ref, v_ref, put, lse_ref)
    moves.send(xc_ref.at[0], xc_hbm.at[0])
    moves.send(lse_ref, lse_hbm)
    weights[3].wait()
    for i in range(xc_ref.shape[1] // BLOCK):
        sl = slice(i * BLOCK, (i + 1) * BLOCK)
        a = xc_ref[1, sl].astype(f32) + dot(xc_ref[0, sl], w_ref[3]) + bo_ref[...]
        center = a - jnp.mean(a, axis=1, keepdims=True)
        rstd = lax.rsqrt(jnp.mean(center * center, axis=1, keepdims=True) + EPS)
        hat_ref[sl] = center * rstd
        rstd_ref[sl] = jnp.broadcast_to(rstd, (BLOCK, rstd_ref.shape[1]))
        moves.send(hat_ref.at[sl], hat_hbm.at[sl])
    moves.send(rstd_ref, rstd_hbm)
    moves.finish()


def norm_back(g, hat, rstd, gain):
    scaled = g * gain
    first = jnp.mean(scaled, axis=1, keepdims=True)
    second = jnp.mean(scaled * hat, axis=1, keepdims=True)
    return rstd * (scaled - first - hat * second)


def feed_kernel(
    parts,
    share,
    steps,
    place_ref,
    gain_one_ref,
    shift_one_ref,
    wi_ref,
    bi_ref,
    wo_ref,
    bo_ref,
    gain_ref,
    shift_ref,
    *refs,
):
    hats, refs = refs[:share], refs[share:]
    cots, refs = refs[:parts], refs[parts:]
    slope_ref, low_hbm, branch_hbm, summed_hbm, *refs = refs
    outs, refs = refs[:parts], refs[parts:]
    sums_ref, keep_ref, send_ref, total_ref, low_ref, branch_ref, act_ref, cot_ref, out_ref, sems = refs
    step = pl.program_id(0)
    count, width = total_ref.shape
    chunk = wi_ref.shape[1]
    me = place_ref[0]
    slots = outs[0].shape[1]
    span = count // share
    blocks = count // BLOCK

    def place(d, r):
        return pl.ds(pl.multiple_of((r * parts + (me ^ d)) * slots, slots), slots)

    rows = [slice(r * span, (r + 1) * span) for r in range(share)]
    pairs = [(d, r) for d in range(parts) for r in range(share)]
    coming = [(hats[r], total_ref.at[rows[r]]) for r in range(share)]
    coming += [(cots[d].at[r, :slots], cot_ref.at[place(d, r)]) for d, r in pairs]
    going = [(low_ref, low_hbm), (branch_ref, branch_hbm), (total_ref, summed_hbm)]
    going += [(out_ref.at[place(d, r)], outs[d].at[r]) for d, r in pairs]
    copies = [
        pltpu.make_async_copy(source, target, sems.at[k])
        for k, (source, target) in enumerate(coming + going)
    ]
    coming, going = copies[: len(coming)], copies[len(coming) :]

    @pl.when(step == 0)
    def _():
        for copy in coming:
            copy.start()
        for r in range(share):
            coming[r].wait()
            normed = total_ref[rows[r]] * gain_one_ref[...] + shift_one_ref[...]
            low_ref[rows[r]] = normed.astype(bf16)
            total_ref[rows[r]] = normed + bo_ref[...]
        going[0].start()

    def run(last):
        def first(i):
            return dot(low_ref[i * BLOCK : (i + 1) * BLOCK], wi_ref[...]) + bi_ref[...]

        if last:
            for copy in coming[share:]:
                copy.wait()
        ahead = first(0)
        sums = [0.0, 0.0, 0.0]
        for i in range(blocks):
            inner = ahead
            if i + 1 < blocks:
                ahead = first(i + 1)
            sl = slice(i * BLOCK, (i + 1) * BLOCK)
            phi = 0.5 + 0.5 * lax.erf(inner * RSQRT2)
            act = (inner * phi).astype(bf16)
            slope_ref[0, sl] = (phi + inner * (jnp.exp(-0.5 * inner * inner) * RSQRT2PI)).astype(bf16)
            act_ref[sl, pl.ds(pl.multiple_of(step * chunk, chunk), chunk)] = act
            a = total_ref[sl] + dot(act, wo_ref[...])
            if not last:
                total_ref[sl] = a
                continue
            center = a - jnp.mean(a, axis=1, keepdims=True)
            rstd = lax.rsqrt(jnp.mean(center * center, axis=1, keepdims=True) + EPS)
            hat = center * rstd
            out_ref[sl] = (hat * gain_ref[...] + shift_ref[...]).astype(bf16)
            g = cot_ref[sl].astype(f32)
            back = norm_back(g, hat, rstd, gain_ref[...])
            total_ref[sl] = back
            low = back.astype(bf16)
            branch_ref[sl] = low
            for k, term in enumerate((g * hat, g, low.astype(f32))):
                sums[k] = sums[k] + row_sum(term)
        if last:
            for copy in going[1:]:
                copy.start()
            sums_ref[...] = jnp.concatenate(sums + [jnp.zeros((5, width), f32)], axis=0)

    pl.when(step < steps - 1)(functools.partial(run, False))
    pl.when(step == steps - 1)(functools.partial(run, True))

    @pl.when(step >= steps)
    def _():
        here = pl.ds(pl.multiple_of((step - steps) * chunk, chunk), chunk)
        grad = dot(act_ref[:, here], branch_ref[...], TN).astype(bf16)
        core = place_ref[1]
        pairs, height = keep_ref.shape[1], keep_ref.shape[2]
        for z in range(pairs):
            for unit in range(parts):
                base = (2 * z * parts + unit) * height
                even = grad[base : base + height]
                odd = grad[base + parts * height : base + (parts + 1) * height]
                keep_ref[unit ^ me, z] = jnp.where(core == 0, even, odd)
                send_ref[unit ^ me, z] = jnp.where(core == 0, odd, even)

    @pl.when(step == 2 * steps - 1)
    def _():
        for copy in going:
            copy.wait()


def feed_back_kernel(share, place_ref, gain_ref, *refs):
    (branch_hbm, summed_hbm, low_hbm, slope_hbm, wi_hbm, wo_hbm), refs = refs[:6], refs[6:]
    hats_hbm, rstds_hbm, refs = refs[:share], refs[share : 2 * share], refs[2 * share :]
    keep_hbm, send_hbm, bias_ref, attended_hbm, attn_hbm, sums_ref, *refs = refs
    branch_ref, low_ref, slope_ref, wi_ref, wo_ref, inner_ref, total_ref, *refs = refs
    attn_ref, hat_ref, rstd_ref, keep_ref, send_ref, sems = refs
    moves = Moves(sems)
    me = place_ref[0]
    count, width = total_ref.shape
    span = count // share
    blocks = count // BLOCK
    units = slope_ref.shape[0]
    coming = [[] for _ in range(units)]

    def take(u, source, target):
        coming[u].append(moves.start(source, target))

    for u in range(units):
        chunk = slice(u * width, (u + 1) * width)
        take(u, wo_hbm.at[chunk], wo_ref.at[u])
        if u == 0:
            take(u, branch_hbm, branch_ref)
        take(u, slope_hbm.at[u], slope_ref.at[u])
        take(u, wi_hbm.at[:, chunk], wi_ref.at[u])
        if u == 0:
            take(u, summed_hbm, total_ref)
            take(u, low_hbm, low_ref)
    for r in range(share):
        rows = slice(r * span, (r + 1) * span)
        take(units - 1, hats_hbm[r], hat_ref.at[rows])
        take(units - 1, rstds_hbm[r], rstd_ref.at[rows])
    for u in range(units):
        last = u == units - 1
        for copy in coming[u]:
            copy.wait()

        def first(i):
            return dot(branch_ref[i * BLOCK : (i + 1) * BLOCK], wo_ref[u], NT)

        ahead = first(0)
        bias = 0.0
        sums = [0.0, 0.0, 0.0]
        for i in range(blocks):
            now = ahead
            if i + 1 < blocks:
                ahead = first(i + 1)
            sl = slice(i * BLOCK, (i + 1) * BLOCK)
            inner = (now * slope_ref[u, sl].astype(f32)).astype(bf16)
            inner_ref[sl] = inner
            bias = bias + row_sum(inner.astype(f32))
            g = total_ref[sl] + dot(inner, wi_ref[u], NT)
            if not last:
                total_ref[sl] = g
                continue
            hat = hat_ref[sl]
            back = norm_back(g, hat, rstd_ref[sl, :1], gain_ref[...])
            total_ref[sl] = back
            low = back.astype(bf16)
            attn_ref[sl] = low
            for k, term in enumerate((g * hat, g, low.astype(f32))):
                sums[k] = sums[k] + row_sum(term)
        bias_ref[u : u + 1] = bias
        if last:
            moves.send(total_ref, attended_hbm)
            moves.send(attn_ref, attn_hbm)
            sums_ref[...] = jnp.concatenate(sums + [jnp.zeros((5, width), f32)], axis=0)
        grad = dot(low_ref[...], inner_ref[...], TN).astype(bf16)
        put_unit(place_ref[1], grad, keep_ref, send_ref, u)
        moves.send(send_ref.at[u], send_hbm.at[u ^ me])
        moves.send(keep_ref.at[u], keep_hbm.at[u ^ me])
    moves.finish()


def put_unit(core, grad, keep_ref, send_ref, unit):
    pairs = keep_ref.shape[1]
    rows = grad.shape[0] // (2 * pairs)
    for z in range(pairs):
        even = grad[2 * z * rows : (2 * z + 1) * rows]
        odd = grad[(2 * z + 1) * rows : (2 * z + 2) * rows]
        keep_ref[unit, z] = jnp.where(core == 0, even, odd)
        send_ref[unit, z] = jnp.where(core == 0, odd, even)


def square_kernel(share, place_ref, two_ref, one_ref, bias_ref, *refs):
    zeros, refs = refs[:share], refs[share:]
    xc_hbm, grads_hbm, refs = refs[:share], refs[share : 2 * share], refs[2 * share :]
    outs_hbm, (xc_ref, grads_ref, *outs, sems) = refs[:4], refs[4:]
    moves = Moves(sems)
    core = place_ref[1]
    units, span = grads_ref.shape[0], grads_ref.shape[1] // share
    coming = [[] for _ in range(units)]
    for u in range(units):
        for r in range(share):
            rows = slice(r * span, (r + 1) * span)
            if u < 2:
                coming[u].append(moves.start(xc_hbm[r].at[u], xc_ref.at[u, rows]))
            coming[u].append(moves.start(grads_hbm[r].at[u], grads_ref.at[u, rows]))
    zero = zeros[0][0:3]
    for ref in zeros[1:]:
        zero = zero + ref[0:3]
    vectors = jnp.concatenate([two_ref[0:3], one_ref[0:3], zero, bias_ref[...]], axis=0)
    blank = jnp.zeros((EXTRA - vectors.shape[0], vectors.shape[1]), f32)
    vectors = jnp.concatenate([vectors, blank], axis=0)
    for u in range(units):
        for copy in coming[u]:
            copy.wait()
        grad = dot(xc_ref[min(u, 1)], grads_ref[u], TN).astype(bf16)
        group, at = u // 2, u % 2
        keep_ref, send_ref = outs[2 * group : 2 * group + 2]
        pairs, rows, width = keep_ref.shape[1:]
        tail = EXTRA if group == 0 else 0
        rows = rows - tail

        def block(b):
            found = grad[b * rows : (b + 1) * rows]
            if not tail:
                return found
            extra = vectors if u == 0 else jnp.zeros_like(vectors)
            return jnp.concatenate([found.astype(f32), extra], axis=0).astype(bf16)

        for z in range(pairs):
            even, odd = block(2 * z), block(2 * z + 1)
            keep_ref[at, z] = jnp.where(core == 0, even, odd)
            send_ref[at, z] = jnp.where(core == 0, odd, even)
        for k, ref in ((1, send_ref), (0, keep_ref)):
            moves.send(ref.at[at], outs_hbm[2 * group + k].at[at])
    moves.finish()


def backward_kernel(parts, row, place_ref, own_ref, *refs):
    hbm, refs = refs[:11], refs[11:]
    wo_hbm, low_hbm, q_hbm, k_hbm, v_hbm, xc_hbm, lse_hbm, attended_hbm, wq_hbm, wk_hbm, wv_hbm = hbm
    values, refs = refs[:parts], refs[parts:]
    before, refs = (refs[:parts], refs[parts:]) if row else ((), refs)
    grads_hbm, outs, sums_ref, refs = refs[0], refs[1 : 1 + parts], refs[1 + parts], refs[2 + parts :]
    *refs, sems, in_sems = refs
    if row:
        *refs, before_ref = refs
    w_ref, low_ref, qkv_ref, context_ref, lse_ref, attended_ref, grads_ref, do_ref, total_ref, value_ref = refs
    moves = Moves(sems)
    me = place_ref[0]
    slots = outs[0].shape[1]
    span, width = low_ref.shape
    rows = slice(row * span, (row + 1) * span)

    def inward(p, k):
        return pltpu.make_async_copy(
            (q_hbm, k_hbm, v_hbm)[k].at[p], qkv_ref.at[k, p], in_sems.at[p, k]
        )

    early = [moves.start(wo_hbm, w_ref.at[0]), moves.start(low_hbm.at[rows], low_ref)]
    early += [moves.start(lse_hbm, lse_ref), moves.start(xc_hbm.at[0], context_ref)]
    for p in range(width // 128):
        for k in range(3):
            inward(p, k).start()
    late = [moves.start(ref, w_ref.at[1 + k]) for k, ref in enumerate((wq_hbm, wk_hbm, wv_hbm))]
    late.append(moves.start(attended_hbm.at[rows], attended_ref))
    for d, pieces in enumerate(before):
        late.append(moves.start(pieces, before_ref.at[d]))
    for d in range(parts):
        here = pl.ds(pl.multiple_of((me ^ d) * slots, slots), slots)
        late.append(moves.start(values[d].at[row, slots:, :slots], value_ref.at[:, here]))
    for copy in early:
        copy.wait()
    moves.send(low_ref, grads_hbm.at[0])
    do_ref[...] = dot(low_ref[...], w_ref[0], NT).astype(bf16)

    def get(p):
        for k in range(3):
            inward(p, k).wait()

    def put(p, sl, *blocks):
        for k, block in enumerate(blocks):
            grads_ref[k, :, sl] = block

    q_ref, k_ref, v_ref = [qkv_ref.at[k] for k in range(3)]
    attend_back(own_ref[row], q_ref, k_ref, v_ref, context_ref, lse_ref, do_ref, get, put)
    moves.send(grads_ref, grads_hbm.at[pl.ds(1, 3)])
    for copy in late:
        copy.wait()
    for d in range(len(before)):
        moves.send(before_ref.at[d], outs[d].at[pl.ds(0, row)])
    dq, dk, dv = grads_ref[0], grads_ref[1], grads_ref[2]
    low = (
        attended_ref[...]
        + dot(dq, w_ref[1], NT)
        + dot(dk, w_ref[2], NT)
        + dot(dv, w_ref[3], NT)
    ).astype(bf16)
    total_ref[...] = low
    for d in range(parts):
        here = pl.ds(pl.multiple_of((me ^ d) * slots, slots), slots)
        moves.send(total_ref.at[here], outs[d].at[row])
    merge = row_sum(dot(value_ref[...], low))
    sums_ref[...] = jnp.concatenate(
        [
            row_sum(dq.astype(f32)),
            row_sum(dv.astype(f32)),
            merge,
            jnp.zeros((5, merge.shape[1]), f32),
        ],
        axis=0,
    )
    moves.finish()


def plane_first_kernel(place_ref, keep_ref, got_ref, *outs):
    keep_x, send_x, keep_y, send_y = outs
    half = keep_x.shape[2]
    units, blocks = keep_ref.shape[:2]
    for d in range(units):
        for i in range(blocks):
            total = (keep_ref[d, i].astype(f32) + got_ref[d, i].astype(f32)).astype(bf16)
            (send_x if d % 2 else keep_x)[d // 2, i] = total[:half]
            (send_y if d // 2 else keep_y)[d % 2, i] = total[half:]


def plane_second_kernel(groups, place_ref, *refs):
    terms, outs = refs[: 4 * groups], refs[4 * groups :]
    for g in range(groups):
        keep_x, got_x, keep_y, got_y = terms[4 * g : 4 * g + 4]
        for i in range(keep_x.shape[1]):
            for j in range(2):
                outs[j][g, i] = (keep_x[j, i].astype(f32) + got_x[j, i].astype(f32)).astype(bf16)
                outs[2 + j][g, i] = (keep_y[j, i].astype(f32) + got_y[j, i].astype(f32)).astype(bf16)


def plane_third_kernel(spot, place_ref, keep_x, got_x, keep_y, got_y, *outs):
    groups, blocks = keep_x.shape[:2]
    bit = place_ref[spot]
    for g in range(groups):
        for i in range(blocks // 2):
            for out, j in ((outs[0], 2 * i + bit), (outs[1], 2 * i + 1 - bit)):
                top = keep_x[g, j].astype(f32) + got_x[g, j].astype(f32)
                bottom = keep_y[g, j].astype(f32) + got_y[g, j].astype(f32)
                out[g, i] = jnp.concatenate([top, bottom], axis=0).astype(bf16)


def quarter_kernel(parts, place_ref, keep_ref, got_ref, *outs):
    me = place_ref[0]
    units, blocks, rows = keep_ref.shape[:3]
    half = rows // 2
    for u in range(units):
        for i in range(blocks):
            total = (keep_ref[u, i].astype(f32) + got_ref[u, i].astype(f32)).astype(bf16)
            for d in range(parts):
                for h in range(2):

                    @pl.when((me ^ d) == 2 * u + h)
                    def _(d=d, h=h, i=i, total=total):
                        outs[d][0, i] = total[h * half : (h + 1) * half]


def halves_kernel(place_ref, keep_ref, got_ref, top_ref, bottom_ref):
    half = top_ref.shape[2]
    for u in range(keep_ref.shape[0]):
        total = keep_ref[u, 0].astype(f32) + got_ref[u, 0].astype(f32)
        top_ref[u, 0] = total[:half].astype(bf16)
        bottom_ref[u, 0] = total[half:].astype(bf16)


def both_kernel(place_ref, top_ref, got_top, bottom_ref, got_bottom, *outs):
    for u in range(top_ref.shape[0]):
        top = top_ref[u, 0].astype(f32) + got_top[u, 0].astype(f32)
        bottom = bottom_ref[u, 0].astype(f32) + got_bottom[u, 0].astype(f32)
        if len(outs) == 2:
            outs[0][u, 0] = top.astype(bf16)
            outs[1][u, 0] = bottom.astype(bf16)
            continue
        total = jnp.concatenate([top, bottom], axis=0)
        rows = outs[u].shape[0]
        outs[u][...] = total[:rows]
        if u == 0:
            outs[2][...] = total[rows:]


def fourth_kernel(parts, bit_spot, place_ref, *refs):
    pieces, outs = refs[:parts], refs[parts:]
    blocks = pieces[0].shape[1]
    bit = place_ref[bit_spot]

    def total(i):
        found = pieces[0][0, i].astype(f32)
        for piece in pieces[1:]:
            found = found + piece[0, i].astype(f32)
        return found.astype(bf16)

    for i in range(blocks // 2):
        outs[0][0, i] = total(2 * i + bit)
        outs[1][0, i] = total(2 * i + 1 - bit)


def merge_kernel(spot, place_ref, keep_ref, got_ref, *outs):
    groups, blocks = keep_ref.shape[:2]

    def total(g, i):
        return (keep_ref[g, i].astype(f32) + got_ref[g, i].astype(f32)).astype(bf16)

    for g in range(groups):
        if spot is None:
            for i in range(blocks):
                outs[0][g, i] = total(g, i)
            continue
        bit = place_ref[spot]
        for i in range(blocks // 2):
            outs[0][g, i] = total(g, 2 * i + bit)
            outs[1][g, i] = total(g, 2 * i + 1 - bit)


def finish_kernel(parts, place_ref, *refs):
    pieces, outs = refs[:parts], refs[parts:]
    me = place_ref[0]
    rows, width = pieces[0].shape[2:]
    for q in range(parts):
        for d in range(parts):

            @pl.when((me ^ d) == q)
            def _(q=q, d=d):
                if pieces[d].shape[0] == 2:
                    outs[0][q * rows : (q + 1) * rows] = pieces[d][0, 0].astype(f32)
                    outs[1][:, q * width : (q + 1) * width] = pieces[d][1, 0].astype(f32)
                else:
                    outs[q // 2][q % 2 * rows : (q % 2 + 1) * rows] = pieces[d][0, 0].astype(f32)


def swap(array, axis, size, distance):
    return lax.ppermute(array, axis, [(i, i ^ distance) for i in range(size)])


def body(
    parts,
    size,
    tokens,
    values,
    lengths,
    merge,
    w_query,
    w_key,
    w_value,
    w_output,
    b_query,
    b_value,
    b_output,
    gain_one,
    shift_one,
    w_inner,
    b_inner,
    w_outer,
    b_outer,
    gain_two,
    shift_two,
    cotangent,
):
    rows, slots, width = tokens.shape
    hidden = w_inner.shape[1]
    share = rows // parts
    span = slots * parts
    count = share * span
    pairs = size // 2
    blk = width // size
    me = lax.axis_index("seq")
    place = lax.axis_index("batch")
    bits = size.bit_length() - 1
    spot = jnp.stack([me] + [(place >> k) & 1 for k in range(bits)]).astype(jnp.int32)
    line = lambda vector: vector.reshape(1, -1)
    low = lambda *shape: Shape(shape, bf16)
    full = lambda *shape: Shape(shape, f32)
    others = range(1, parts)
    call = Sequence()

    def exchange(pieces):
        return [pieces[0]] + [swap(pieces[d], "seq", parts, d) for d in others]

    packed = call(
        functools.partial(pack_kernel, parts),
        [(VM, low(slots, width))] * rows
        + [(SM, Shape((rows,), jnp.int32)), (SM, Shape((share,), jnp.int32))],
        [(SM, spot), (SM, lengths), (VM, tokens), (VM, values), (VM, line(merge))],
        limit=60,
        name="pack",
    )
    order, own = packed[rows:]
    x_parts = [exchange(packed[r * parts : (r + 1) * parts]) for r in range(share)]
    cot_parts = exchange(
        call(
            functools.partial(deal_kernel, parts),
            [(VM, low(share, slots + EXTRA, width))] * parts,
            [(SM, spot), (SM, order), (VM, cotangent), (VM, values)],
            limit=60,
            name="deal",
        )
    )

    forward = []
    DMA = pltpu.SemaphoreType.DMA
    for r in range(share):
        results = (
            [low(2, span, width)]
            + [low(width // 128, span, 128)] * 3
            + [full(span, 128), full(span, width), full(span, 128)]
        )
        forward.append(
            call(
                functools.partial(forward_kernel, parts, r),
                [(HBM, shape) for shape in results],
                [(SM, spot), (SM, own)]
                + [(VM, line(b)) for b in (b_query, b_value, b_output)]
                + [(HBM, w) for w in (w_query, w_key, w_value, w_output)]
                + [(HBM, x) for x in x_parts[r]],
                scratch=[pltpu.VMEM((4, width, width), bf16)]
                + [pltpu.VMEM(shape.shape, shape.dtype) for shape in results]
                + [DMA((4 + parts + 2 * parts + 6,))],
                limit=60,
                heavy=True,
                name="attention_forward",
            )
        )
    hats = [f[5] for f in forward]
    rstds = [f[6] for f in forward]

    chunk = width
    steps = hidden // chunk
    clip = lambda i: jnp.minimum(i, steps - 1)
    tall_low, tall_full = low(count, width), full(count, width)
    piece_low = low(share, slots, width)
    unit_low = low(parts, pairs, blk, width)
    outer_spec = pl.BlockSpec(
        (parts, pairs // steps, blk, width), lambda i: (0, jnp.maximum(i - steps, 0), 0, 0)
    )
    fed = call(
        functools.partial(feed_kernel, parts, share, steps),
        [(pl.BlockSpec((1, count, chunk), lambda i: (clip(i), 0, 0)), low(steps, count, chunk))]
        + [(HBM, tall_low), (HBM, tall_low), (HBM, tall_full)]
        + [(HBM, piece_low)] * parts
        + [(VM, full(8, width))]
        + [(outer_spec, unit_low)] * 2,
        [
            (SM, spot),
            (VM, line(gain_one)),
            (VM, line(shift_one)),
            (pl.BlockSpec((width, chunk), lambda i: (0, clip(i))), w_inner),
            (pl.BlockSpec((1, chunk), lambda i: (0, clip(i))), line(b_inner)),
            (pl.BlockSpec((chunk, width), lambda i: (clip(i), 0)), w_outer),
            (VM, line(b_outer)),
            (VM, line(gain_two)),
            (VM, line(shift_two)),
        ]
        + [(HBM, hat) for hat in hats]
        + [(HBM, c) for c in cot_parts],
        scratch=[pltpu.VMEM((count, width), f32)]
        + [pltpu.VMEM((count, width), bf16)] * 2
        + [pltpu.VMEM((count, hidden), bf16)]
        + [pltpu.VMEM((count, width), bf16)] * 2
        + [DMA((share + 3 + 2 * share * parts,))],
        grid=(2 * steps,),
        limit=60,
        heavy=True,
        name="feed_forward",
    )
    slope, normed_low, d_branch, d_summed = fed[:4]
    out_parts = exchange(fed[4 : 4 + parts])
    sums_two, outer_keep, outer_send = fed[4 + parts :]
    outer_got = swap(outer_send, "batch", size, 1)

    inner_keep, inner_send, inner_bias, d_attended, d_attn, sums_one = call(
        functools.partial(feed_back_kernel, share),
        [(HBM, unit_low)] * 2
        + [(VM, full(steps, width)), (HBM, tall_full), (HBM, tall_low), (VM, full(8, width))],
        [(SM, spot), (VM, line(gain_one))]
        + [(HBM, a) for a in (d_branch, d_summed, normed_low, slope, w_inner, w_outer)]
        + [(HBM, hat) for hat in hats]
        + [(HBM, rstd) for rstd in rstds],
        scratch=[pltpu.VMEM((count, width), bf16)] * 2
        + [pltpu.VMEM((steps, count, width), bf16)]
        + [pltpu.VMEM((steps, width, width), bf16)] * 2
        + [pltpu.VMEM((count, width), bf16), pltpu.VMEM((count, width), f32)]
        + [pltpu.VMEM((count, width), bf16), pltpu.VMEM((count, width), f32)]
        + [pltpu.VMEM((count, 128), f32)]
        + [pltpu.VMEM(unit_low.shape, bf16)] * 2
        + [DMA((3 * steps + 3 + 2 * share + 2 + 2 * steps,))],
        limit=60,
        heavy=True,
        name="feed_backward",
    )
    inner_got = swap(inner_send, "batch", size, 1)

    def simple(kernel, ins, outs, name, heavy=False):
        return call(
            kernel,
            [(VM, shape) for shape in outs],
            [(SM, spot)] + [(VM, array) for array in ins],
            heavy=heavy,
            name=name,
        )

    def plane_first(keep, got, name):
        rows = keep.shape[2]
        first, rest = low(2, pairs, blk // 2, width), low(2, pairs, rows - blk // 2, width)
        keep_x, send_x, keep_y, send_y = simple(
            plane_first_kernel, [keep, got], [first, first, rest, rest], name
        )
        return keep_x, swap(send_x, "seq", parts, 1), keep_y, swap(send_y, "seq", parts, 2)

    def plane_second(groups, name):
        count = len(groups)
        first, rest = [low(count, *groups[0][k].shape[1:]) for k in (0, 2)]
        keep_x, send_x, keep_y, send_y = simple(
            functools.partial(plane_second_kernel, count),
            [term for terms in groups for term in terms],
            [first, first, rest, rest],
            name,
        )
        return keep_x, swap(send_x, "seq", parts, 2), keep_y, swap(send_y, "seq", parts, 1)

    def plane_third(terms, name):
        shape = low(terms[0].shape[0], pairs // 2, terms[0].shape[2] + terms[2].shape[2], width)
        keep, send = simple(
            functools.partial(plane_third_kernel, 2), list(terms), [shape, shape], name
        )
        return keep, swap(send, "batch", size, 2)

    def merge_terms(spot_index, terms, name):
        groups, blocks, rows, _ = terms[0].shape
        if spot_index is None:
            shapes = [low(groups, blocks, rows, width)]
        else:
            shapes = [low(groups, blocks // 2, rows, width)] * 2
        kernel = functools.partial(merge_kernel, spot_index)
        return simple(kernel, terms, shapes, name)

    def along_line(terms, name):
        for bit in range(2, bits):
            keep, send = merge_terms(1 + bit, terms, name)
            terms = keep, swap(send, "batch", size, 1 << bit)
        return terms

    def gather(terms, name):
        (block,) = merge_terms(None, terms, name)
        return exchange([block] * parts)

    def undeal(pieces):
        return call(
            functools.partial(undeal_kernel, parts, share),
            [(HBM, full(rows, slots, width))],
            [(SM, spot), (SM, order)] + [(HBM, piece) for piece in pieces],
            scratch=[pltpu.VMEM((rows, slots, width), dtype) for dtype in (bf16, f32)]
            + [DMA((2 * rows,))],
            limit=16,
            heavy=True,
            name="undeal",
        )[0]

    layer_out = undeal(out_parts)
    outer_terms = plane_first(outer_keep, outer_got, "outer_core")
    inner_terms = plane_first(inner_keep, inner_got, "inner_core")

    grads, token_parts, sums_zero = [], [], []
    pair_count = width // 128
    for r in range(share):
        xc, query, key, value, lse = forward[r][:5]
        back = call(
            functools.partial(backward_kernel, parts, r),
            [(HBM, low(4, span, width))]
            + [(HBM, low(r + 1, slots, width))] * parts
            + [(VM, full(8, width))],
            [(SM, spot), (SM, own)]
            + [(HBM, array) for array in (w_output, d_attn, query, key, value, xc, lse, d_attended)]
            + [(HBM, w) for w in (w_query, w_key, w_value)]
            + [(HBM, c) for c in cot_parts]
            + [(HBM, piece) for piece in token_parts],
            scratch=[
                pltpu.VMEM((4, width, width), bf16),
                pltpu.VMEM((span, width), bf16),
                pltpu.VMEM((3, pair_count, span, 128), bf16),
                pltpu.VMEM((span, width), bf16),
                pltpu.VMEM((span, 128), f32),
                pltpu.VMEM((span, width), f32),
                pltpu.VMEM((3, span, width), bf16),
                pltpu.VMEM((span, width), bf16),
                pltpu.VMEM((span, width), bf16),
                pltpu.VMEM((EXTRA, span), bf16),
            ]
            + ([pltpu.VMEM((parts, r, slots, width), bf16)] if r else [])
            + [DMA((10 + 4 * parts,)), DMA((pair_count, 3))],
            limit=60,
            heavy=True,
            name="attention_backward",
        )
        grads.append(back[0])
        token_parts = back[1 : 1 + parts]
        sums_zero.append(back[1 + parts])
        if r == 0:
            feed_terms = plane_second([outer_terms, inner_terms], "feed_plane")
    feed_terms = plane_third(feed_terms, "feed_plane")
    token_parts = exchange(token_parts)

    early_low, late_low = low(2, pairs, blk + EXTRA, width), low(2, pairs, blk, width)
    early_keep, early_send, late_keep, late_send = call(
        functools.partial(square_kernel, share),
        [(HBM, early_low)] * 2 + [(HBM, late_low)] * 2,
        [(SM, spot)]
        + [(VM, sums) for sums in (sums_two, sums_one, inner_bias, *sums_zero)]
        + [(HBM, f[0]) for f in forward]
        + [(HBM, g) for g in grads],
        scratch=[pltpu.VMEM((2, count, width), bf16), pltpu.VMEM((4, count, width), bf16)]
        + [pltpu.VMEM(early_low.shape, bf16)] * 2
        + [pltpu.VMEM(late_low.shape, bf16)] * 2
        + [DMA((6 * share + 8,))],
        limit=60,
        heavy=True,
        name="square_grad",
    )
    early_got = swap(early_send, "batch", size, 1)
    late_got = swap(late_send, "batch", size, 1)
    feed_terms = along_line(feed_terms, "feed_line")
    grad_tokens = undeal(token_parts)
    early_terms = merge_terms(2, [early_keep, early_got], "early_core")
    early_terms = early_terms[0], swap(early_terms[1], "batch", size, 2)
    quarters = exchange(
        simple(
            functools.partial(quarter_kernel, parts),
            [late_keep, late_got],
            [low(1, pairs, blk // 2, width)] * parts,
            "late_core",
        )
    )
    early_terms = along_line(early_terms, "early_line")
    feed_all = gather(feed_terms, "feed_line")
    late_keep, late_send = simple(
        functools.partial(fourth_kernel, parts, 2),
        quarters,
        [low(1, pairs // 2, blk // 2, width)] * 2,
        "late_plane",
    )
    late_terms = late_keep, swap(late_send, "batch", size, 2)
    late_terms = along_line(late_terms, "late_line")
    grad_w_outer, grad_w_inner = simple(
        functools.partial(finish_kernel, parts),
        feed_all,
        [full(parts * blk, width), full(blk, parts * width)],
        "feed_finish",
    )
    halves = [low(2, 1, blk // 2, width), low(2, 1, blk + EXTRA - blk // 2, width)]
    top, bottom = simple(halves_kernel, list(early_terms), halves, "early_line")
    got_top, got_bottom = swap(top, "seq", parts, 1), swap(bottom, "seq", parts, 2)
    late_all = gather(late_terms, "late_line")
    top, bottom = simple(both_kernel, [top, got_top, bottom, got_bottom], halves, "early_plane")
    got_top, got_bottom = swap(top, "seq", parts, 2), swap(bottom, "seq", parts, 1)
    grad_w_key, grad_w_value = simple(
        functools.partial(finish_kernel, parts), late_all, [full(blk, width)] * 2, "late_finish"
    )
    grad_w_output, grad_w_query, vectors = simple(
        both_kernel,
        [top, got_top, bottom, got_bottom],
        [full(blk, width)] * 2 + [full(EXTRA, width)],
        "early_finish",
    )
    nine = lax.dynamic_slice(vectors, (0, place * blk), (9, blk))
    grad_b_inner = lax.dynamic_slice(
        vectors[9 : 9 + steps].reshape(-1), (place * (hidden // size),), (hidden // size,)
    )
    grad_gain_two, grad_shift_two, grad_b_outer = nine[0], nine[1], nine[2]
    grad_gain_one, grad_shift_one, grad_b_output = nine[3], nine[4], nine[5]
    grad_b_query, grad_b_value, grad_merge = nine[6], nine[7], nine[8]
    return (
        layer_out,
        grad_tokens,
        grad_merge,
        grad_w_query,
        grad_w_key,
        grad_w_value,
        grad_w_output,
        grad_b_query,
        grad_b_value,
        grad_b_output,
        grad_gain_one,
        grad_shift_one,
        grad_w_inner,
        grad_b_inner,
        grad_w_outer,
        grad_b_outer,
        grad_gain_two,
        grad_shift_two,
    )


def solution(mesh):
    parts, size = mesh.shape["seq"], mesh.shape["batch"]
    rowwise = P("batch", "seq", None)
    in_specs = (rowwise, P("batch", "seq"), P("batch")) + (P(),) * 16 + (rowwise,)
    matrix, vector = P("batch", None), P("batch")
    out_specs = (
        (rowwise, rowwise, vector)
        + (matrix,) * 4
        + (vector,) * 5
        + (matrix, vector, matrix)
        + (vector,) * 3
    )
    return jax.shard_map(
        functools.partial(body, parts, size),
        mesh=mesh,
        in_specs=in_specs,
        out_specs=out_specs,
        check_vma=False,
    )
```

```python
import functools

import jax
import jax.numpy as jnp
from jax import lax
from jax.experimental import pallas as pl
from jax.experimental.pallas import tpu as pltpu
from jax.sharding import PartitionSpec as P

DH = 64
LOG2E = 1.4426950408889634
RSQRT2 = 0.7071067811865476
RSQRT2PI = 0.3989422804014327
EPS = 1e-05
EXTRA = 16
bf16 = jnp.bfloat16
f32 = jnp.float32
NN = (((1,), (0,)), ((), ()))
NT = (((1,), (1,)), ((), ()))
TN = (((0,), (0,)), ((), ()))
Shape = jax.ShapeDtypeStruct
VM = pl.BlockSpec(memory_space=pltpu.VMEM)
SM = pl.BlockSpec(memory_space=pltpu.SMEM)
ANY = pl.BlockSpec(memory_space=pl.ANY)
HBM = pl.BlockSpec(memory_space=pltpu.HBM)
BLOCK = 256


def dot(left, right, dims=NN):
    return lax.dot_general(left, right, dims, preferred_element_type=f32)


def params(limit, *semantics):
    return pltpu.CompilerParams(
        vmem_limit_bytes=limit * 1024 * 1024, dimension_semantics=semantics or None
    )


class Sequence:
    def __init__(self):
        self.last = ()

    def __call__(
        self, kernel, outs, ins, scratch=(), grid=None, prefetch=0, limit=6, alias=None, heavy=False, name=None
    ):
        count, extra = len(ins), len(self.last)

        outs = [*outs, (ANY, Shape((8, 128), f32))]
        results = len(outs) - 1

        def run(*refs):
            refs = refs[:count] + refs[count + extra :]
            kernel(*refs[: count + results], *refs[count + results + 1 :])

        *got, token = pl.pallas_call(
            run,
            grid_spec=pltpu.PrefetchScalarGridSpec(
                num_scalar_prefetch=prefetch,
                grid=grid or (),
                in_specs=[spec for spec, _ in ins[prefetch:]]
                + [ANY] * extra,
                out_specs=[spec for spec, _ in outs],
                scratch_shapes=list(scratch),
            ),
            out_shape=[shape for _, shape in outs],
            input_output_aliases=alias or {},
            compiler_params=params(limit, *(["arbitrary"] * len(grid or ()))),
            cost_estimate=pl.CostEstimate(
                flops=10**12 if heavy else 10**3,
                transcendentals=0,
                bytes_accessed=10**9 if heavy else 10**3,
            ),
            name=name,
        )(*[array for _, array in ins], *self.last)
        self.last = (token,)
        return got


class Moves:
    def __init__(self, semaphores):
        self.semaphores = semaphores
        self.used = 0
        self.out = []

    def start(self, source, target):
        copy = pltpu.make_async_copy(source, target, self.semaphores.at[self.used])
        self.used += 1
        copy.start()
        return copy

    def send(self, source, target):
        self.out.append(self.start(source, target))

    def finish(self):
        for copy in self.out:
            copy.wait()


class Unpack:
    def __init__(self, moves, pieces, target, low_ref, full_ref):
        self.moves, self.target, self.low_ref, self.full_ref = moves, target, low_ref, full_ref
        self.coming = [moves.start(piece, low_ref.at[k]) for k, piece in enumerate(pieces)]

    def run(self, places):
        for k, place in enumerate(places):
            self.coming[k].wait()
            self.full_ref[k] = self.low_ref[k].astype(f32)
            self.moves.send(self.full_ref.at[k], self.target.at[place])


class Line:
    def __init__(self, ref):
        self.ref = ref

    def __getitem__(self, _):
        return self.ref[...].reshape(1, -1)


def row_sum(block):
    return jnp.sum(block, axis=0, keepdims=True)


def pack_kernel(parts, place_ref, lengths_ref, tokens_ref, values_ref, merge_ref, *outs):
    order_ref, own_ref = outs[-2:]
    merge_ref = Line(merge_ref)
    rows = tokens_ref.shape[0]
    share = rows // parts
    me = place_ref[0]
    for i in range(rows):
        rank = jnp.int32(0)
        for j in range(rows):
            if j != i:
                ahead = lengths_ref[j] >= lengths_ref[i] if j < i else lengths_ref[j] > lengths_ref[i]
                rank = rank + ahead.astype(jnp.int32)
        turn = rank // parts
        spot = rank % parts
        owner = jnp.where(turn % 2 == 0, spot, parts - 1 - spot)
        order_ref[owner * share + turn] = jnp.int32(i)
    for r in range(share):
        own_ref[r] = lengths_ref[order_ref[me * share + r]]
    columns = values_ref[...].T
    lane = lax.broadcasted_iota(jnp.int32, columns.shape, 1)
    for r in range(share):
        for d in range(parts):
            row = order_ref[(me ^ d) * share + r]
            column = jnp.sum(jnp.where(lane == row, columns, 0.0), axis=1, keepdims=True)
            outs[r * parts + d][...] = (
                tokens_ref[row].astype(f32) + column * merge_ref[...]
            ).astype(bf16)


def deal_kernel(parts, place_ref, order_ref, source_ref, values_ref, *sends):
    rows, slots, width = source_ref.shape
    share = rows // parts
    me = place_ref[0]
    for d in range(parts):
        for r in range(share):
            row = order_ref[(me ^ d) * share + r]
            sends[d][r, :slots] = source_ref[row]
            value = values_ref[pl.ds(row, 1), :]
            high = value.astype(bf16).astype(f32)
            rest = value - high
            middle = rest.astype(bf16).astype(f32)
            three = jnp.concatenate(
                [high, middle, rest - middle, jnp.zeros((EXTRA - 3, slots), f32)], axis=0
            )
            if width > slots:
                three = jnp.concatenate([three, jnp.zeros((EXTRA, width - slots), f32)], axis=1)
            sends[d][r, slots:] = three.astype(bf16)


def undeal_kernel(parts, share, place_ref, order_ref, *refs):
    pieces, (out_hbm, low_ref, full_ref, sems) = refs[:parts], refs[parts:]
    moves = Moves(sems)
    me = place_ref[0]
    places = [(d, r) for d in range(parts) for r in range(share)]
    unpack = Unpack(moves, [pieces[d].at[r] for d, r in places], out_hbm, low_ref, full_ref)
    unpack.run([order_ref[(me ^ d) * share + r] for d, r in places])
    moves.finish()


def attend(length, q_ref, k_ref, v_ref, put_context, lse_ref):
    pairs, span, _ = q_ref.shape
    c = LOG2E / DH**0.5
    lane = lax.broadcasted_iota(jnp.int32, (1, 128), 1)
    low = lane < DH

    def branch(n):
        def pair(p, carry):
            sl = pl.ds(pl.multiple_of(p * 128, 128), 128)
            q, k, v = q_ref[p], k_ref[p, :n], v_ref[p, :n]
            real = lax.broadcasted_iota(jnp.int32, (span, 128), 1) + (n - 128) < length
            found, sizes = [], []
            for h in range(2):
                mine = low if h == 0 else ~low
                s = dot(jnp.where(mine, q, jnp.zeros_like(q)), k, NT)
                tail = jnp.where(real, s[:, n - 128 :], -1e30)
                s = jnp.concatenate([s[:, : n - 128], tail], axis=1) if n > 128 else tail
                peak = jnp.max(s, axis=1, keepdims=True) * c
                e = jnp.exp2(s * c - peak)
                total = jnp.sum(e, axis=1, keepdims=True)
                found.append(dot(e.astype(bf16), jnp.where(mine, v, jnp.zeros_like(v))) / total)
                sizes.append(peak + jnp.log2(total))
            put_context(sl, (found[0] + found[1]).astype(bf16))
            kept = jnp.where(lane == 2 * p, sizes[0], lse_ref[...])
            lse_ref[...] = jnp.where(lane == 2 * p + 1, sizes[1], kept)
            return carry

        lse_ref[...] = jnp.zeros_like(lse_ref)
        lax.fori_loop(0, pairs, pair, 0)

    blocks = (length + 127) // 128
    for b in range(1, span // 128 + 1):
        pl.when(blocks == b)(functools.partial(branch, 128 * b))


def attend_back(length, q_ref, k_ref, v_ref, ctx_ref, lse_ref, do_ref, get, put):
    pairs, span, _ = q_ref.shape
    scale = 1.0 / DH**0.5
    c = LOG2E * scale
    lane = lax.broadcasted_iota(jnp.int32, (1, 128), 1)
    low = lane < DH

    def branch(n):
        def pair(p, carry):
            sl = pl.ds(pl.multiple_of(p * 128, 128), 128)
            get(p)
            q, k, v, do = q_ref[p], k_ref[p, :n], v_ref[p, :n], do_ref[:, sl]
            real = lax.broadcasted_iota(jnp.int32, (span, 128), 1) + (n - 128) < length
            product = do.astype(f32) * ctx_ref[:, sl].astype(f32)
            sizes = lse_ref[...]
            dq = dk = dv = 0.0
            for h in range(2):
                mine = low if h == 0 else ~low
                qh = jnp.where(mine, q, jnp.zeros_like(q))
                doh = jnp.where(mine, do, jnp.zeros_like(do))
                kh = jnp.where(mine, k, jnp.zeros_like(k))
                delta = jnp.sum(jnp.where(mine, product, 0.0), axis=1, keepdims=True)
                lse = jnp.sum(jnp.where(lane == 2 * p + h, sizes, 0.0), axis=1, keepdims=True)
                prob = jnp.exp2(dot(qh, k, NT) * c - lse)
                tail = jnp.where(real, prob[:, n - 128 :], 0.0)
                prob = jnp.concatenate([prob[:, : n - 128], tail], axis=1) if n > 128 else tail
                ds = (prob * (dot(doh, v, NT) - delta)).astype(bf16)
                dq = dq + dot(ds, kh)
                dk = dk + dot(ds, qh, TN)
                dv = dv + dot(prob.astype(bf16), doh, TN)
            dk, dv = (dk * scale).astype(bf16), dv.astype(bf16)
            if n < span:
                blank = jnp.zeros((span - n, 128), bf16)
                dk = jnp.concatenate([dk, blank], axis=0)
                dv = jnp.concatenate([dv, blank], axis=0)
            put(p, sl, (dq * scale).astype(bf16), dk, dv)
            return carry

        lax.fori_loop(0, pairs, pair, 0)

    blocks = (length + 127) // 128
    for b in range(1, span // 128 + 1):
        pl.when(blocks == b)(functools.partial(branch, 128 * b))


def forward_kernel(
    parts, row, place_ref, own_ref, bq_ref, bv_ref, bo_ref, wq_hbm, wk_hbm, wv_hbm, wo_hbm, *refs
):
    bq_ref, bv_ref, bo_ref = Line(bq_ref), Line(bv_ref), Line(bo_ref)
    pieces = refs[:parts]
    xc_hbm, q_hbm, k_hbm, v_hbm, lse_hbm, hat_hbm, rstd_hbm = refs[parts : parts + 7]
    w_ref, xc_ref, q_ref, k_ref, v_ref, lse_ref, hat_ref, rstd_ref, sems = refs[parts + 7 :]
    moves = Moves(sems)
    me = place_ref[0]
    step = pieces[0].shape[0]
    arriving = []
    for d in range(parts):
        here = pl.ds(pl.multiple_of((me ^ d) * step, step), step)
        arriving.append(moves.start(pieces[d], xc_ref.at[1, here]))
    hbm = (wq_hbm, wk_hbm, wv_hbm, wo_hbm)
    weights = [moves.start(w, w_ref.at[k]) for k, w in enumerate(hbm)]
    for copy in arriving:
        copy.wait()
    moves.send(xc_ref.at[1], xc_hbm.at[1])
    x = xc_ref[1]
    weights[0].wait()

    def by_pair(ref, block):
        for p in range(ref.shape[0]):
            ref[p] = block[:, p * 128 : (p + 1) * 128].astype(bf16)

    by_pair(q_ref, dot(x, w_ref[0]) + bq_ref[...])
    moves.send(q_ref, q_hbm)
    weights[1].wait()
    by_pair(k_ref, dot(x, w_ref[1]))
    moves.send(k_ref, k_hbm)
    weights[2].wait()
    by_pair(v_ref, dot(x, w_ref[2]) + bv_ref[...])
    moves.send(v_ref, v_hbm)

    def put(sl, block):
        xc_ref[0, :, sl] = block

    attend(own_ref[row], q_ref, k_ref, v_ref, put, lse_ref)
    moves.send(xc_ref.at[0], xc_hbm.at[0])
    moves.send(lse_ref, lse_hbm)
    weights[3].wait()
    for i in range(xc_ref.shape[1] // BLOCK):
        sl = slice(i * BLOCK, (i + 1) * BLOCK)
        a = xc_ref[1, sl].astype(f32) + dot(xc_ref[0, sl], w_ref[3]) + bo_ref[...]
        center = a - jnp.mean(a, axis=1, keepdims=True)
        rstd = lax.rsqrt(jnp.mean(center * center, axis=1, keepdims=True) + EPS)
        hat_ref[sl] = center * rstd
        rstd_ref[sl] = jnp.broadcast_to(rstd, (BLOCK, rstd_ref.shape[1]))
        moves.send(hat_ref.at[sl], hat_hbm.at[sl])
    moves.send(rstd_ref, rstd_hbm)
    moves.finish()


def norm_back(g, hat, rstd, gain):
    scaled = g * gain
    first = jnp.mean(scaled, axis=1, keepdims=True)
    second = jnp.mean(scaled * hat, axis=1, keepdims=True)
    return rstd * (scaled - first - hat * second)


def feed_kernel(
    parts,
    share,
    steps,
    place_ref,
    gain_one_ref,
    shift_one_ref,
    wi_ref,
    bi_ref,
    wo_ref,
    bo_ref,
    gain_ref,
    shift_ref,
    *refs,
):
    gain_one_ref, shift_one_ref, bo_ref = Line(gain_one_ref), Line(shift_one_ref), Line(bo_ref)
    gain_ref, shift_ref = Line(gain_ref), Line(shift_ref)
    hats, refs = refs[:share], refs[share:]
    cots, refs = refs[:parts], refs[parts:]
    slope_ref, low_hbm, branch_hbm, summed_hbm, *refs = refs
    outs, refs = refs[:parts], refs[parts:]
    sums_ref, keep_ref, send_ref, total_ref, low_ref, branch_ref, act_ref, cot_ref, out_ref, sems = refs
    step = pl.program_id(0)
    count, width = total_ref.shape
    chunk = wi_ref.shape[1]
    me = place_ref[0]
    slots = outs[0].shape[1]
    span = count // share
    blocks = count // BLOCK

    def place(d, r):
        return pl.ds(pl.multiple_of((r * parts + (me ^ d)) * slots, slots), slots)

    rows = [slice(r * span, (r + 1) * span) for r in range(share)]
    pairs = [(d, r) for d in range(parts) for r in range(share)]
    coming = [(hats[r], total_ref.at[rows[r]]) for r in range(share)]
    coming += [(cots[d].at[r, :slots], cot_ref.at[place(d, r)]) for d, r in pairs]
    going = [(low_ref, low_hbm), (branch_ref, branch_hbm), (total_ref, summed_hbm)]
    going += [(out_ref.at[place(d, r)], outs[d].at[r]) for d, r in pairs]
    copies = [
        pltpu.make_async_copy(source, target, sems.at[k])
        for k, (source, target) in enumerate(coming + going)
    ]
    coming, going = copies[: len(coming)], copies[len(coming) :]

    @pl.when(step == 0)
    def _():
        for copy in coming:
            copy.start()
        for r in range(share):
            coming[r].wait()
            normed = total_ref[rows[r]] * gain_one_ref[...] + shift_one_ref[...]
            low_ref[rows[r]] = normed.astype(bf16)
            total_ref[rows[r]] = normed + bo_ref[...]
        going[0].start()

    def run(last):
        def first(i):
            return dot(low_ref[i * BLOCK : (i + 1) * BLOCK], wi_ref[...]) + bi_ref[...]

        if last:
            for copy in coming[share:]:
                copy.wait()
        ahead = first(0)
        sums = [0.0, 0.0, 0.0]
        for i in range(blocks):
            inner = ahead
            if i + 1 < blocks:
                ahead = first(i + 1)
            sl = slice(i * BLOCK, (i + 1) * BLOCK)
            phi = 0.5 + 0.5 * lax.erf(inner * RSQRT2)
            act = (inner * phi).astype(bf16)
            slope_ref[0, sl] = (phi + inner * (jnp.exp(-0.5 * inner * inner) * RSQRT2PI)).astype(bf16)
            act_ref[sl, pl.ds(pl.multiple_of(step * chunk, chunk), chunk)] = act
            a = total_ref[sl] + dot(act, wo_ref[...])
            if not last:
                total_ref[sl] = a
                continue
            center = a - jnp.mean(a, axis=1, keepdims=True)
            rstd = lax.rsqrt(jnp.mean(center * center, axis=1, keepdims=True) + EPS)
            hat = center * rstd
            out_ref[sl] = (hat * gain_ref[...] + shift_ref[...]).astype(bf16)
            g = cot_ref[sl].astype(f32)
            back = norm_back(g, hat, rstd, gain_ref[...])
            total_ref[sl] = back
            low = back.astype(bf16)
            branch_ref[sl] = low
            for k, term in enumerate((g * hat, g, low.astype(f32))):
                sums[k] = sums[k] + row_sum(term)
        if last:
            for copy in going[1:]:
                copy.start()
            sums_ref[...] = jnp.concatenate(sums + [jnp.zeros((5, width), f32)], axis=0)

    pl.when(step < steps - 1)(functools.partial(run, False))
    pl.when(step == steps - 1)(functools.partial(run, True))

    @pl.when(step >= steps)
    def _():
        here = pl.ds(pl.multiple_of((step - steps) * chunk, chunk), chunk)
        grad = dot(act_ref[:, here], branch_ref[...], TN).astype(bf16)
        core = place_ref[1]
        pairs, height = keep_ref.shape[1], keep_ref.shape[2]
        for z in range(pairs):
            for unit in range(parts):
                base = (2 * z * parts + unit) * height
                even = grad[base : base + height]
                odd = grad[base + parts * height : base + (parts + 1) * height]
                keep_ref[unit ^ me, z] = jnp.where(core == 0, even, odd)
                send_ref[unit ^ me, z] = jnp.where(core == 0, odd, even)

    @pl.when(step == 2 * steps - 1)
    def _():
        for copy in going:
            copy.wait()


def feed_back_kernel(share, place_ref, gain_ref, *refs):
    gain_ref = Line(gain_ref)
    (branch_hbm, summed_hbm, low_hbm, slope_hbm, wi_hbm, wo_hbm), refs = refs[:6], refs[6:]
    hats_hbm, rstds_hbm, refs = refs[:share], refs[share : 2 * share], refs[2 * share :]
    keep_hbm, send_hbm, bias_ref, attended_hbm, attn_hbm, sums_ref, *refs = refs
    branch_ref, low_ref, slope_ref, wi_ref, wo_ref, inner_ref, total_ref, *refs = refs
    attn_ref, hat_ref, rstd_ref, keep_ref, send_ref, sems = refs
    moves = Moves(sems)
    me = place_ref[0]
    count, width = total_ref.shape
    span = count // share
    blocks = count // BLOCK
    units = slope_ref.shape[0]
    coming = [[] for _ in range(units)]

    def take(u, source, target):
        coming[u].append(moves.start(source, target))

    for u in range(units):
        chunk = slice(u * width, (u + 1) * width)
        take(u, wo_hbm.at[chunk], wo_ref.at[u])
        if u == 0:
            take(u, branch_hbm, branch_ref)
        take(u, slope_hbm.at[u], slope_ref.at[u])
        take(u, wi_hbm.at[:, chunk], wi_ref.at[u])
        if u == 0:
            take(u, summed_hbm, total_ref)
            take(u, low_hbm, low_ref)
    for r in range(share):
        rows = slice(r * span, (r + 1) * span)
        take(units - 1, hats_hbm[r], hat_ref.at[rows])
        take(units - 1, rstds_hbm[r], rstd_ref.at[rows])
    for u in range(units):
        last = u == units - 1
        for copy in coming[u]:
            copy.wait()

        def first(i):
            return dot(branch_ref[i * BLOCK : (i + 1) * BLOCK], wo_ref[u], NT)

        ahead = first(0)
        bias = 0.0
        sums = [0.0, 0.0, 0.0]
        for i in range(blocks):
            now = ahead
            if i + 1 < blocks:
                ahead = first(i + 1)
            sl = slice(i * BLOCK, (i + 1) * BLOCK)
            inner = (now * slope_ref[u, sl].astype(f32)).astype(bf16)
            inner_ref[sl] = inner
            bias = bias + row_sum(inner.astype(f32))
            g = total_ref[sl] + dot(inner, wi_ref[u], NT)
            if not last:
                total_ref[sl] = g
                continue
            hat = hat_ref[sl]
            back = norm_back(g, hat, rstd_ref[sl, :1], gain_ref[...])
            total_ref[sl] = back
            low = back.astype(bf16)
            attn_ref[sl] = low
            for k, term in enumerate((g * hat, g, low.astype(f32))):
                sums[k] = sums[k] + row_sum(term)
        bias_ref[u : u + 1] = bias
        if last:
            moves.send(total_ref, attended_hbm)
            moves.send(attn_ref, attn_hbm)
            sums_ref[...] = jnp.concatenate(sums + [jnp.zeros((5, width), f32)], axis=0)
        grad = dot(low_ref[...], inner_ref[...], TN).astype(bf16)
        put_unit(place_ref[1], grad, keep_ref, send_ref, u)
        moves.send(send_ref.at[u], send_hbm.at[u ^ me])
        moves.send(keep_ref.at[u], keep_hbm.at[u ^ me])
    moves.finish()


def put_unit(core, grad, keep_ref, send_ref, unit):
    pairs = keep_ref.shape[1]
    rows = grad.shape[0] // (2 * pairs)
    for z in range(pairs):
        even = grad[2 * z * rows : (2 * z + 1) * rows]
        odd = grad[(2 * z + 1) * rows : (2 * z + 2) * rows]
        keep_ref[unit, z] = jnp.where(core == 0, even, odd)
        send_ref[unit, z] = jnp.where(core == 0, odd, even)


def square_kernel(share, place_ref, two_ref, one_ref, bias_ref, *refs):
    zeros, refs = refs[:share], refs[share:]
    xc_hbm, grads_hbm, refs = refs[:share], refs[share : 2 * share], refs[2 * share :]
    outs_hbm, (xc_ref, grads_ref, *outs, sems) = refs[:4], refs[4:]
    moves = Moves(sems)
    core = place_ref[1]
    units, span = grads_ref.shape[0], grads_ref.shape[1] // share
    coming = [[] for _ in range(units)]
    for u in range(units):
        for r in range(share):
            rows = slice(r * span, (r + 1) * span)
            if u < 2:
                coming[u].append(moves.start(xc_hbm[r].at[u], xc_ref.at[u, rows]))
            coming[u].append(moves.start(grads_hbm[r].at[u], grads_ref.at[u, rows]))
    zero = zeros[0][0:3]
    for ref in zeros[1:]:
        zero = zero + ref[0:3]
    vectors = jnp.concatenate([two_ref[0:3], one_ref[0:3], zero, bias_ref[...]], axis=0)
    blank = jnp.zeros((EXTRA - vectors.shape[0], vectors.shape[1]), f32)
    vectors = jnp.concatenate([vectors, blank], axis=0)
    for u in range(units):
        for copy in coming[u]:
            copy.wait()
        grad = dot(xc_ref[min(u, 1)], grads_ref[u], TN).astype(bf16)
        group, at = u // 2, u % 2
        keep_ref, send_ref = outs[2 * group : 2 * group + 2]
        pairs, rows, width = keep_ref.shape[1:]
        tail = EXTRA if group == 0 else 0
        rows = rows - tail

        def block(b):
            found = grad[b * rows : (b + 1) * rows]
            if not tail:
                return found
            extra = vectors if u == 0 else jnp.zeros_like(vectors)
            return jnp.concatenate([found.astype(f32), extra], axis=0).astype(bf16)

        for z in range(pairs):
            even, odd = block(2 * z), block(2 * z + 1)
            keep_ref[at, z] = jnp.where(core == 0, even, odd)
            send_ref[at, z] = jnp.where(core == 0, odd, even)
        for k, ref in ((1, send_ref), (0, keep_ref)):
            moves.send(ref.at[at], outs_hbm[2 * group + k].at[at])
    moves.finish()


def backward_kernel(parts, row, place_ref, own_ref, *refs):
    hbm, refs = refs[:11], refs[11:]
    wo_hbm, low_hbm, q_hbm, k_hbm, v_hbm, xc_hbm, lse_hbm, attended_hbm, wq_hbm, wk_hbm, wv_hbm = hbm
    values, refs = refs[:parts], refs[parts:]
    before, refs = (refs[:parts], refs[parts:]) if row else ((), refs)
    grads_hbm, outs, sums_ref, refs = refs[0], refs[1 : 1 + parts], refs[1 + parts], refs[2 + parts :]
    *refs, sems, in_sems = refs
    if row:
        *refs, before_ref = refs
    w_ref, low_ref, qkv_ref, context_ref, lse_ref, attended_ref, grads_ref, do_ref, total_ref, value_ref = refs
    moves = Moves(sems)
    me = place_ref[0]
    slots = outs[0].shape[1]
    span, width = low_ref.shape
    rows = slice(row * span, (row + 1) * span)

    def inward(p, k):
        return pltpu.make_async_copy(
            (q_hbm, k_hbm, v_hbm)[k].at[p], qkv_ref.at[k, p], in_sems.at[p, k]
        )

    early = [moves.start(wo_hbm, w_ref.at[0]), moves.start(low_hbm.at[rows], low_ref)]
    early += [moves.start(lse_hbm, lse_ref), moves.start(xc_hbm.at[0], context_ref)]
    for p in range(width // 128):
        for k in range(3):
            inward(p, k).start()
    late = [moves.start(ref, w_ref.at[1 + k]) for k, ref in enumerate((wq_hbm, wk_hbm, wv_hbm))]
    late.append(moves.start(attended_hbm.at[rows], attended_ref))
    for d, pieces in enumerate(before):
        late.append(moves.start(pieces, before_ref.at[d]))
    for d in range(parts):
        here = pl.ds(pl.multiple_of((me ^ d) * slots, slots), slots)
        late.append(moves.start(values[d].at[row, slots:, :slots], value_ref.at[:, here]))
    for copy in early:
        copy.wait()
    moves.send(low_ref, grads_hbm.at[0])
    do_ref[...] = dot(low_ref[...], w_ref[0], NT).astype(bf16)

    def get(p):
        for k in range(3):
            inward(p, k).wait()

    def put(p, sl, *blocks):
        for k, block in enumerate(blocks):
            grads_ref[k, :, sl] = block

    q_ref, k_ref, v_ref = [qkv_ref.at[k] for k in range(3)]
    attend_back(own_ref[row], q_ref, k_ref, v_ref, context_ref, lse_ref, do_ref, get, put)
    moves.send(grads_ref, grads_hbm.at[pl.ds(1, 3)])
    for copy in late:
        copy.wait()
    for d in range(len(before)):
        moves.send(before_ref.at[d], outs[d].at[pl.ds(0, row)])
    dq, dk, dv = grads_ref[0], grads_ref[1], grads_ref[2]
    low = (
        attended_ref[...]
        + dot(dq, w_ref[1], NT)
        + dot(dk, w_ref[2], NT)
        + dot(dv, w_ref[3], NT)
    ).astype(bf16)
    total_ref[...] = low
    for d in range(parts):
        here = pl.ds(pl.multiple_of((me ^ d) * slots, slots), slots)
        moves.send(total_ref.at[here], outs[d].at[row])
    merge = row_sum(dot(value_ref[...], low))
    sums_ref[...] = jnp.concatenate(
        [
            row_sum(dq.astype(f32)),
            row_sum(dv.astype(f32)),
            merge,
            jnp.zeros((5, merge.shape[1]), f32),
        ],
        axis=0,
    )
    moves.finish()


def plane_first_kernel(place_ref, keep_ref, got_ref, *outs):
    keep_x, send_x, keep_y, send_y = outs
    half = keep_x.shape[2]
    units, blocks = keep_ref.shape[:2]
    for d in range(units):
        for i in range(blocks):
            total = (keep_ref[d, i].astype(f32) + got_ref[d, i].astype(f32)).astype(bf16)
            (send_x if d % 2 else keep_x)[d // 2, i] = total[:half]
            (send_y if d // 2 else keep_y)[d % 2, i] = total[half:]


def plane_second_kernel(groups, place_ref, *refs):
    terms, outs = refs[: 4 * groups], refs[4 * groups :]
    for g in range(groups):
        keep_x, got_x, keep_y, got_y = terms[4 * g : 4 * g + 4]
        for i in range(keep_x.shape[1]):
            for j in range(2):
                outs[j][g, i] = (keep_x[j, i].astype(f32) + got_x[j, i].astype(f32)).astype(bf16)
                outs[2 + j][g, i] = (keep_y[j, i].astype(f32) + got_y[j, i].astype(f32)).astype(bf16)


def plane_third_kernel(spot, place_ref, keep_x, got_x, keep_y, got_y, *outs):
    groups, blocks = keep_x.shape[:2]
    bit = place_ref[spot]
    for g in range(groups):
        for i in range(blocks // 2):
            for out, j in ((outs[0], 2 * i + bit), (outs[1], 2 * i + 1 - bit)):
                top = keep_x[g, j].astype(f32) + got_x[g, j].astype(f32)
                bottom = keep_y[g, j].astype(f32) + got_y[g, j].astype(f32)
                out[g, i] = jnp.concatenate([top, bottom], axis=0).astype(bf16)


def quarter_kernel(parts, place_ref, keep_ref, got_ref, *outs):
    me = place_ref[0]
    units, blocks, rows = keep_ref.shape[:3]
    half = rows // 2
    for u in range(units):
        for i in range(blocks):
            total = (keep_ref[u, i].astype(f32) + got_ref[u, i].astype(f32)).astype(bf16)
            for d in range(parts):
                for h in range(2):

                    @pl.when((me ^ d) == 2 * u + h)
                    def _(d=d, h=h, i=i, total=total):
                        outs[d][0, i] = total[h * half : (h + 1) * half]


def halves_kernel(place_ref, keep_ref, got_ref, top_ref, bottom_ref):
    half = top_ref.shape[2]
    for u in range(keep_ref.shape[0]):
        total = keep_ref[u, 0].astype(f32) + got_ref[u, 0].astype(f32)
        top_ref[u, 0] = total[:half].astype(bf16)
        bottom_ref[u, 0] = total[half:].astype(bf16)


def both_kernel(place_ref, top_ref, got_top, bottom_ref, got_bottom, *outs):
    for u in range(top_ref.shape[0]):
        top = top_ref[u, 0].astype(f32) + got_top[u, 0].astype(f32)
        bottom = bottom_ref[u, 0].astype(f32) + got_bottom[u, 0].astype(f32)
        if len(outs) == 2:
            outs[0][u, 0] = top.astype(bf16)
            outs[1][u, 0] = bottom.astype(bf16)
            continue
        total = jnp.concatenate([top, bottom], axis=0)
        rows = outs[u].shape[0]
        outs[u][...] = total[:rows]
        if u == 0:
            outs[2][...] = total[rows:]


def fourth_kernel(parts, bit_spot, place_ref, *refs):
    pieces, outs = refs[:parts], refs[parts:]
    blocks = pieces[0].shape[1]
    bit = place_ref[bit_spot]

    def total(i):
        found = pieces[0][0, i].astype(f32)
        for piece in pieces[1:]:
            found = found + piece[0, i].astype(f32)
        return found.astype(bf16)

    for i in range(blocks // 2):
        outs[0][0, i] = total(2 * i + bit)
        outs[1][0, i] = total(2 * i + 1 - bit)


def merge_kernel(spot, place_ref, keep_ref, got_ref, *outs):
    groups, blocks = keep_ref.shape[:2]

    def total(g, i):
        return (keep_ref[g, i].astype(f32) + got_ref[g, i].astype(f32)).astype(bf16)

    for g in range(groups):
        if spot is None:
            for i in range(blocks):
                outs[0][g, i] = total(g, i)
            continue
        bit = place_ref[spot]
        for i in range(blocks // 2):
            outs[0][g, i] = total(g, 2 * i + bit)
            outs[1][g, i] = total(g, 2 * i + 1 - bit)


def finish_kernel(parts, place_ref, *refs):
    pieces, outs = refs[:parts], refs[parts:]
    me = place_ref[0]
    rows, width = pieces[0].shape[2:]
    for q in range(parts):
        for d in range(parts):

            @pl.when((me ^ d) == q)
            def _(q=q, d=d):
                if pieces[d].shape[0] == 2:
                    outs[0][q * rows : (q + 1) * rows] = pieces[d][0, 0].astype(f32)
                    outs[1][:, q * width : (q + 1) * width] = pieces[d][1, 0].astype(f32)
                else:
                    outs[q // 2][q % 2 * rows : (q % 2 + 1) * rows] = pieces[d][0, 0].astype(f32)


def swap(array, axis, size, distance):
    return lax.ppermute(array, axis, [(i, i ^ distance) for i in range(size)])


def body(
    parts,
    size,
    tokens,
    values,
    lengths,
    merge,
    w_query,
    w_key,
    w_value,
    w_output,
    b_query,
    b_value,
    b_output,
    gain_one,
    shift_one,
    w_inner,
    b_inner,
    w_outer,
    b_outer,
    gain_two,
    shift_two,
    cotangent,
):
    rows, slots, width = tokens.shape
    hidden = w_inner.shape[1]
    share = rows // parts
    span = slots * parts
    count = share * span
    pairs = size // 2
    blk = width // size
    me = lax.axis_index("seq")
    place = lax.axis_index("batch")
    bits = size.bit_length() - 1
    spot = jnp.stack([me] + [(place >> k) & 1 for k in range(bits)]).astype(jnp.int32)
    line = lambda vector: vector.reshape(1, -1)
    low = lambda *shape: Shape(shape, bf16)
    full = lambda *shape: Shape(shape, f32)
    others = range(1, parts)
    call = Sequence()

    def exchange(pieces):
        return [pieces[0]] + [swap(pieces[d], "seq", parts, d) for d in others]

    packed = call(
        functools.partial(pack_kernel, parts),
        [(VM, low(slots, width))] * rows
        + [(SM, Shape((rows,), jnp.int32)), (SM, Shape((share,), jnp.int32))],
        [(SM, spot), (SM, lengths), (VM, tokens), (VM, values), (VM, merge)],
        limit=60,
        name="pack",
    )
    order, own = packed[rows:]
    x_parts = [exchange(packed[r * parts : (r + 1) * parts]) for r in range(share)]
    cot_parts = exchange(
        call(
            functools.partial(deal_kernel, parts),
            [(VM, low(share, slots + EXTRA, width))] * parts,
            [(SM, spot), (SM, order), (VM, cotangent), (VM, values)],
            limit=60,
            name="deal",
        )
    )

    forward = []
    DMA = pltpu.SemaphoreType.DMA
    for r in range(share):
        results = (
            [low(2, span, width)]
            + [low(width // 128, span, 128)] * 3
            + [full(span, 128), full(span, width), full(span, 128)]
        )
        forward.append(
            call(
                functools.partial(forward_kernel, parts, r),
                [(HBM, shape) for shape in results],
                [(SM, spot), (SM, own)]
                + [(VM, b) for b in (b_query, b_value, b_output)]
                + [(HBM, w) for w in (w_query, w_key, w_value, w_output)]
                + [(HBM, x) for x in x_parts[r]],
                scratch=[pltpu.VMEM((4, width, width), bf16)]
                + [pltpu.VMEM(shape.shape, shape.dtype) for shape in results]
                + [DMA((4 + parts + 2 * parts + 6,))],
                limit=60,
                heavy=True,
                name="attention_forward",
            )
        )
    hats = [f[5] for f in forward]
    rstds = [f[6] for f in forward]

    chunk = width
    steps = hidden // chunk
    clip = lambda i: jnp.minimum(i, steps - 1)
    tall_low, tall_full = low(count, width), full(count, width)
    piece_low = low(share, slots, width)
    unit_low = low(parts, pairs, blk, width)
    outer_spec = pl.BlockSpec(
        (parts, pairs // steps, blk, width), lambda i: (0, jnp.maximum(i - steps, 0), 0, 0)
    )
    fed = call(
        functools.partial(feed_kernel, parts, share, steps),
        [(pl.BlockSpec((1, count, chunk), lambda i: (clip(i), 0, 0)), low(steps, count, chunk))]
        + [(HBM, tall_low), (HBM, tall_low), (HBM, tall_full)]
        + [(HBM, piece_low)] * parts
        + [(VM, full(8, width))]
        + [(outer_spec, unit_low)] * 2,
        [
            (SM, spot),
            (VM, gain_one),
            (VM, shift_one),
            (pl.BlockSpec((width, chunk), lambda i: (0, clip(i))), w_inner),
            (pl.BlockSpec((1, chunk), lambda i: (0, clip(i))), line(b_inner)),
            (pl.BlockSpec((chunk, width), lambda i: (clip(i), 0)), w_outer),
            (VM, b_outer),
            (VM, gain_two),
            (VM, shift_two),
        ]
        + [(HBM, hat) for hat in hats]
        + [(HBM, c) for c in cot_parts],
        scratch=[pltpu.VMEM((count, width), f32)]
        + [pltpu.VMEM((count, width), bf16)] * 2
        + [pltpu.VMEM((count, hidden), bf16)]
        + [pltpu.VMEM((count, width), bf16)] * 2
        + [DMA((share + 3 + 2 * share * parts,))],
        grid=(2 * steps,),
        limit=60,
        heavy=True,
        name="feed_forward",
    )
    slope, normed_low, d_branch, d_summed = fed[:4]
    out_parts = exchange(fed[4 : 4 + parts])
    sums_two, outer_keep, outer_send = fed[4 + parts :]
    outer_got = swap(outer_send, "batch", size, 1)

    inner_keep, inner_send, inner_bias, d_attended, d_attn, sums_one = call(
        functools.partial(feed_back_kernel, share),
        [(HBM, unit_low)] * 2
        + [(VM, full(steps, width)), (HBM, tall_full), (HBM, tall_low), (VM, full(8, width))],
        [(SM, spot), (VM, gain_one)]
        + [(HBM, a) for a in (d_branch, d_summed, normed_low, slope, w_inner, w_outer)]
        + [(HBM, hat) for hat in hats]
        + [(HBM, rstd) for rstd in rstds],
        scratch=[pltpu.VMEM((count, width), bf16)] * 2
        + [pltpu.VMEM((steps, count, width), bf16)]
        + [pltpu.VMEM((steps, width, width), bf16)] * 2
        + [pltpu.VMEM((count, width), bf16), pltpu.VMEM((count, width), f32)]
        + [pltpu.VMEM((count, width), bf16), pltpu.VMEM((count, width), f32)]
        + [pltpu.VMEM((count, 128), f32)]
        + [pltpu.VMEM(unit_low.shape, bf16)] * 2
        + [DMA((3 * steps + 3 + 2 * share + 2 + 2 * steps,))],
        limit=60,
        heavy=True,
        name="feed_backward",
    )
    inner_got = swap(inner_send, "batch", size, 1)

    def simple(kernel, ins, outs, name, heavy=False):
        return call(
            kernel,
            [(VM, shape) for shape in outs],
            [(SM, spot)] + [(VM, array) for array in ins],
            heavy=heavy,
            name=name,
        )

    def plane_first(keep, got, name):
        rows = keep.shape[2]
        first, rest = low(2, pairs, blk // 2, width), low(2, pairs, rows - blk // 2, width)
        keep_x, send_x, keep_y, send_y = simple(
            plane_first_kernel, [keep, got], [first, first, rest, rest], name
        )
        return keep_x, swap(send_x, "seq", parts, 1), keep_y, swap(send_y, "seq", parts, 2)

    def plane_second(groups, name):
        count = len(groups)
        first, rest = [low(count, *groups[0][k].shape[1:]) for k in (0, 2)]
        keep_x, send_x, keep_y, send_y = simple(
            functools.partial(plane_second_kernel, count),
            [term for terms in groups for term in terms],
            [first, first, rest, rest],
            name,
        )
        return keep_x, swap(send_x, "seq", parts, 2), keep_y, swap(send_y, "seq", parts, 1)

    def plane_third(terms, name):
        shape = low(terms[0].shape[0], pairs // 2, terms[0].shape[2] + terms[2].shape[2], width)
        keep, send = simple(
            functools.partial(plane_third_kernel, 2), list(terms), [shape, shape], name
        )
        return keep, swap(send, "batch", size, 2)

    def merge_terms(spot_index, terms, name):
        groups, blocks, rows, _ = terms[0].shape
        if spot_index is None:
            shapes = [low(groups, blocks, rows, width)]
        else:
            shapes = [low(groups, blocks // 2, rows, width)] * 2
        kernel = functools.partial(merge_kernel, spot_index)
        return simple(kernel, terms, shapes, name)

    def along_line(terms, name):
        for bit in range(2, bits):
            keep, send = merge_terms(1 + bit, terms, name)
            terms = keep, swap(send, "batch", size, 1 << bit)
        return terms

    def gather(terms, name):
        (block,) = merge_terms(None, terms, name)
        return exchange([block] * parts)

    def undeal(pieces):
        return call(
            functools.partial(undeal_kernel, parts, share),
            [(HBM, full(rows, slots, width))],
            [(SM, spot), (SM, order)] + [(HBM, piece) for piece in pieces],
            scratch=[pltpu.VMEM((rows, slots, width), dtype) for dtype in (bf16, f32)]
            + [DMA((2 * rows,))],
            limit=16,
            heavy=True,
            name="undeal",
        )[0]

    layer_out = undeal(out_parts)
    outer_terms = plane_first(outer_keep, outer_got, "outer_core")
    inner_terms = plane_first(inner_keep, inner_got, "inner_core")

    grads, token_parts, sums_zero = [], [], []
    pair_count = width // 128
    for r in range(share):
        xc, query, key, value, lse = forward[r][:5]
        back = call(
            functools.partial(backward_kernel, parts, r),
            [(HBM, low(4, span, width))]
            + [(HBM, low(r + 1, slots, width))] * parts
            + [(VM, full(8, width))],
            [(SM, spot), (SM, own)]
            + [(HBM, array) for array in (w_output, d_attn, query, key, value, xc, lse, d_attended)]
            + [(HBM, w) for w in (w_query, w_key, w_value)]
            + [(HBM, c) for c in cot_parts]
            + [(HBM, piece) for piece in token_parts],
            scratch=[
                pltpu.VMEM((4, width, width), bf16),
                pltpu.VMEM((span, width), bf16),
                pltpu.VMEM((3, pair_count, span, 128), bf16),
                pltpu.VMEM((span, width), bf16),
                pltpu.VMEM((span, 128), f32),
                pltpu.VMEM((span, width), f32),
                pltpu.VMEM((3, span, width), bf16),
                pltpu.VMEM((span, width), bf16),
                pltpu.VMEM((span, width), bf16),
                pltpu.VMEM((EXTRA, span), bf16),
            ]
            + ([pltpu.VMEM((parts, r, slots, width), bf16)] if r else [])
            + [DMA((10 + 4 * parts,)), DMA((pair_count, 3))],
            limit=60,
            heavy=True,
            name="attention_backward",
        )
        grads.append(back[0])
        token_parts = back[1 : 1 + parts]
        sums_zero.append(back[1 + parts])
        if r == 0:
            feed_terms = plane_second([outer_terms, inner_terms], "feed_plane")
    feed_terms = plane_third(feed_terms, "feed_plane")
    token_parts = exchange(token_parts)

    early_low, late_low = low(2, pairs, blk + EXTRA, width), low(2, pairs, blk, width)
    early_keep, early_send, late_keep, late_send = call(
        functools.partial(square_kernel, share),
        [(HBM, early_low)] * 2 + [(HBM, late_low)] * 2,
        [(SM, spot)]
        + [(VM, sums) for sums in (sums_two, sums_one, inner_bias, *sums_zero)]
        + [(HBM, f[0]) for f in forward]
        + [(HBM, g) for g in grads],
        scratch=[pltpu.VMEM((2, count, width), bf16), pltpu.VMEM((4, count, width), bf16)]
        + [pltpu.VMEM(early_low.shape, bf16)] * 2
        + [pltpu.VMEM(late_low.shape, bf16)] * 2
        + [DMA((6 * share + 8,))],
        limit=60,
        heavy=True,
        name="square_grad",
    )
    early_got = swap(early_send, "batch", size, 1)
    late_got = swap(late_send, "batch", size, 1)
    feed_terms = along_line(feed_terms, "feed_line")
    grad_tokens = undeal(token_parts)
    early_terms = merge_terms(2, [early_keep, early_got], "early_core")
    early_terms = early_terms[0], swap(early_terms[1], "batch", size, 2)
    quarters = exchange(
        simple(
            functools.partial(quarter_kernel, parts),
            [late_keep, late_got],
            [low(1, pairs, blk // 2, width)] * parts,
            "late_core",
        )
    )
    early_terms = along_line(early_terms, "early_line")
    feed_all = gather(feed_terms, "feed_line")
    late_keep, late_send = simple(
        functools.partial(fourth_kernel, parts, 2),
        quarters,
        [low(1, pairs // 2, blk // 2, width)] * 2,
        "late_plane",
    )
    late_terms = late_keep, swap(late_send, "batch", size, 2)
    late_terms = along_line(late_terms, "late_line")
    grad_w_outer, grad_w_inner = simple(
        functools.partial(finish_kernel, parts),
        feed_all,
        [full(parts * blk, width), full(blk, parts * width)],
        "feed_finish",
    )
    halves = [low(2, 1, blk // 2, width), low(2, 1, blk + EXTRA - blk // 2, width)]
    top, bottom = simple(halves_kernel, list(early_terms), halves, "early_line")
    got_top, got_bottom = swap(top, "seq", parts, 1), swap(bottom, "seq", parts, 2)
    late_all = gather(late_terms, "late_line")
    top, bottom = simple(both_kernel, [top, got_top, bottom, got_bottom], halves, "early_plane")
    got_top, got_bottom = swap(top, "seq", parts, 2), swap(bottom, "seq", parts, 1)
    grad_w_key, grad_w_value = simple(
        functools.partial(finish_kernel, parts), late_all, [full(blk, width)] * 2, "late_finish"
    )
    grad_w_output, grad_w_query, vectors = simple(
        both_kernel,
        [top, got_top, bottom, got_bottom],
        [full(blk, width)] * 2 + [full(EXTRA, width)],
        "early_finish",
    )
    nine = lax.dynamic_slice(vectors, (0, place * blk), (9, blk))
    grad_b_inner = lax.dynamic_slice(
        vectors[9 : 9 + steps].reshape(-1), (place * (hidden // size),), (hidden // size,)
    )
    grad_gain_two, grad_shift_two, grad_b_outer = nine[0], nine[1], nine[2]
    grad_gain_one, grad_shift_one, grad_b_output = nine[3], nine[4], nine[5]
    grad_b_query, grad_b_value, grad_merge = nine[6], nine[7], nine[8]
    return (
        layer_out,
        grad_tokens,
        grad_merge,
        grad_w_query,
        grad_w_key,
        grad_w_value,
        grad_w_output,
        grad_b_query,
        grad_b_value,
        grad_b_output,
        grad_gain_one,
        grad_shift_one,
        grad_w_inner,
        grad_b_inner,
        grad_w_outer,
        grad_b_outer,
        grad_gain_two,
        grad_shift_two,
    )


def solution(mesh):
    parts, size = mesh.shape["seq"], mesh.shape["batch"]
    rowwise = P("batch", "seq", None)
    in_specs = (rowwise, P("batch", "seq"), P("batch")) + (P(),) * 16 + (rowwise,)
    matrix, vector = P("batch", None), P("batch")
    out_specs = (
        (rowwise, rowwise, vector)
        + (matrix,) * 4
        + (vector,) * 5
        + (matrix, vector, matrix)
        + (vector,) * 3
    )
    return jax.shard_map(
        functools.partial(body, parts, size),
        mesh=mesh,
        in_specs=in_specs,
        out_specs=out_specs,
        check_vma=False,
    )
```
